32 devices in a mesh: dp: 1, expert: 32 (over z, y, x, core).
Axes of the slice: x: 2, y: 2, z: 4, core: 2. Of those that a mesh axis runs over, the one named last changes fastest.
Arguments:
- queries: bfloat16 [1024, 4096], P('dp', 'expert'), may hold values from -140 to 140
- keys: bfloat16 [1024, 256], P(('dp', 'expert')), may hold values from -4 to 4
- values: bfloat16 [1024, 256], P(('dp', 'expert')), may hold values from -4 to 4
- span_ids: int32 [1024], P('dp'), may hold values from 0 to 9, as said below
- residual: bfloat16 [1024, 4096], P(('dp', 'expert')), may hold values from -6 to 6
- norm_gain: float32 [4096], replicated, may hold values from 0.1 to 1.9
- routes: int32 [1024, 8], P(('dp', 'expert')), may hold values from 0 to 127, as said below
- gates: float32 [1024, 8], P(('dp', 'expert')), may hold values from 0.2 to 1
- w_gate: bfloat16 [4096, 4096], P('expert'), may hold values from -0.09375 to 0.09375
- w_up: bfloat16 [4096, 4096], P('expert'), may hold values from -0.09375 to 0.09375
- w_down: bfloat16 [4096, 4096], P('expert'), may hold values from -0.1875 to 0.1875
Outputs:
- mixed: bfloat16 [1024, 4096], P(('dp', 'expert'))
The draws below stay inside these ranges and needn't reach their ends.
Inputs may be any that keep to these rules, and one draw needn't show every extreme that they name: `span_ids`: span numbers start at 0 and never fall along the positions; every span starts at an even position, has 2 to 512 positions and never crosses a multiple of 512; one aligned block of 512 positions is a single span, and every other holds exactly 9 spans. `routes`: each row names 8 different experts. In the rows of one device (aligned blocks of 32 rows) each expert below 4 is named by at most 8 rows, and exactly one such expert, changing from block to block, by exactly 8 rows; every expert below 4 is that one in some block.
All inputs are finite; a program needn't handle non-finite values.
Results may differ from the reference program's by a relative error of at most 0.0054.
Values may be sent and summed in bfloat16 or wider, within the bound.
A program may use at most 64 MiB of HBM per device.

```python
import math
import jax
import jax.numpy as jnp
from jax import lax

D = 4096
HEADS = 64
KV_HEADS = 4
EXPERTS = 128
TOP = 8
HEAD_DIM = 64
FF_WIN = 1024
FF_DEV = 128
SPAN = 512
TOK_DEV = 32
TOKENS = 1024
WAVE = 4


def shared_keys(key):
    sampled = jax.random.normal(jax.random.fold_in(key, 101), (TOKENS, KV_HEADS * HEAD_DIM), jnp.float32)
    return jnp.clip(sampled, -4.0, 4.0)


def draw_keys(key, part):
    key_rows = shared_keys(key)
    return key_rows.astype(jnp.bfloat16)


def draw_queries(key, part):
    sampled = jnp.clip(jax.random.normal(jax.random.fold_in(key, 102), (TOKENS, D), jnp.float32), -4.0, 4.0)
    return sampled.astype(jnp.bfloat16)


def draw_span_ids(key, part):
    blocks = TOKENS // SPAN
    pairs = SPAN // 2
    extra = SPAN // 64
    whole_block = jax.random.randint(jax.random.fold_in(key, 301), (), 0, blocks)
    scores = jax.random.randint(jax.random.fold_in(key, 302), (blocks, pairs), 0, 1 << 20) * pairs + jnp.arange(pairs)[None, :]
    scores = jnp.where(jnp.arange(pairs)[None, :] == 0, 1 << 30, scores)
    rank_order = jnp.argsort(jnp.argsort(scores, axis=1), axis=1)
    cut_pair = rank_order < extra
    cut_pair = cut_pair & (jnp.arange(blocks)[:, None] != whole_block)
    first_pair = jnp.arange(pairs)[None, :] == 0
    starts_pair = cut_pair | first_pair
    starts = jnp.stack([starts_pair, jnp.zeros_like(starts_pair)], axis=2).reshape(TOKENS)
    return (jnp.cumsum(starts.astype(jnp.int32)) - 1).astype(jnp.int32)


def draw_routes(key, part):
    blocks = TOKENS // TOK_DEV
    capacity = TOK_DEV // 4
    spare_ids = EXPERTS - WAVE
    base = jax.random.randint(jax.random.fold_in(key, 201), (), 0, WAVE)
    favored = (base + jnp.arange(blocks)) % WAVE
    modest = jax.random.randint(jax.random.fold_in(key, 202), (blocks, WAVE), 1, capacity // 2 + 1)
    counts = jnp.where(jnp.arange(WAVE)[None, :] == favored[:, None], capacity, modest)
    scores = jax.random.randint(jax.random.fold_in(key, 203), (blocks, WAVE, TOK_DEV), 0, 1 << 20) * TOK_DEV + jnp.arange(TOK_DEV)
    rank_order = jnp.argsort(jnp.argsort(scores, axis=2), axis=2)
    chosen = rank_order < counts[:, :, None]
    chosen = jnp.transpose(chosen, (0, 2, 1)).reshape(TOKENS, WAVE)
    taken_count = jnp.sum(chosen.astype(jnp.int32), axis=1)
    position = jnp.cumsum(chosen.astype(jnp.int32), axis=1) - 1
    columns = jnp.arange(TOP)
    matches = chosen[:, :, None] & (position[:, :, None] == columns[None, None, :])
    inside = jnp.sum(jnp.where(matches, jnp.arange(WAVE)[None, :, None], 0), axis=1)
    offset = jax.random.randint(jax.random.fold_in(key, 204), (TOKENS,), 0, spare_ids)
    outside = WAVE + (offset[:, None] + columns[None, :] - taken_count[:, None]) % spare_ids
    listed = jnp.where(columns[None, :] < taken_count[:, None], inside, outside)
    shuffle = jax.random.randint(jax.random.fold_in(key, 205), (TOKENS, TOP), 0, 1 << 20) * TOP + columns[None, :]
    reorder = jnp.argsort(shuffle, axis=1)
    return jnp.take_along_axis(listed, reorder, axis=1).astype(jnp.int32)


def levels(key, shape, cuts, smallest, high):
    def one(axis_at, parts):
        heights = jax.random.uniform(jax.random.fold_in(jax.random.fold_in(key, 6), axis_at), (parts,), jnp.float32, smallest / len(cuts), high / len(cuts))
        return jnp.repeat(jnp.exp(heights), shape[axis_at] // parts).reshape((-1,) + (1,) * (len(shape) - axis_at - 1))

    factor_of = one(*cuts[0])
    for cut in cuts[1:]:
        factor_of = factor_of * one(*cut)
    return factor_of


def noise(key, extent, scale, reach, shards=(), held_as=jnp.bfloat16):
    result = scale * jax.random.normal(key, extent, jnp.float32)
    if shards:
        result = result * levels(key, extent, shards, -0.22, 0.18)
    return jnp.clip(result, -reach, reach).astype(held_as)


def setup_inputs(seed: int = 0, part: int = 0) -> dict:
    arg_keys = jax.random.split(jax.random.key(seed), 12)
    part_splits = jax.random.split(jax.random.fold_in(arg_keys[11], part), 12)
    return {
        "queries": draw_queries(jax.random.fold_in(jax.random.fold_in(arg_keys[11], part), 71), part),
        "keys": draw_keys(jax.random.fold_in(jax.random.fold_in(arg_keys[11], part), 71), part),
        "values": noise(part_splits[2], (TOKENS, KV_HEADS * HEAD_DIM), 1.0, 4.0, ((0, 32),)),
        "span_ids": draw_span_ids(jax.random.fold_in(jax.random.fold_in(arg_keys[11], part), 71), part),
        "residual": noise(part_splits[4], (TOKENS, D), 1.0, 6.0, ((0, 32),)),
        "norm_gain": jnp.clip(1.0 + 0.18 * jax.random.normal(arg_keys[5], (D,), jnp.float32), 0.1, 1.9),
        "routes": draw_routes(jax.random.fold_in(jax.random.fold_in(arg_keys[11], part), 71), part),
        "gates": jnp.clip(0.2 + 0.8 * jax.random.uniform(part_splits[7], (TOKENS, TOP), jnp.float32) ** levels(part_splits[7], (TOKENS, TOP), ((0, 32),), -0.2, 0.2), 0.2, 1.0),
        "w_gate": noise(arg_keys[8], (WAVE * FF_WIN, D), D ** -0.5, 0.09375, ((0, 32),)),
        "w_up": noise(arg_keys[9], (WAVE * FF_WIN, D), D ** -0.5, 0.09375, ((0, 32),)),
        "w_down": noise(arg_keys[10], (WAVE * FF_WIN, D), FF_WIN ** -0.5, 0.1875, ((0, 32),)),
    }


def reference(queries, keys, values, span_ids, residual, norm_gain, routes, gates, w_gate, w_up, w_down):
    group_heads = HEADS // KV_HEADS
    blocks = TOKENS // SPAN
    score_scale = 1.0 / math.sqrt(HEAD_DIM)
    positions = jnp.arange(SPAN)
    causal = positions[None, :] <= positions[:, None]

    def one_block(pieces):
        query_blk, key_blk, value_blk, ids_blk = pieces
        key_full = jnp.repeat(key_blk, group_heads, axis=1).astype(jnp.float32)
        value_full = jnp.repeat(value_blk, group_heads, axis=1).astype(jnp.float32)
        scores = jnp.einsum('qhd,khd->hqk', query_blk.astype(jnp.float32), key_full) * score_scale
        allowed = causal & (ids_blk[None, :] == ids_blk[:, None])
        scores = jnp.where(allowed[None], scores, -jnp.inf)
        highest = lax.optimization_barrier(jnp.max(scores, axis=-1, keepdims=True))
        raised = jnp.exp(scores - highest)
        probabilities = raised / lax.optimization_barrier(jnp.sum(raised, axis=-1, keepdims=True))
        attn_weights = lax.optimization_barrier(probabilities.astype(jnp.bfloat16))
        attended_blk = jnp.einsum('hqk,khd->qhd', attn_weights.astype(jnp.float32), value_full)
        return attended_blk.astype(jnp.bfloat16)
    attended = lax.map(one_block, (queries.reshape(blocks, SPAN, HEADS, HEAD_DIM), keys.reshape(blocks, SPAN, KV_HEADS, HEAD_DIM), values.reshape(blocks, SPAN, KV_HEADS, HEAD_DIM), span_ids.reshape(blocks, SPAN))).reshape(TOKENS, D)
    stream = (residual.astype(jnp.float32) + attended.astype(jnp.float32)).astype(jnp.bfloat16)
    stream_wide = stream.astype(jnp.float32)
    inverse = lax.rsqrt(lax.optimization_barrier(jnp.mean(stream_wide * stream_wide, axis=-1, keepdims=True)) + 1e-06)
    normed = (stream_wide * inverse * norm_gain.astype(jnp.float32)).astype(jnp.bfloat16)
    group = FF_WIN // FF_DEV
    most_rows = TOKENS // 4

    def one_expert(total, expert):
        hits = routes == expert
        named = jnp.any(hits, axis=1)
        weight = lax.optimization_barrier(jnp.sum(jnp.where(hits, gates, 0.0), axis=1))
        number = jnp.sum(named.astype(jnp.int32))
        index = jnp.nonzero(named, size=most_rows, fill_value=0)[0].astype(jnp.int32)
        valid = jnp.arange(most_rows, dtype=jnp.int32) < number
        token_rows = normed[index]
        start = (expert * FF_WIN).astype(jnp.int32)
        gate_rows = lax.dynamic_slice_in_dim(w_gate, start, FF_WIN, 0)
        up_rows = lax.dynamic_slice_in_dim(w_up, start, FF_WIN, 0)
        down_rows = lax.dynamic_slice_in_dim(w_down, start, FF_WIN, 0)
        dims = (((1,), (1,)), ((), ()))
        gate_pre = lax.dot_general(token_rows, gate_rows, dims, preferred_element_type=jnp.float32)
        up_pre = lax.dot_general(token_rows, up_rows, dims, preferred_element_type=jnp.float32)
        hidden = lax.optimization_barrier((jax.nn.silu(gate_pre) * up_pre).astype(jnp.bfloat16))
        partial_sums = jnp.einsum('rgf,gfd->grd', hidden.reshape(most_rows, group, FF_DEV).astype(jnp.float32), down_rows.reshape(group, FF_DEV, D).astype(jnp.float32))
        rounded = lax.optimization_barrier(partial_sums.astype(jnp.bfloat16))
        expert_out = lax.optimization_barrier(jnp.sum(rounded.astype(jnp.float32), axis=0))
        contribution = jnp.where(valid, weight[index], 0.0)[:, None] * expert_out
        return (total.at[index].add(contribution), None)
    total, _ = lax.scan(one_expert, jnp.zeros((TOKENS, D), jnp.float32), jnp.arange(WAVE, dtype=jnp.int32))
    return (stream_wide + total).astype(jnp.bfloat16)
```

```python
import functools
import math

import jax
import jax.numpy as jnp
from jax import lax
from jax.experimental import pallas as pl
from jax.experimental.pallas import tpu as pltpu
from jax.sharding import PartitionSpec as P

KV_HEADS = 4
HEAD_DIM = 64
FF_WIN = 1024
SPAN = 512
CHUNKS = 4
MESH = pl.DeviceIdType.MESH
F32 = jnp.float32
BF16 = jnp.bfloat16


def remote(src, dst, send, recv, device):
    return pltpu.make_async_remote_copy(
        src_ref=src, dst_ref=dst, send_sem=send, recv_sem=recv,
        device_id={"expert": device}, device_id_type=MESH,
    )


def arrived(ref, sem):
    pltpu.make_async_copy(ref, ref, sem).wait()


def route_matrix(routes, gates, wave, capacity):
    tokens = routes.shape[0]
    here = tokens // 2
    columns = wave * 2 * capacity
    column = lax.broadcasted_iota(jnp.int32, (tokens, columns), 1)
    token = lax.broadcasted_iota(jnp.int32, (tokens, columns), 0)
    one = lax.broadcasted_iota(jnp.int32, (tokens, tokens), 0)
    other = lax.broadcasted_iota(jnp.int32, (tokens, tokens), 1)
    lower = jnp.where((one >= other) & (one // here == other // here), 1.0, 0.0)
    named_wide = jnp.zeros((tokens, columns), F32)
    weight_wide = jnp.zeros((tokens, columns), F32)
    for expert in range(wave):
        hits = routes == expert
        named = jnp.max(jnp.where(hits, 1.0, 0.0), axis=1, keepdims=True)
        weight = jnp.sum(jnp.where(hits, gates, 0.0), axis=1, keepdims=True)
        mask = column // (2 * capacity) == expert
        named_wide = jnp.where(mask, named, named_wide)
        weight_wide = jnp.where(mask, weight, weight_wide)
    count = jnp.dot(lower.astype(BF16), named_wide.astype(BF16), preferred_element_type=F32)
    slot = (column % capacity + 1).astype(F32)
    fits = (count == slot) & (column % (2 * capacity) // capacity == token // here)
    chosen = jnp.where(fits, named_wide, 0.0)
    return chosen, chosen * weight_wide


def moe_kernel(names, group, *refs):
    at = dict(zip(names, refs, strict=True))
    (queries, keys, values, ids, res, gain, routes, gates, wg, wu, wd, out) = (
        at[name] for name in ("queries", "keys", "values", "ids", "res", "gain", "routes", "gates", "wg", "wu", "wd", "out")
    )
    (keys_v, values_v, ids_v, gain_v, routes_v, gates_v, rg_v, res_v, w_v, wd_v) = (
        at[name] for name in ("keys_v", "values_v", "ids_v", "gain_v", "routes_v", "gates_v", "rg_v", "res_v", "w_v", "wd_v")
    )
    (kv_pack, kv_far, kv_buf, q_buf, bias_v, stream_v, outg, x_buf, pre_out, pre_in) = (
        at[name] for name in ("kv_pack", "kv_far", "kv_buf", "q_buf", "bias_v", "stream_v", "outg", "x_buf", "pre_out", "pre_in")
    )
    (s1, r1, s2, r2, keep, own, final, back, out_v) = (
        at[name] for name in ("s1", "r1", "s2", "r2", "keep", "own", "final", "back", "out_v")
    )
    (in_sem, w_sem, ready_sem, send_sem, kv_sem, q_sem, pair_sem, z_sem, x_sem, pre_sem, r1_sem, r2_sem, back_sem, out_sem) = (
        at[name] for name in (
            "in_sem", "w_sem", "ready_sem", "send_sem", "kv_sem", "q_sem", "pair_sem", "z_sem", "x_sem",
            "pre_sem", "r1_sem", "r2_sem", "back_sem", "out_sem")
    )
    me = lax.axis_index("expert")
    wave = x_buf.shape[2]
    devices = wave * group
    tokens, width = out.shape
    both = 2 * tokens
    half = width // 2
    quarter = half // 2
    block = half // CHUNKS
    rows = wave * 16
    plane = me // group
    mine = me % group
    core = me % 2
    other = 1 - core
    here = pl.ds(pl.multiple_of(core * half, 128), half)
    there = pl.ds(pl.multiple_of(other * half, 128), half)

    def across(rz):
        return (plane ^ rz) * group + mine

    def within(r):
        return plane * group + (mine ^ r)

    partner = within(1)
    fetched = {}
    for number, (name, source, target) in enumerate((
        ("keys", keys, keys_v), ("values", values, values_v), ("routes", routes, routes_v), ("gates", gates, gates_v),
        ("ids", ids, ids_v), ("gain", gain.at[:, here], gain_v),
    )):
        fetched[name] = pltpu.make_async_copy(source, target, in_sem.at[number])
        fetched[name].start()
    barrier = pltpu.get_barrier_semaphore()
    partners = [within(r) for r in range(1, group)] + [across(rz) for rz in range(1, wave)]
    for device in partners:
        pl.semaphore_signal(barrier, inc=1, device_id={"expert": device}, device_id_type=MESH)
    pltpu.make_async_copy(res.at[:, here], res_v.at[core], pair_sem.at[1]).start()
    pltpu.make_async_copy(wg.at[:, here], w_v.at[0, core], w_sem.at[0]).start()
    pltpu.make_async_copy(wu.at[:, here], w_v.at[1, core], w_sem.at[0]).start()
    pltpu.make_async_copy(wd.at[:, here], wd_v.at[core], w_sem.at[1]).start()
    for name in ("keys", "values", "routes", "gates"):
        fetched[name].wait()
    for head in range(KV_HEADS):
        columns = slice(head * HEAD_DIM, (head + 1) * HEAD_DIM)
        kv_pack[head] = jnp.concatenate([keys_v[:, columns], values_v[:, columns]], axis=1)
    rg_v[core, :8, :tokens] = routes_v[...].astype(F32)
    rg_v[core, 8:, :tokens] = gates_v[...]
    pl.semaphore_wait(barrier, len(partners))

    sends = []

    def go(src, dst, recv, device):
        copy = remote(src, dst, send_sem, recv, device)
        copy.start()
        sends.append(copy)

    planes = SPAN // (group * tokens)
    halves = KV_HEADS // 2
    for rz in range(1, planes):
        go(kv_pack, kv_far.at[rz - 1], kv_sem.at[0], across(rz))
    for rz in range(1, wave):
        pl.semaphore_signal(ready_sem, inc=1, device_id={"expert": across(rz)}, device_id_type=MESH)
    for r in range(1, group):
        which = (core ^ (r % 2)) * halves
        go(kv_pack.at[pl.ds(which, halves)], kv_buf.at[plane % planes, mine], kv_sem.at[1], within(r))
    kv_buf[plane % planes, mine] = kv_pack[pl.ds(core * halves, halves)]
    go(rg_v.at[core], rg_v.at[core], pair_sem.at[0], partner)
    pl.semaphore_wait(ready_sem, wave - 1)
    side = me // (devices // 2)
    number = me % (devices // 2)
    per_chunk = devices // 2 // CHUNKS
    query_sem = q_sem.at[number // per_chunk]
    for r in range(devices // 2 - 1, 0, -1):
        pair = (me // 2) ^ r
        source = queries.at[pl.ds(pl.multiple_of(pair * both, both), both)]
        go(source, q_buf.at[number], query_sem, pair * 2 + side)
    source = queries.at[pl.ds(pl.multiple_of(me // 2 * both, both), both)]

    @pl.when(core == side)
    def _():
        pltpu.make_async_copy(source, q_buf.at[number], query_sem).start()

    @pl.when(core != side)
    def _():
        remote(source, q_buf.at[number], at["self_sem"], query_sem, partner).start()

    for rz in range(1, planes):
        arrived(kv_far.at[rz - 1], kv_sem.at[0])
        for r in range(1, group):
            which = (core ^ (r % 2)) * halves
            go(kv_far.at[rz - 1, pl.ds(which, halves)], kv_buf.at[(plane ^ rz) % planes, mine], kv_sem.at[2], within(r))
        kv_buf[(plane ^ rz) % planes, mine] = kv_far[rz - 1, pl.ds(core * halves, halves)]
    go(res.at[:, there], res_v.at[core], pair_sem.at[1], partner)
    go(wg.at[:, there], w_v.at[0, core], w_sem.at[0], partner)
    go(wu.at[:, there], w_v.at[1, core], w_sem.at[0], partner)
    go(wd.at[:, there], wd_v.at[core], w_sem.at[1], partner)
    fetched["ids"].wait()
    arrived(rg_v.at[0], pair_sem.at[0])
    named = jnp.concatenate([rg_v[c, :8, :].T[:tokens] for c in range(2)], axis=0)
    weights = jnp.concatenate([rg_v[c, 8:, :].T[:tokens] for c in range(2)], axis=0)
    chosen, mix = route_matrix(named, weights, wave, 8)
    chosen = chosen.T.astype(BF16)

    stretch = group * tokens
    wide = per_chunk * both
    first = plane // planes * planes
    key_ids = jnp.concatenate(
        [jnp.broadcast_to(ids_v[first + i].astype(F32), (128, stretch)).T for i in range(planes)], axis=0
    )
    key_ids = jnp.concatenate([key_ids] * (wide // 128), axis=1)
    key_at = lax.broadcasted_iota(jnp.int32, (SPAN, wide), 0)
    query_at = (
        lax.broadcasted_iota(jnp.int32, (SPAN, wide), 1) % both
        + ((plane - first) * stretch + mine // 2 * both)
    )
    query_ids = jnp.sum(jnp.where(key_at == query_at, key_ids, 0.0), axis=0, keepdims=True)
    bias_v[...] = jnp.where((key_at <= query_at) & (key_ids == query_ids), 0.0, -jnp.inf)
    arrived(kv_buf.at[0, pl.ds(0, group - 1)], kv_sem.at[1])
    if planes > 1:
        arrived(kv_buf.at[pl.ds(0, planes - 1), pl.ds(0, group - 1)], kv_sem.at[2])

    def attend(g):
        head = g * halves // CHUNKS
        held = kv_buf[:, :, head].reshape(SPAN, 2 * HEAD_DIM)
        key_blk = held[:, :HEAD_DIM]
        value_rows = held.T[HEAD_DIM:]
        query = q_buf[g * per_chunk:(g + 1) * per_chunk].reshape(wide, -1) * BF16(1.0 / math.sqrt(HEAD_DIM))
        heads = []
        for number in range(query.shape[1] // HEAD_DIM):
            one = query[:, number * HEAD_DIM:(number + 1) * HEAD_DIM]
            scores = lax.dot_general(key_blk, one, (((1,), (1,)), ((), ())), preferred_element_type=F32)
            scores = scores + bias_v[...]
            raised = jnp.exp(scores - jnp.max(scores, axis=0, keepdims=True))
            total = jnp.sum(raised, axis=0, keepdims=True)
            heads.append(jnp.dot(value_rows, raised.astype(BF16), preferred_element_type=F32) * (1.0 / total))
        joined = heads[0] if len(heads) == 1 else jnp.concatenate(heads, axis=0)
        joined = joined.T.astype(BF16)
        return jnp.concatenate([joined[i * both:(i + 1) * both] for i in range(per_chunk)], axis=1)

    low, high = pl.ds(0, wave // 2), pl.ds(wave // 2, wave - wave // 2)
    parts = (low, high)
    near = (within(2), within(4))

    def forward(g):
        for part in range(2):
            if part:
                arrived(x_buf.at[g, 0, high], z_sem.at[g, 1])
            elif wave > 2:
                arrived(x_buf.at[g, 0, pl.ds(1, wave // 2 - 1)], z_sem.at[g, 0])
            piece = x_buf.at[g, 0, parts[part]]
            for hop in range(2):
                go(piece, x_buf.at[g, 1 + hop, parts[part]], x_sem.at[g, hop, part], near[hop])

    def relay(g):
        for hop in range(2):
            piece = x_buf.at[g, 1 + hop, parts[hop]]
            arrived(piece, x_sem.at[g, hop, hop])
            go(piece, x_buf.at[g, 3, parts[hop]], x_sem.at[g, 2, hop], near[1 - hop])

    for g in range(CHUNKS):
        arrived(q_buf.at[pl.ds(g * per_chunk, per_chunk)], q_sem.at[g])
        if g == 0:
            arrived(res_v, pair_sem.at[1])
        columns = slice(g * block, (g + 1) * block)
        attended = attend(g)
        stream = (res_v[:, :, columns].reshape(both, block).astype(F32) + attended.astype(F32)).astype(BF16)
        stream_v[g] = stream
        outg[g] = jnp.dot(chosen, stream, preferred_element_type=F32).astype(BF16).reshape(wave, 16, block)
        for rz in range(wave - 1, 0, -1):
            go(outg.at[g, plane ^ rz], x_buf.at[g, 0, rz], z_sem.at[g, rz // (wave // 2)], across(rz))
        x_buf[g, 0, 0] = outg[g, plane]
        if g >= 2:
            forward(g - 2)
    fetched["gain"].wait()
    arrived(w_v, w_sem.at[0])

    squares = None
    pre = None

    def up(g):
        for hop in range(2):
            arrived(x_buf.at[g, 1 + hop, parts[1 - hop]], x_sem.at[g, hop, 1 - hop])
            arrived(x_buf.at[g, 3, parts[hop]], x_sem.at[g, 2, hop])
        columns = slice(g * block, (g + 1) * block)
        x = x_buf[g].reshape(4 * rows, block).astype(F32)
        square = x * x
        square = sum(square[:, i:i + 128] for i in range(0, block, 128))
        x = (x * gain_v[:, columns]).astype(BF16)
        weight = w_v[:, :, :, columns].reshape(-1, block)
        return square, lax.dot_general(x, weight, (((1,), (1,)), ((), ())), preferred_element_type=F32)

    steps = [(forward, CHUNKS - 2), (relay, 0), (forward, CHUNKS - 1)]
    for g in range(CHUNKS):
        if g + 1 < CHUNKS:
            steps.append((relay, g + 1))
        steps.append((up, g))
    for step, g in steps:
        result = step(g)
        if result is not None:
            squares = result[0] if squares is None else squares + result[0]
            pre = result[1] if pre is None else pre + result[1]
    units = pre.shape[1]
    square = jnp.sum(squares, axis=1, keepdims=True)
    coarse = square.astype(BF16)
    rest = (square - coarse.astype(F32)).astype(BF16)
    lane = lax.broadcasted_iota(jnp.int32, (4 * rows, 128), 1)
    pre_out[:, :units] = pre.astype(BF16)
    pre_out[:, units:] = jnp.where(lane < 64, coarse.astype(F32), rest.astype(F32)).astype(BF16)
    go(pre_out, pre_in, pre_sem, partner)
    arrived(pre_in, pre_sem)
    square = square + pre_in[:, units:units + 1].astype(F32) + pre_in[:, units + 64:units + 65].astype(F32)
    inverse = lax.rsqrt(square * (1.0 / width) + 1e-06)
    pre = (pre + pre_in[:, :units].astype(F32)) * inverse
    gate_pre, up_pre = pre[:, :units // 2], pre[:, units // 2:]
    hidden = (gate_pre / (1.0 + jnp.exp(-gate_pre)) * up_pre).astype(BF16)
    arrived(wd_v, w_sem.at[1])

    def down(blk):
        weight = wd_v[...].reshape(-1, half)
        piece = jnp.dot(hidden[blk * rows:(blk + 1) * rows], weight, preferred_element_type=F32)
        return piece.reshape(wave, 16, half)

    def first_hop(which, kind, piece):
        s1[which, kind] = piece.astype(BF16)
        for part in (1, 0):
            go(s1.at[which, kind, parts[part]], r1.at[which, kind, parts[part]], r1_sem.at[which, kind, part], near[which])

    piece = down(3)
    first_hop(0, 0, piece[:, :, :quarter])
    first_hop(1, 0, piece[:, :, quarter:])
    piece = down(1)
    first_hop(0, 1, piece[:, :, :quarter])
    keep[1] = piece[:, :, quarter:]
    piece = down(2)
    first_hop(1, 1, piece[:, :, quarter:])
    keep[0] = piece[:, :, :quarter]
    piece = down(0)
    own[0] = piece[:, :, :quarter]
    own[1] = piece[:, :, quarter:]
    for part in (1, 0):
        for which in range(2):
            chunk = parts[part]
            arrived(r1.at[which, 0, chunk], r1_sem.at[which, 0, part])
            s2[which, chunk] = (keep[which, chunk] + r1[which, 0, chunk].astype(F32)).astype(BF16)
            go(s2.at[which, chunk], r2.at[which, chunk], r2_sem.at[which, part], near[1 - which])
    for part in (1, 0):
        chunk = parts[part]
        for which in range(2):
            arrived(r1.at[which, 1, chunk], r1_sem.at[which, 1, part])
            arrived(r2.at[which, chunk], r2_sem.at[which, part])
            total = own[which, chunk] + r1[which, 1, chunk].astype(F32) + r2[which, chunk].astype(F32)
            final[chunk, :, which * quarter:(which + 1) * quarter] = total.astype(BF16)
        for rz in range((part + 1) * (wave // 2) - 1, part * (wave // 2) - 1, -1):
            if rz:
                go(final.at[rz], back.at[plane], back_sem, across(rz))
            else:
                back[plane] = final[0]
    arrived(back.at[pl.ds(0, wave - 1)], back_sem)
    high_mix = mix.astype(BF16)
    rest = mix - high_mix.astype(F32)
    middle = rest.astype(BF16)
    lowest = (rest - middle.astype(F32)).astype(BF16)
    for g in range(CHUNKS):
        columns = slice(g * block, (g + 1) * block)
        outs = back[:, :, columns].reshape(rows, block)
        added = (
            jnp.dot(lowest, outs, preferred_element_type=F32)
            + jnp.dot(middle, outs, preferred_element_type=F32)
            + jnp.dot(high_mix, outs, preferred_element_type=F32)
        )
        out_v[:, :, columns] = (stream_v[g].astype(F32) + added).astype(BF16).reshape(2, tokens, block)
    go(out_v.at[other], out.at[:, here], out_sem.at[0], partner)
    copy = pltpu.make_async_copy(out_v.at[core], out.at[:, here], out_sem.at[1])
    copy.start()
    copy.wait()
    arrived(out.at[:, there], out_sem.at[0])

    @pl.when(core != side)
    def _():
        remote(source, q_buf.at[number], at["self_sem"], query_sem, partner).wait_send()

    for copy in sends:
        copy.wait_send()


def layer(queries, keys, values, span_ids, res, gain, routes, gates, wg, wu, wd):
    devices = lax.axis_size("expert")
    group = FF_WIN // wg.shape[0]
    wave = devices // group
    tokens, width = res.shape
    half = width // 2
    hidden = wg.shape[0]
    both = 2 * tokens
    block = half // CHUNKS
    planes = SPAN // (group * tokens)
    halves = KV_HEADS // 2
    rows = wave * 16
    per_chunk = devices // 2 // CHUNKS
    hbm = pl.BlockSpec(memory_space=pl.ANY)
    dma = pltpu.SemaphoreType.DMA

    def vmem(*shape, dtype=BF16):
        return pltpu.VMEM(shape, dtype)

    scratch = {
        "keys_v": vmem(*keys.shape),
        "values_v": vmem(*values.shape),
        "ids_v": vmem(wave, 1, group * tokens, dtype=jnp.int32),
        "gain_v": vmem(1, half, dtype=F32),
        "routes_v": vmem(*routes.shape[::-1], dtype=jnp.int32),
        "gates_v": vmem(*gates.shape[::-1], dtype=F32),
        "rg_v": vmem(2, 16, 128, dtype=F32),
        "res_v": vmem(2, tokens, half),
        "w_v": vmem(2, 2, hidden, half),
        "wd_v": vmem(2, hidden, half),
        "kv_pack": vmem(KV_HEADS, tokens, 2 * HEAD_DIM),
        "kv_far": vmem(max(planes - 1, 1), KV_HEADS, tokens, 2 * HEAD_DIM),
        "kv_buf": vmem(planes, group, halves, tokens, 2 * HEAD_DIM),
        "q_buf": vmem(devices // 2, both, queries.shape[1]),
        "bias_v": vmem(SPAN, per_chunk * both, dtype=F32),
        "stream_v": vmem(CHUNKS, both, block),
        "outg": vmem(CHUNKS, wave, 16, block),
        "x_buf": vmem(CHUNKS, 4, wave, 16, block),
        "pre_out": vmem(4 * rows, 4 * hidden + 128),
        "pre_in": vmem(4 * rows, 4 * hidden + 128),
        "s1": vmem(2, 2, wave, 16, half // 2),
        "r1": vmem(2, 2, wave, 16, half // 2),
        "s2": vmem(2, wave, 16, half // 2),
        "r2": vmem(2, wave, 16, half // 2),
        "keep": vmem(2, wave, 16, half // 2, dtype=F32),
        "own": vmem(2, wave, 16, half // 2, dtype=F32),
        "final": vmem(wave, 16, half),
        "back": vmem(wave, 16, half),
        "out_v": vmem(2, tokens, half),
        "in_sem": dma((6,)),
        "w_sem": dma((2,)),
        "ready_sem": pltpu.SemaphoreType.REGULAR,
        "send_sem": dma(()),
        "self_sem": dma(()),
        "kv_sem": dma((3,)),
        "q_sem": dma((CHUNKS,)),
        "pair_sem": dma((2,)),
        "z_sem": dma((CHUNKS, 2)),
        "x_sem": dma((CHUNKS, 3, 2)),
        "pre_sem": dma(()),
        "r1_sem": dma((2, 2, 2)),
        "r2_sem": dma((2, 2)),
        "back_sem": dma(()),
        "out_sem": dma((2,)),
    }
    names = ("queries", "keys", "values", "ids", "res", "gain", "routes", "gates", "wg", "wu", "wd", "out", *scratch)
    return pl.pallas_call(
        functools.partial(moe_kernel, names, group),
        out_shape=jax.ShapeDtypeStruct((tokens, width), BF16),
        in_specs=[hbm] * 11,
        out_specs=hbm,
        scratch_shapes=list(scratch.values()),
        compiler_params=pltpu.CompilerParams(
            collective_id=0, has_side_effects=True, vmem_limit_bytes=60 * 2**20
        ),
    )(
        queries, keys, values, span_ids.reshape(wave, 1, group * tokens), res, gain.reshape(1, width),
        routes.T, gates.T, wg, wu, wd,
    )


def solution(mesh):
    return jax.shard_map(
        layer,
        mesh=mesh,
        in_specs=(
            P("dp", "expert"),
            P(("dp", "expert"), None),
            P(("dp", "expert"), None),
            P("dp"),
            P(("dp", "expert"), None),
            P(),
            P(("dp", "expert"), None),
            P(("dp", "expert"), None),
            P("expert", None),
            P("expert", None),
            P("expert", None),
        ),
        out_specs=P(("dp", "expert"), None),
        check_vma=False,
    )
```

```python
import functools
import math

import jax
import jax.numpy as jnp
from jax import lax
from jax.experimental import pallas as pl
from jax.experimental.pallas import tpu as pltpu
from jax.sharding import PartitionSpec as P

KV_HEADS = 4
HEAD_DIM = 64
FF_WIN = 1024
SPAN = 512
CHUNKS = 4
WINDOW = 3
MESH = pl.DeviceIdType.MESH
F32 = jnp.float32
BF16 = jnp.bfloat16


def remote(src, dst, send, recv, device):
    return pltpu.make_async_remote_copy(
        src_ref=src, dst_ref=dst, send_sem=send, recv_sem=recv,
        device_id={"expert": device}, device_id_type=MESH,
    )


def arrived(ref, sem):
    pltpu.make_async_copy(ref, ref, sem).wait()


def route_matrix(routes, gates, wave, capacity, cores):
    tokens = routes.shape[0]
    here = tokens // cores
    columns = wave * cores * capacity
    column = lax.broadcasted_iota(jnp.int32, (tokens, columns), 1)
    token = lax.broadcasted_iota(jnp.int32, (tokens, columns), 0)
    one = lax.broadcasted_iota(jnp.int32, (tokens, tokens), 0)
    other = lax.broadcasted_iota(jnp.int32, (tokens, tokens), 1)
    lower = jnp.where((one >= other) & (one // here == other // here), 1.0, 0.0)
    named_wide = jnp.zeros((tokens, columns), F32)
    weight_wide = jnp.zeros((tokens, columns), F32)
    for expert in range(wave):
        hits = routes == expert
        named = jnp.max(jnp.where(hits, 1.0, 0.0), axis=1, keepdims=True)
        weight = jnp.sum(jnp.where(hits, gates, 0.0), axis=1, keepdims=True)
        mask = column // (cores * capacity) == expert
        named_wide = jnp.where(mask, named, named_wide)
        weight_wide = jnp.where(mask, weight, weight_wide)
    count = jnp.dot(lower.astype(BF16), named_wide.astype(BF16), preferred_element_type=F32)
    slot = (column % capacity + 1).astype(F32)
    fits = (count == slot) & (column % (cores * capacity) // capacity == token // here)
    chosen = jnp.where(fits, named_wide, 0.0)
    return chosen, chosen * weight_wide


def moe_kernel(names, group, *refs):
    at = dict(zip(names, refs, strict=True))
    (queries, keys, values, ids, res, gain, routes, gates, wg, wu, wd, out) = (
        at[name] for name in ("queries", "keys", "values", "ids", "res", "gain", "routes", "gates", "wg", "wu", "wd", "out")
    )
    (keys_v, values_v, ids_v, gain_v, routes_v, gates_v, rg_v, res_v, w_v, wd_v) = (
        at[name] for name in ("keys_v", "values_v", "ids_v", "gain_v", "routes_v", "gates_v", "rg_v", "res_v", "w_v", "wd_v")
    )
    (kv_pack, kv_far, kv_buf, q_buf, bias_v, stream_v, stream_all, outg, x_buf, pre_out, pre_in) = (
        at[name] for name in (
            "kv_pack", "kv_far", "kv_buf", "q_buf", "bias_v", "stream_v", "stream_all", "outg", "x_buf", "pre_out", "pre_in")
    )
    (s1, r1, s2, r2, keep, own, final, back) = (
        at[name] for name in ("s1", "r1", "s2", "r2", "keep", "own", "final", "back")
    )
    (far_sem, in_sem, w_sem, ready_sem, send_sem, kv_sem, q_sem, pair_sem, z_sem, x_sem, pre_sem, r1_sem, r2_sem, back_sem) = (
        at[name] for name in (
            "far_sem", "in_sem", "w_sem", "ready_sem", "send_sem", "kv_sem", "q_sem", "pair_sem", "z_sem", "x_sem",
            "pre_sem", "r1_sem", "r2_sem", "back_sem")
    )
    me = lax.axis_index("expert")
    wave = x_buf.shape[2]
    devices = wave * group
    tokens, width = out.shape
    both = 2 * tokens
    half = width // 2
    quarter = half // 2
    block = half // CHUNKS
    rows = wave * 16
    plane = me // group
    mine = me % group
    core = me % 2
    other = 1 - core


    sends = []

    def go(src, dst, recv, device):
        copy = remote(src, dst, send_sem, recv, device)
        copy.start()
        sends.append(copy)

    def early(c):
        return [pl.ds(pl.multiple_of(q * quarter, 128), quarter) for q in (1 + c, 3 * c)]

    def split(source, target, sem, send):
        for n, columns in enumerate(early(core if send is None else other)):
            place = target.at[:, pl.ds(n * quarter, quarter)]
            if send is None:
                pltpu.make_async_copy(source.at[:, columns], place, sem).start()
            else:
                go(source.at[:, columns], place, sem, send)

    def across(rz):
        return (plane ^ rz) * group + mine

    def within(r):
        return plane * group + (mine ^ r)

    partner = within(1)
    fetched = {}
    for number, (name, source, target) in enumerate((
        ("keys", keys, keys_v), ("values", values, values_v), ("routes", routes, routes_v), ("gates", gates, gates_v),
        ("ids", ids, ids_v),
    )):
        fetched[name] = pltpu.make_async_copy(source, target, in_sem.at[number])
        fetched[name].start()
    barrier = pltpu.get_barrier_semaphore()
    partners = [within(r) for r in range(1, group)] + [across(rz) for rz in range(1, wave)]
    for device in partners:
        pl.semaphore_signal(barrier, inc=1, device_id={"expert": device}, device_id_type=MESH)
    split(res, res_v.at[core], pair_sem.at[1], None)
    split(gain, gain_v, in_sem.at[5], None)
    split(wg, w_v.at[0, core], w_sem.at[0], None)
    split(wu, w_v.at[1, core], w_sem.at[0], None)
    split(wd, wd_v.at[core], w_sem.at[1], None)
    pl.semaphore_wait(barrier, len(partners))
    for rz in range(1, wave):
        pl.semaphore_signal(ready_sem, inc=1, device_id={"expert": across(rz)}, device_id_type=MESH)

    for name in ("keys", "values"):
        fetched[name].wait()
    for place, head in enumerate((1, 2, 0, 3)):
        columns = slice(head * HEAD_DIM, (head + 1) * HEAD_DIM)
        kv_pack[place] = jnp.concatenate([keys_v[:, columns], values_v[:, columns]], axis=1)
    planes = SPAN // (group * tokens)
    halves = KV_HEADS // 2
    for h in range(halves):
        for rz in range(1, planes):
            pair = pl.ds(2 * h, 2)
            go(kv_pack.at[pair], kv_far.at[rz - 1, pair], far_sem.at[rz - 1, h], across(rz))

    def share(h, source, at_plane, sem):
        for r in range(1, group):
            go(source.at[2 * h + (core ^ (r % 2))], kv_buf.at[h, at_plane, mine], sem, within(r))
        kv_buf[h, at_plane, mine] = source[2 * h + core]

    share(0, kv_pack, plane % planes, kv_sem.at[0, 0])
    pl.semaphore_wait(ready_sem, wave - 1)
    side = me // (devices // 2)
    number = (me % (devices // 2)) ^ ((1 - side) * (devices // 4))
    per_chunk = devices // 2 // CHUNKS
    query_sem = q_sem.at[number // per_chunk]

    def ask(r):
        pair = (me // 2) ^ r
        source = queries.at[pl.ds(pl.multiple_of(pair * both, both), both)]
        return remote(source, q_buf.at[number], at["ask_sem"], query_sem, pair * 2 + side)

    def ask_all():
        for r in range(devices // 2 - 1, 0, -1):
            ask(r).start()

        @pl.when(core == side)
        def _():
            source = queries.at[pl.ds(pl.multiple_of(me // 2 * both, both), both)]
            pltpu.make_async_copy(source, q_buf.at[number], query_sem).start()

        @pl.when(core != side)
        def _():
            ask(0).start()

    @pl.when(number < devices // 4)
    def _():
        ask_all()

    for name in ("routes", "gates"):
        fetched[name].wait()
    rg_v[core, :8, :tokens] = routes_v[...].astype(F32)
    rg_v[core, 8:, :tokens] = gates_v[...]
    go(rg_v.at[core], rg_v.at[core], pair_sem.at[0], partner)
    def pass_on(h):
        for rz in range(1, planes):
            arrived(kv_far.at[rz - 1, pl.ds(2 * h, 2)], far_sem.at[rz - 1, h])
            share(h, kv_far.at[rz - 1], (plane ^ rz) % planes, kv_sem.at[1, h])

    pass_on(0)
    split(res, res_v.at[core], pair_sem.at[1], partner)
    fetched["ids"].wait()
    _, mix = route_matrix(routes_v[...].astype(F32).T, gates_v[...].T, wave, 8, 1)
    arrived(rg_v.at[0], pair_sem.at[0])
    named = jnp.concatenate([rg_v[c, :8, :].T[:tokens] for c in range(2)], axis=0)
    weights = jnp.concatenate([rg_v[c, 8:, :].T[:tokens] for c in range(2)], axis=0)
    chosen, _ = route_matrix(named, weights, wave, 8, 2)
    chosen = chosen.T.astype(BF16)

    stretch = group * tokens
    wide = per_chunk * both
    first = plane // planes * planes
    key_ids = jnp.concatenate(
        [jnp.broadcast_to(ids_v[first + i].astype(F32), (128, stretch)).T for i in range(planes)], axis=0
    )
    key_ids = jnp.concatenate([key_ids] * (wide // 128), axis=1)
    key_at = lax.broadcasted_iota(jnp.int32, (SPAN, wide), 0)
    query_at = (
        lax.broadcasted_iota(jnp.int32, (SPAN, wide), 1) % both
        + ((plane - first) * stretch + mine // 2 * both)
    )
    query_ids = jnp.sum(jnp.where(key_at == query_at, key_ids, 0.0), axis=0, keepdims=True)
    bias_v[...] = jnp.where((key_at <= query_at) & (key_ids == query_ids), 0.0, -jnp.inf)
    share(1, kv_pack, plane % planes, kv_sem.at[0, 1])
    pass_on(1)

    @pl.when(number >= devices // 4)
    def _():
        ask_all()

    def gathered(h):
        arrived(kv_buf.at[h, 0, pl.ds(0, group - 1)], kv_sem.at[0, h])
        if planes > 1:
            arrived(kv_buf.at[h, pl.ds(0, planes - 1), pl.ds(0, group - 1)], kv_sem.at[1, h])

    gathered(0)
    split(wg, w_v.at[0, core], w_sem.at[0], partner)
    split(wu, w_v.at[1, core], w_sem.at[0], partner)
    split(wd, wd_v.at[core], w_sem.at[1], partner)

    def attend(g):
        head = g * halves // CHUNKS
        held = kv_buf[head].reshape(SPAN, 2 * HEAD_DIM)
        key_blk = held[:, :HEAD_DIM]
        value_rows = held.T[HEAD_DIM:]
        query = q_buf[g * per_chunk:(g + 1) * per_chunk].reshape(wide, -1) * BF16(1.0 / math.sqrt(HEAD_DIM))
        heads = []
        for number in range(query.shape[1] // HEAD_DIM):
            one = query[:, number * HEAD_DIM:(number + 1) * HEAD_DIM]
            scores = lax.dot_general(key_blk, one, (((1,), (1,)), ((), ())), preferred_element_type=F32)
            scores = scores + bias_v[...]
            raised = jnp.exp(scores - jnp.max(scores, axis=0, keepdims=True))
            total = jnp.sum(raised, axis=0, keepdims=True)
            heads.append(jnp.dot(value_rows, raised.astype(BF16), preferred_element_type=F32) * (1.0 / total))
        joined = heads[0] if len(heads) == 1 else jnp.concatenate(heads, axis=0)
        joined = joined.T.astype(BF16)
        return jnp.concatenate([joined[i * both:(i + 1) * both] for i in range(per_chunk)], axis=1)

    near = (within(2), within(4))

    def attention(g):
        if g == CHUNKS // halves:
            gathered(1)
        arrived(q_buf.at[pl.ds(g * per_chunk, per_chunk)], q_sem.at[g])
        if g == 0:
            arrived(res_v, pair_sem.at[1])
        columns = slice(g * block, (g + 1) * block)
        attended = attend(g)
        stream = (res_v[:, :, columns].reshape(both, block).astype(F32) + attended.astype(F32)).astype(BF16)
        stream_v[g] = stream
        outg[g] = jnp.dot(chosen, stream, preferred_element_type=F32).astype(BF16).reshape(wave, 16, block)

    def leave(g, rz):
        go(outg.at[g, plane ^ rz], x_buf.at[g, 0, rz], z_sem.at[g, rz], across(rz))

    def spread(g, rz):
        for hop in range(2):
            recv = x_sem.at[g, rz] if rz % 2 == hop else x_sem.at[g, wave]
            go(x_buf.at[g, 0, rz], x_buf.at[g, 1 + hop, rz], recv, near[hop])

    def forward(g, rz):
        arrived(x_buf.at[g, 0, rz], z_sem.at[g, rz])
        spread(g, rz)

    def relay(g, rz):
        hop = rz % 2
        piece = x_buf.at[g, 1 + hop, rz]
        arrived(piece, x_sem.at[g, rz])
        go(piece, x_buf.at[g, 3, rz], x_sem.at[g, wave], near[1 - hop])

    def tell(g):
        ours = pl.ds(pl.multiple_of(other * tokens, tokens), tokens)
        go(stream_v.at[g, ours], stream_all.at[core, g], pair_sem.at[2], partner)
        stream_all[core, g] = stream_v[g, pl.ds(pl.multiple_of(core * tokens, tokens), tokens)]
        x_buf[g, 0, 0] = outg[g, plane]
        spread(g, 0)

    total = {}

    def up(g):
        if g == 0:
            arrived(gain_v, in_sem.at[5])
            arrived(w_v, w_sem.at[0])
        arrived(x_buf.at[g, pl.ds(0, 2)], x_sem.at[g, wave])
        columns = slice(g * block, (g + 1) * block)
        x = x_buf[g].reshape(4 * rows, block).astype(F32)
        square = x * x
        square = sum(square[:, i:i + 128] for i in range(0, block, 128))
        x = (x * gain_v[:, columns]).astype(BF16)
        weight = w_v[:, :, :, columns].reshape(-1, block)
        pre = lax.dot_general(x, weight, (((1,), (1,)), ((), ())), preferred_element_type=F32)
        total["square"] = square if g == 0 else total["square"] + square
        total["pre"] = pre if g == 0 else total["pre"] + pre

    def offer():
        pre = total["pre"]
        units = pre.shape[1]
        square = jnp.sum(total["square"], axis=1, keepdims=True)
        total["square"] = square
        coarse = square.astype(BF16)
        rest = (square - coarse.astype(F32)).astype(BF16)
        lane = lax.broadcasted_iota(jnp.int32, (4 * rows, 128), 1)
        pre_out[:, :units] = pre.astype(BF16)
        pre_out[:, units:] = jnp.where(lane < 64, coarse.astype(F32), rest.astype(F32)).astype(BF16)
        go(pre_out, pre_in, pre_sem, partner)

    def hide():
        units = total["pre"].shape[1]
        arrived(pre_in, pre_sem)
        square = (
            total["square"] + pre_in[:, units:units + 1].astype(F32) + pre_in[:, units + 64:units + 65].astype(F32)
        )
        inverse = lax.rsqrt(square * (1.0 / width) + 1e-06)
        pre = (total["pre"] + pre_in[:, :units].astype(F32)) * inverse
        gate_pre, up_pre = pre[:, :units // 2], pre[:, units // 2:]
        total["hidden"] = (gate_pre / (1.0 + jnp.exp(-gate_pre)) * up_pre).astype(BF16)
        arrived(wd_v, w_sem.at[1])

    def product(blk):
        weight = wd_v[...].reshape(-1, half)
        piece = jnp.dot(total["hidden"][blk * rows:(blk + 1) * rows], weight, preferred_element_type=F32)
        piece = piece.reshape(wave, 16, half)
        return piece[:, :, :quarter], piece[:, :, quarter:]

    def first_hop(rz, sides=(0, 1)):
        for which in sides:
            go(s1.at[which, rz], r1.at[which, rz], r1_sem.at[which, rz], near[which])

    def down(early):
        one, two = product(3)
        s1[0, :, 0], s1[1, :, 0] = one.astype(BF16), two.astype(BF16)
        one, keep[1] = product(1)
        s1[0, :, 1] = one.astype(BF16)
        for rz in early:
            first_hop(rz, (0,))
        keep[0], two = product(2)
        s1[1, :, 1] = two.astype(BF16)
        for rz in early:
            first_hop(rz, (1,))
        own[0], own[1] = product(0)

    def second_hop(rz):
        for which in range(2):
            arrived(r1.at[which, rz], r1_sem.at[which, rz])
            s2[which, rz] = (keep[which, rz] + r1[which, rz, 0].astype(F32)).astype(BF16)
            go(s2.at[which, rz], r2.at[which, rz], r2_sem.at[which, rz], near[1 - which])

    def finish(rz):
        for which in range(2):
            arrived(r2.at[which, rz], r2_sem.at[which, rz])
        sides = [
            own[which, rz] + r1[which, rz, 1].astype(F32) + r2[which, rz].astype(F32) for which in range(2)
        ]
        for c in range(2):
            final[rz, c] = jnp.concatenate([one[c * 8:(c + 1) * 8] for one in sides], axis=0).astype(BF16)
        go(final.at[rz, other], back.at[plane * 2 + core], back_sem, (plane ^ rz) * group + (mine ^ 1))
        if rz:
            go(final.at[rz, core], back.at[plane * 2 + core], back_sem, across(rz))
        else:
            back[plane * 2 + core] = final[0, core]

    for g in range(CHUNKS):
        attention(g)
        for i in range(1, wave):
            leave(g, i)
        tell(g)
        if g >= 2:
            relay(g - 2, 0)

    come = range(1, wave)
    steps = []

    def then(step, *where):
        steps.append((step, *where))

    def many(step, g):
        for rz in come:
            then(step, g, rz)

    many(forward, 0)
    then(relay, 2, 0)
    many(forward, 1)
    then(relay, 3, 0)
    many(forward, 2)
    many(forward, 3)
    many(relay, 0)
    many(relay, 1)
    many(relay, 2)
    many(relay, 3)
    for g in range(CHUNKS):
        then(up, g)
    then(offer)
    then(hide)
    behind = list(range(wave - 1, -1, -1))
    then(down, behind[:WINDOW])
    for n, rz in enumerate(behind):
        then(second_hop, rz)
        if n + WINDOW < wave:
            then(first_hop, behind[n + WINDOW])
        if n >= 1:
            then(finish, behind[n - 1])
    then(finish, behind[-1])
    for step, *where in steps:
        step(*where)
    arrived(back.at[pl.ds(0, 2 * wave - 1)], back_sem)
    arrived(stream_all.at[0], pair_sem.at[2])
    high_mix = mix.astype(BF16)
    rest = mix - high_mix.astype(F32)
    middle = rest.astype(BF16)
    lowest = (rest - middle.astype(F32)).astype(BF16)
    outs = back[...].reshape(wave, 2, 16, quarter).astype(F32)
    for c in range(2):
        for which in range(2):
            rows = outs[:, c, which * 8:(which + 1) * 8].reshape(wave * 8, quarter).astype(BF16)
            added = (
                jnp.dot(lowest, rows, preferred_element_type=F32)
                + jnp.dot(middle, rows, preferred_element_type=F32)
                + jnp.dot(high_mix, rows, preferred_element_type=F32)
            )
            for g in range(CHUNKS // 2):
                at_chunk = which * (CHUNKS // 2) + g
                start = (1 + c, 3 * c)[which] * quarter + g * block
                out[:, start:start + block] = (
                    stream_all[c, at_chunk].astype(F32) + added[:, g * block:(g + 1) * block]
                ).astype(BF16)

    for r in range(1, devices // 2):
        ask(r).wait_send()

    @pl.when(core != side)
    def _():
        ask(0).wait_send()

    for copy in sends:
        copy.wait_send()


def layer(queries, keys, values, span_ids, res, gain, routes, gates, wg, wu, wd):
    devices = lax.axis_size("expert")
    group = FF_WIN // wg.shape[0]
    wave = devices // group
    tokens, width = res.shape
    half = width // 2
    hidden = wg.shape[0]
    both = 2 * tokens
    block = half // CHUNKS
    planes = SPAN // (group * tokens)
    halves = KV_HEADS // 2
    rows = wave * 16
    per_chunk = devices // 2 // CHUNKS
    hbm = pl.BlockSpec(memory_space=pl.ANY)
    dma = pltpu.SemaphoreType.DMA

    def vmem(*shape, dtype=BF16):
        return pltpu.VMEM(shape, dtype)

    scratch = {
        "keys_v": vmem(*keys.shape),
        "values_v": vmem(*values.shape),
        "ids_v": vmem(wave, 1, group * tokens, dtype=jnp.int32),
        "gain_v": vmem(1, half, dtype=F32),
        "routes_v": vmem(*routes.shape[::-1], dtype=jnp.int32),
        "gates_v": vmem(*gates.shape[::-1], dtype=F32),
        "rg_v": vmem(2, 16, 128, dtype=F32),
        "res_v": vmem(2, tokens, half),
        "w_v": vmem(2, 2, hidden, half),
        "wd_v": vmem(2, hidden, half),
        "kv_pack": vmem(KV_HEADS, tokens, 2 * HEAD_DIM),
        "kv_far": vmem(max(planes - 1, 1), KV_HEADS, tokens, 2 * HEAD_DIM),
        "kv_buf": vmem(halves, planes, group, tokens, 2 * HEAD_DIM),
        "q_buf": vmem(devices // 2, both, queries.shape[1]),
        "bias_v": vmem(SPAN, per_chunk * both, dtype=F32),
        "stream_v": vmem(CHUNKS, both, block),
        "stream_all": vmem(2, CHUNKS, tokens, block),
        "outg": vmem(CHUNKS, wave, 16, block),
        "x_buf": vmem(CHUNKS, 4, wave, 16, block),
        "pre_out": vmem(4 * rows, 4 * hidden + 128),
        "pre_in": vmem(4 * rows, 4 * hidden + 128),
        "s1": vmem(2, wave, 2, 16, half // 2),
        "r1": vmem(2, wave, 2, 16, half // 2),
        "s2": vmem(2, wave, 16, half // 2),
        "r2": vmem(2, wave, 16, half // 2),
        "keep": vmem(2, wave, 16, half // 2, dtype=F32),
        "own": vmem(2, wave, 16, half // 2, dtype=F32),
        "final": vmem(wave, 2, 16, half // 2),
        "back": vmem(2 * wave, 16, half // 2),
        "in_sem": dma((6,)),
        "w_sem": dma((2,)),
        "ready_sem": pltpu.SemaphoreType.REGULAR,
        "send_sem": dma(()),
        "ask_sem": dma(()),
        "far_sem": dma((max(planes - 1, 1), halves)),
        "kv_sem": dma((2, halves)),
        "q_sem": dma((CHUNKS,)),
        "pair_sem": dma((3,)),
        "z_sem": dma((CHUNKS, wave)),
        "x_sem": dma((CHUNKS, wave + 1)),
        "pre_sem": dma(()),
        "r1_sem": dma((2, wave)),
        "r2_sem": dma((2, wave)),
        "back_sem": dma(()),
    }
    names = ("queries", "keys", "values", "ids", "res", "gain", "routes", "gates", "wg", "wu", "wd", "out", *scratch)
    return pl.pallas_call(
        functools.partial(moe_kernel, names, group),
        out_shape=pltpu.VMEM((tokens, width), BF16),
        in_specs=[hbm] * 11,
        out_specs=pl.BlockSpec(memory_space=pltpu.VMEM),
        scratch_shapes=list(scratch.values()),
        compiler_params=pltpu.CompilerParams(
            collective_id=0, has_side_effects=True, vmem_limit_bytes=60 * 2**20
        ),
    )(
        queries, keys, values, span_ids.reshape(wave, 1, group * tokens), res, gain.reshape(1, width),
        routes.T, gates.T, wg, wu, wd,
    )


def solution(mesh):
    return jax.shard_map(
        layer,
        mesh=mesh,
        in_specs=(
            P("dp", "expert"),
            P(("dp", "expert"), None),
            P(("dp", "expert"), None),
            P("dp"),
            P(("dp", "expert"), None),
            P(),
            P(("dp", "expert"), None),
            P(("dp", "expert"), None),
            P("expert", None),
            P("expert", None),
            P("expert", None),
        ),
        out_specs=P(("dp", "expert"), None),
        check_vma=False,
    )
```

```python
import functools
import math

import jax
import jax.numpy as jnp
from jax import lax
from jax.experimental import pallas as pl
from jax.experimental.pallas import tpu as pltpu
from jax.sharding import PartitionSpec as P

KV_HEADS = 4
HEAD_DIM = 64
FF_WIN = 1024
SPAN = 512
CHUNKS = 4
WINDOW = 3
SOON = (1,)
MESH = pl.DeviceIdType.MESH
F32 = jnp.float32
BF16 = jnp.bfloat16


def remote(src, dst, send, recv, device):
    return pltpu.make_async_remote_copy(
        src_ref=src, dst_ref=dst, send_sem=send, recv_sem=recv,
        device_id={"expert": device}, device_id_type=MESH,
    )


def arrived(ref, sem):
    pltpu.make_async_copy(ref, ref, sem).wait()


def route_matrix(routes, gates, wave, capacity, cores):
    tokens = routes.shape[0]
    here = tokens // cores
    columns = wave * cores * capacity
    column = lax.broadcasted_iota(jnp.int32, (tokens, columns), 1)
    token = lax.broadcasted_iota(jnp.int32, (tokens, columns), 0)
    one = lax.broadcasted_iota(jnp.int32, (tokens, tokens), 0)
    other = lax.broadcasted_iota(jnp.int32, (tokens, tokens), 1)
    lower = jnp.where((one >= other) & (one // here == other // here), 1.0, 0.0)
    named_wide = jnp.zeros((tokens, columns), F32)
    weight_wide = jnp.zeros((tokens, columns), F32)
    for expert in range(wave):
        hits = routes == expert
        named = jnp.max(jnp.where(hits, 1.0, 0.0), axis=1, keepdims=True)
        weight = jnp.sum(jnp.where(hits, gates, 0.0), axis=1, keepdims=True)
        mask = column // (cores * capacity) == expert
        named_wide = jnp.where(mask, named, named_wide)
        weight_wide = jnp.where(mask, weight, weight_wide)
    count = jnp.dot(lower.astype(BF16), named_wide.astype(BF16), preferred_element_type=F32)
    slot = (column % capacity + 1).astype(F32)
    fits = (count == slot) & (column % (cores * capacity) // capacity == token // here)
    chosen = jnp.where(fits, named_wide, 0.0)
    return chosen, chosen * weight_wide


def moe_kernel(names, group, *refs):
    at = dict(zip(names, refs, strict=True))
    (queries, keys, values, ids, res, gain, routes, gates, wg, wu, wd, out) = (
        at[name] for name in ("queries", "keys", "values", "ids", "res", "gain", "routes", "gates", "wg", "wu", "wd", "out")
    )
    (keys_v, values_v, ids_v, gain_v, routes_v, gates_v, rg_v, res_v, w_v, wd_v) = (
        at[name] for name in ("keys_v", "values_v", "ids_v", "gain_v", "routes_v", "gates_v", "rg_v", "res_v", "w_v", "wd_v")
    )
    (kv_pack, kv_far, kv_buf, q_buf, bias_v, stream_v, stream_all, outg, x_buf, pre_out, pre_in) = (
        at[name] for name in (
            "kv_pack", "kv_far", "kv_buf", "q_buf", "bias_v", "stream_v", "stream_all", "outg", "x_buf", "pre_out", "pre_in")
    )
    (s1, r1, s2, r2, keep, own, final, back) = (
        at[name] for name in ("s1", "r1", "s2", "r2", "keep", "own", "final", "back")
    )
    (far_sem, in_sem, w_sem, ready_sem, send_sem, kv_sem, q_sem, pair_sem, z_sem, x_sem, pre_sem, r1_sem, r2_sem, back_sem) = (
        at[name] for name in (
            "far_sem", "in_sem", "w_sem", "ready_sem", "send_sem", "kv_sem", "q_sem", "pair_sem", "z_sem", "x_sem",
            "pre_sem", "r1_sem", "r2_sem", "back_sem")
    )
    me = lax.axis_index("expert")
    wave = x_buf.shape[2]
    devices = wave * group
    tokens, width = out.shape
    both = 2 * tokens
    half = width // 2
    quarter = half // 2
    block = half // CHUNKS
    rows = wave * 16
    plane = me // group
    mine = me % group
    core = me % 2
    other = 1 - core


    sends = []

    def go(src, dst, recv, device):
        copy = remote(src, dst, send_sem, recv, device)
        copy.start()
        sends.append(copy)

    def early(c):
        return [pl.ds(pl.multiple_of(q * quarter, 128), quarter) for q in (1 + c, 3 * c)]

    def split(source, target, sem, send):
        for n, columns in enumerate(early(core if send is None else other)):
            place = target.at[:, pl.ds(n * quarter, quarter)]
            if send is None:
                pltpu.make_async_copy(source.at[:, columns], place, sem).start()
            else:
                go(source.at[:, columns], place, sem, send)

    def across(rz):
        return (plane ^ rz) * group + mine

    def within(r):
        return plane * group + (mine ^ r)

    partner = within(1)
    fetched = {}
    for number, (name, source, target) in enumerate((
        ("keys", keys, keys_v), ("values", values, values_v), ("routes", routes, routes_v), ("gates", gates, gates_v),
        ("ids", ids, ids_v),
    )):
        fetched[name] = pltpu.make_async_copy(source, target, in_sem.at[number])
        fetched[name].start()
    barrier = pltpu.get_barrier_semaphore()
    partners = [within(r) for r in range(1, group)] + [across(rz) for rz in range(1, wave)]
    for device in partners:
        pl.semaphore_signal(barrier, inc=1, device_id={"expert": device}, device_id_type=MESH)
    split(res, res_v.at[core], pair_sem.at[1], None)
    split(gain, gain_v, in_sem.at[5], None)
    split(wg, w_v.at[0, core], w_sem.at[0], None)
    split(wu, w_v.at[1, core], w_sem.at[0], None)
    split(wd, wd_v.at[core], w_sem.at[1], None)
    pl.semaphore_wait(barrier, len(partners))
    for rz in range(1, wave):
        pl.semaphore_signal(ready_sem, inc=1, device_id={"expert": across(rz)}, device_id_type=MESH)

    for name in ("keys", "values"):
        fetched[name].wait()
    for place, head in enumerate((1, 2, 0, 3)):
        columns = slice(head * HEAD_DIM, (head + 1) * HEAD_DIM)
        kv_pack[place] = jnp.concatenate([keys_v[:, columns], values_v[:, columns]], axis=1)
    planes = SPAN // (group * tokens)
    halves = KV_HEADS // 2
    for h in range(halves):
        for rz in range(1, planes):
            pair = pl.ds(2 * h, 2)
            go(kv_pack.at[pair], kv_far.at[rz - 1, pair], far_sem.at[rz - 1, h], across(rz))

    def share(h, source, at_plane, sem):
        for r in range(1, group):
            go(source.at[2 * h + (core ^ (r % 2))], kv_buf.at[h, at_plane, mine], sem, within(r))
        kv_buf[h, at_plane, mine] = source[2 * h + core]

    share(0, kv_pack, plane % planes, kv_sem.at[0, 0])
    pl.semaphore_wait(ready_sem, wave - 1)
    side = me // (devices // 2)
    number = (me % (devices // 2)) ^ ((1 - side) * (devices // 4))
    per_chunk = devices // 2 // CHUNKS
    query_sem = q_sem.at[number // per_chunk]

    def ask(r):
        pair = (me // 2) ^ r
        source = queries.at[pl.ds(pl.multiple_of(pair * both, both), both)]
        return remote(source, q_buf.at[number], at["ask_sem"], query_sem, pair * 2 + side)

    def ask_planes(distances):
        for rz in distances:
            for r in range((rz + 1) * group // 2 - 1, rz * group // 2 - 1, -1):
                if r:
                    ask(r).start()
        if 0 in distances:

            @pl.when(core == side)
            def _():
                source = queries.at[pl.ds(pl.multiple_of(me // 2 * both, both), both)]
                pltpu.make_async_copy(source, q_buf.at[number], query_sem).start()

            @pl.when(core != side)
            def _():
                ask(0).start()

    distant = list(range(wave - 1, -1, -1))
    soon = SOON

    @pl.when(number < devices // 4)
    def _():
        ask_planes(distant)

    @pl.when(number >= devices // 4)
    def _():
        ask_planes([rz for rz in distant if rz in soon])

    for name in ("routes", "gates"):
        fetched[name].wait()
    rg_v[core, :8, :tokens] = routes_v[...].astype(F32)
    rg_v[core, 8:, :tokens] = gates_v[...]
    go(rg_v.at[core], rg_v.at[core], pair_sem.at[0], partner)
    def pass_on(h):
        for rz in range(1, planes):
            arrived(kv_far.at[rz - 1, pl.ds(2 * h, 2)], far_sem.at[rz - 1, h])
            share(h, kv_far.at[rz - 1], (plane ^ rz) % planes, kv_sem.at[1, h])

    pass_on(0)
    split(res, res_v.at[core], pair_sem.at[1], partner)
    fetched["ids"].wait()
    _, mix = route_matrix(routes_v[...].astype(F32).T, gates_v[...].T, wave, 8, 1)
    arrived(rg_v.at[0], pair_sem.at[0])
    named = jnp.concatenate([rg_v[c, :8, :].T[:tokens] for c in range(2)], axis=0)
    weights = jnp.concatenate([rg_v[c, 8:, :].T[:tokens] for c in range(2)], axis=0)
    chosen, _ = route_matrix(named, weights, wave, 8, 2)
    chosen = chosen.T.astype(BF16)

    stretch = group * tokens
    wide = per_chunk * both
    first = plane // planes * planes
    key_ids = jnp.concatenate(
        [jnp.broadcast_to(ids_v[first + i].astype(F32), (128, stretch)).T for i in range(planes)], axis=0
    )
    key_ids = jnp.concatenate([key_ids] * (wide // 128), axis=1)
    key_at = lax.broadcasted_iota(jnp.int32, (SPAN, wide), 0)
    query_at = (
        lax.broadcasted_iota(jnp.int32, (SPAN, wide), 1) % both
        + ((plane - first) * stretch + mine // 2 * both)
    )
    query_ids = jnp.sum(jnp.where(key_at == query_at, key_ids, 0.0), axis=0, keepdims=True)
    bias_v[...] = jnp.where((key_at <= query_at) & (key_ids == query_ids), 0.0, -jnp.inf)
    share(1, kv_pack, plane % planes, kv_sem.at[0, 1])
    pass_on(1)

    @pl.when(number >= devices // 4)
    def _():
        ask_planes([rz for rz in distant if rz not in soon])

    def gathered(h):
        arrived(kv_buf.at[h, 0, pl.ds(0, group - 1)], kv_sem.at[0, h])
        if planes > 1:
            arrived(kv_buf.at[h, pl.ds(0, planes - 1), pl.ds(0, group - 1)], kv_sem.at[1, h])

    gathered(0)
    split(wg, w_v.at[0, core], w_sem.at[0], partner)
    split(wu, w_v.at[1, core], w_sem.at[0], partner)
    split(wd, wd_v.at[core], w_sem.at[1], partner)

    def attend(g):
        head = g * halves // CHUNKS
        held = kv_buf[head].reshape(SPAN, 2 * HEAD_DIM)
        key_blk = held[:, :HEAD_DIM]
        value_rows = jnp.concatenate([held.T[HEAD_DIM:], jnp.ones((16, SPAN), BF16)], axis=0)
        query = q_buf[g * per_chunk:(g + 1) * per_chunk].reshape(wide, -1) * BF16(1.0 / math.sqrt(HEAD_DIM))
        count = query.shape[1] // HEAD_DIM
        query = jnp.concatenate([query[:, n * HEAD_DIM:(n + 1) * HEAD_DIM] for n in range(count)], axis=0)
        scores = lax.dot_general(key_blk, query, (((1,), (1,)), ((), ())), preferred_element_type=F32)
        scores = scores + jnp.concatenate([bias_v[...]] * count, axis=1)
        raised = jnp.exp(scores - jnp.max(scores, axis=0, keepdims=True)).astype(BF16)
        summed = jnp.dot(value_rows, raised, preferred_element_type=F32)
        summed = summed[:HEAD_DIM] * (1.0 / summed[HEAD_DIM:HEAD_DIM + 1])
        heads = [summed[:, n * wide:(n + 1) * wide] for n in range(count)]
        joined = heads[0] if len(heads) == 1 else jnp.concatenate(heads, axis=0)
        joined = joined.T.astype(BF16)
        return jnp.concatenate([joined[i * both:(i + 1) * both] for i in range(per_chunk)], axis=1)

    near = (within(2), within(4))

    def attention(g):
        if g == CHUNKS // halves:
            gathered(1)
        arrived(q_buf.at[pl.ds(g * per_chunk, per_chunk)], q_sem.at[g])
        if g == 0:
            arrived(res_v, pair_sem.at[1])
        columns = slice(g * block, (g + 1) * block)
        attended = attend(g)
        stream = (res_v[:, :, columns].reshape(both, block).astype(F32) + attended.astype(F32)).astype(BF16)
        stream_v[g] = stream
        outg[g] = jnp.dot(chosen, stream, preferred_element_type=F32).astype(BF16).reshape(wave, 16, block)

    def leave(g, rz):
        go(outg.at[g, plane ^ rz], x_buf.at[g, 0, rz], z_sem.at[g, rz], across(rz))

    def spread(g, rz):
        for hop in range(2):
            recv = x_sem.at[g, rz] if rz % 2 == hop else x_sem.at[g, wave]
            go(x_buf.at[g, 0, rz], x_buf.at[g, 1 + hop, rz], recv, near[hop])

    def forward(g, rz):
        arrived(x_buf.at[g, 0, rz], z_sem.at[g, rz])
        spread(g, rz)

    def relay(g, rz):
        hop = rz % 2
        piece = x_buf.at[g, 1 + hop, rz]
        arrived(piece, x_sem.at[g, rz])
        go(piece, x_buf.at[g, 3, rz], x_sem.at[g, wave], near[1 - hop])

    def tell(g):
        ours = pl.ds(pl.multiple_of(other * tokens, tokens), tokens)
        go(stream_v.at[g, ours], stream_all.at[core, g], pair_sem.at[2], partner)
        stream_all[core, g] = stream_v[g, pl.ds(pl.multiple_of(core * tokens, tokens), tokens)]
        x_buf[g, 0, 0] = outg[g, plane]
        spread(g, 0)

    total = {}

    def up(g):
        if g == 0:
            arrived(gain_v, in_sem.at[5])
            arrived(w_v, w_sem.at[0])
        arrived(x_buf.at[g, pl.ds(0, 2)], x_sem.at[g, wave])
        columns = slice(g * block, (g + 1) * block)
        x = x_buf[g].reshape(4 * rows, block).astype(F32)
        square = x * x
        square = sum(square[:, i:i + 128] for i in range(0, block, 128))
        x = (x * gain_v[:, columns]).astype(BF16)
        weight = w_v[:, :, :, columns].reshape(-1, block)
        pre = lax.dot_general(x, weight, (((1,), (1,)), ((), ())), preferred_element_type=F32)
        total["square"] = square if g == 0 else total["square"] + square
        total["pre"] = pre if g == 0 else total["pre"] + pre

    def offer():
        pre = total["pre"]
        units = pre.shape[1]
        square = jnp.sum(total["square"], axis=1, keepdims=True)
        total["square"] = square
        coarse = square.astype(BF16)
        rest = (square - coarse.astype(F32)).astype(BF16)
        lane = lax.broadcasted_iota(jnp.int32, (4 * rows, 128), 1)
        pre_out[:, :units] = pre.astype(BF16)
        pre_out[:, units:] = jnp.where(lane < 64, coarse.astype(F32), rest.astype(F32)).astype(BF16)
        go(pre_out, pre_in, pre_sem, partner)

    def hide():
        units = total["pre"].shape[1]
        arrived(pre_in, pre_sem)
        square = (
            total["square"] + pre_in[:, units:units + 1].astype(F32) + pre_in[:, units + 64:units + 65].astype(F32)
        )
        inverse = lax.rsqrt(square * (1.0 / width) + 1e-06)
        pre = (total["pre"] + pre_in[:, :units].astype(F32)) * inverse
        gate_pre, up_pre = pre[:, :units // 2], pre[:, units // 2:]
        total["hidden"] = (gate_pre / (1.0 + jnp.exp(-gate_pre)) * up_pre).astype(BF16)
        arrived(wd_v, w_sem.at[1])

    def product(blk):
        weight = wd_v[...].reshape(-1, half)
        piece = jnp.dot(total["hidden"][blk * rows:(blk + 1) * rows], weight, preferred_element_type=F32)
        piece = piece.reshape(wave, 16, half)
        return piece[:, :, :quarter], piece[:, :, quarter:]

    def first_hop(rz, sides=(0, 1)):
        for which in sides:
            go(s1.at[which, rz], r1.at[which, rz], r1_sem.at[which, rz], near[which])

    def down(early):
        one, two = product(3)
        s1[0, :, 0], s1[1, :, 0] = one.astype(BF16), two.astype(BF16)
        one, keep[1] = product(1)
        s1[0, :, 1] = one.astype(BF16)
        for rz in early:
            first_hop(rz, (0,))
        keep[0], two = product(2)
        s1[1, :, 1] = two.astype(BF16)
        for rz in early:
            first_hop(rz, (1,))
        own[0], own[1] = product(0)

    def second_hop(rz):
        for which in range(2):
            arrived(r1.at[which, rz], r1_sem.at[which, rz])
            s2[which, rz] = (keep[which, rz] + r1[which, rz, 0].astype(F32)).astype(BF16)
            go(s2.at[which, rz], r2.at[which, rz], r2_sem.at[which, rz], near[1 - which])

    def finish(rz):
        for which in range(2):
            arrived(r2.at[which, rz], r2_sem.at[which, rz])
        sides = [
            own[which, rz] + r1[which, rz, 1].astype(F32) + r2[which, rz].astype(F32) for which in range(2)
        ]
        for c in range(2):
            final[rz, c] = jnp.concatenate([one[c * 8:(c + 1) * 8] for one in sides], axis=0).astype(BF16)
        go(final.at[rz, other], back.at[plane * 2 + core], back_sem, (plane ^ rz) * group + (mine ^ 1))
        if rz:
            go(final.at[rz, core], back.at[plane * 2 + core], back_sem, across(rz))
        else:
            back[plane * 2 + core] = final[0, core]

    for g in range(CHUNKS):
        attention(g)
        for i in range(1, wave):
            leave(g, i)
        tell(g)
        if g >= 2:
            relay(g - 2, 0)

    come = range(1, wave)
    steps = []

    def then(step, *where):
        steps.append((step, *where))

    def many(step, g):
        for rz in come:
            then(step, g, rz)

    many(forward, 0)
    then(relay, 2, 0)
    many(forward, 1)
    then(relay, 3, 0)
    many(forward, 2)
    many(forward, 3)
    many(relay, 0)
    many(relay, 1)
    many(relay, 2)
    many(relay, 3)
    for g in range(CHUNKS):
        then(up, g)
    then(offer)
    then(hide)
    behind = list(range(wave - 1, -1, -1))
    then(down, behind[:WINDOW])
    for n, rz in enumerate(behind):
        then(second_hop, rz)
        if n + WINDOW < wave:
            then(first_hop, behind[n + WINDOW])
        if n >= 1:
            then(finish, behind[n - 1])
    then(finish, behind[-1])
    for step, *where in steps:
        step(*where)
    arrived(back.at[pl.ds(0, 2 * wave - 1)], back_sem)
    arrived(stream_all.at[0], pair_sem.at[2])
    high_mix = mix.astype(BF16)
    rest = mix - high_mix.astype(F32)
    middle = rest.astype(BF16)
    lowest = (rest - middle.astype(F32)).astype(BF16)
    outs = back[...].reshape(wave, 2, 16, quarter).astype(F32)
    for c in range(2):
        for which in range(2):
            rows = outs[:, c, which * 8:(which + 1) * 8].reshape(wave * 8, quarter).astype(BF16)
            added = (
                jnp.dot(lowest, rows, preferred_element_type=F32)
                + jnp.dot(middle, rows, preferred_element_type=F32)
                + jnp.dot(high_mix, rows, preferred_element_type=F32)
            )
            for g in range(CHUNKS // 2):
                at_chunk = which * (CHUNKS // 2) + g
                start = (1 + c, 3 * c)[which] * quarter + g * block
                out[:, start:start + block] = (
                    stream_all[c, at_chunk].astype(F32) + added[:, g * block:(g + 1) * block]
                ).astype(BF16)

    for r in range(1, devices // 2):
        ask(r).wait_send()

    @pl.when(core != side)
    def _():
        ask(0).wait_send()

    for copy in sends:
        copy.wait_send()


def layer(queries, keys, values, span_ids, res, gain, routes, gates, wg, wu, wd):
    devices = lax.axis_size("expert")
    group = FF_WIN // wg.shape[0]
    wave = devices // group
    tokens, width = res.shape
    half = width // 2
    hidden = wg.shape[0]
    both = 2 * tokens
    block = half // CHUNKS
    planes = SPAN // (group * tokens)
    halves = KV_HEADS // 2
    rows = wave * 16
    per_chunk = devices // 2 // CHUNKS
    hbm = pl.BlockSpec(memory_space=pl.ANY)
    dma = pltpu.SemaphoreType.DMA

    def vmem(*shape, dtype=BF16):
        return pltpu.VMEM(shape, dtype)

    scratch = {
        "keys_v": vmem(*keys.shape),
        "values_v": vmem(*values.shape),
        "ids_v": vmem(wave, 1, group * tokens, dtype=jnp.int32),
        "gain_v": vmem(1, half, dtype=F32),
        "routes_v": vmem(*routes.shape[::-1], dtype=jnp.int32),
        "gates_v": vmem(*gates.shape[::-1], dtype=F32),
        "rg_v": vmem(2, 16, 128, dtype=F32),
        "res_v": vmem(2, tokens, half),
        "w_v": vmem(2, 2, hidden, half),
        "wd_v": vmem(2, hidden, half),
        "kv_pack": vmem(KV_HEADS, tokens, 2 * HEAD_DIM),
        "kv_far": vmem(max(planes - 1, 1), KV_HEADS, tokens, 2 * HEAD_DIM),
        "kv_buf": vmem(halves, planes, group, tokens, 2 * HEAD_DIM),
        "q_buf": vmem(devices // 2, both, queries.shape[1]),
        "bias_v": vmem(SPAN, per_chunk * both, dtype=F32),
        "stream_v": vmem(CHUNKS, both, block),
        "stream_all": vmem(2, CHUNKS, tokens, block),
        "outg": vmem(CHUNKS, wave, 16, block),
        "x_buf": vmem(CHUNKS, 4, wave, 16, block),
        "pre_out": vmem(4 * rows, 4 * hidden + 128),
        "pre_in": vmem(4 * rows, 4 * hidden + 128),
        "s1": vmem(2, wave, 2, 16, half // 2),
        "r1": vmem(2, wave, 2, 16, half // 2),
        "s2": vmem(2, wave, 16, half // 2),
        "r2": vmem(2, wave, 16, half // 2),
        "keep": vmem(2, wave, 16, half // 2, dtype=F32),
        "own": vmem(2, wave, 16, half // 2, dtype=F32),
        "final": vmem(wave, 2, 16, half // 2),
        "back": vmem(2 * wave, 16, half // 2),
        "in_sem": dma((6,)),
        "w_sem": dma((2,)),
        "ready_sem": pltpu.SemaphoreType.REGULAR,
        "send_sem": dma(()),
        "ask_sem": dma(()),
        "far_sem": dma((max(planes - 1, 1), halves)),
        "kv_sem": dma((2, halves)),
        "q_sem": dma((CHUNKS,)),
        "pair_sem": dma((3,)),
        "z_sem": dma((CHUNKS, wave)),
        "x_sem": dma((CHUNKS, wave + 1)),
        "pre_sem": dma(()),
        "r1_sem": dma((2, wave)),
        "r2_sem": dma((2, wave)),
        "back_sem": dma(()),
    }
    names = ("queries", "keys", "values", "ids", "res", "gain", "routes", "gates", "wg", "wu", "wd", "out", *scratch)
    return pl.pallas_call(
        functools.partial(moe_kernel, names, group),
        out_shape=pltpu.VMEM((tokens, width), BF16),
        in_specs=[hbm] * 11,
        out_specs=pl.BlockSpec(memory_space=pltpu.VMEM),
        scratch_shapes=list(scratch.values()),
        compiler_params=pltpu.CompilerParams(
            collective_id=0, has_side_effects=True, vmem_limit_bytes=60 * 2**20
        ),
    )(
        queries, keys, values, span_ids.reshape(wave, 1, group * tokens), res, gain.reshape(1, width),
        routes.T, gates.T, wg, wu, wd,
    )


def solution(mesh):
    return jax.shard_map(
        layer,
        mesh=mesh,
        in_specs=(
            P("dp", "expert"),
            P(("dp", "expert"), None),
            P(("dp", "expert"), None),
            P("dp"),
            P(("dp", "expert"), None),
            P(),
            P(("dp", "expert"), None),
            P(("dp", "expert"), None),
            P("expert", None),
            P("expert", None),
            P("expert", None),
        ),
        out_specs=P(("dp", "expert"), None),
        check_vma=False,
    )
```

```python
import functools
import math

import jax
import jax.numpy as jnp
from jax import lax
from jax.experimental import pallas as pl
from jax.experimental.pallas import tpu as pltpu
from jax.sharding import PartitionSpec as P

KV_HEADS = 4
HEAD_DIM = 64
FF_WIN = 1024
SPAN = 512
CHUNKS = 4
WINDOW = 3
SOON = (1,)
MESH = pl.DeviceIdType.MESH
F32 = jnp.float32
BF16 = jnp.bfloat16


def remote(src, dst, send, recv, device):
    return pltpu.make_async_remote_copy(
        src_ref=src, dst_ref=dst, send_sem=send, recv_sem=recv,
        device_id={"expert": device}, device_id_type=MESH,
    )


def arrived(ref, sem):
    pltpu.make_async_copy(ref, ref, sem).wait()


def route_matrix(routes, gates, wave, capacity, cores):
    tokens = routes.shape[0]
    here = tokens // cores
    columns = wave * cores * capacity
    column = lax.broadcasted_iota(jnp.int32, (tokens, columns), 1)
    token = lax.broadcasted_iota(jnp.int32, (tokens, columns), 0)
    one = lax.broadcasted_iota(jnp.int32, (tokens, tokens), 0)
    other = lax.broadcasted_iota(jnp.int32, (tokens, tokens), 1)
    lower = jnp.where((one >= other) & (one // here == other // here), 1.0, 0.0)
    named_wide = jnp.zeros((tokens, columns), F32)
    weight_wide = jnp.zeros((tokens, columns), F32)
    for expert in range(wave):
        hits = routes == expert
        named = jnp.max(jnp.where(hits, 1.0, 0.0), axis=1, keepdims=True)
        weight = jnp.sum(jnp.where(hits, gates, 0.0), axis=1, keepdims=True)
        mask = column // (cores * capacity) == expert
        named_wide = jnp.where(mask, named, named_wide)
        weight_wide = jnp.where(mask, weight, weight_wide)
    count = jnp.dot(lower.astype(BF16), named_wide.astype(BF16), preferred_element_type=F32)
    slot = (column % capacity + 1).astype(F32)
    fits = (count == slot) & (column % (cores * capacity) // capacity == token // here)
    chosen = jnp.where(fits, named_wide, 0.0)
    return chosen, chosen * weight_wide


def moe_kernel(names, group, *refs):
    at = dict(zip(names, refs, strict=True))
    (queries, keys, values, ids, res, gain, routes, gates, wg, wu, wd, out) = (
        at[name] for name in ("queries", "keys", "values", "ids", "res", "gain", "routes", "gates", "wg", "wu", "wd", "out")
    )
    (keys_v, values_v, ids_v, gain_v, routes_v, gates_v, rg_v, res_v, w_v, wd_v) = (
        at[name] for name in ("keys_v", "values_v", "ids_v", "gain_v", "routes_v", "gates_v", "rg_v", "res_v", "w_v", "wd_v")
    )
    (kv_pack, kv_far, kv_buf, q_buf, bias_v, stream_v, stream_all, outg, x_buf, pre_out, pre_in) = (
        at[name] for name in (
            "kv_pack", "kv_far", "kv_buf", "q_buf", "bias_v", "stream_v", "stream_all", "outg", "x_buf", "pre_out", "pre_in")
    )
    (s1, r1, s2, r2, keep, own, final, back) = (
        at[name] for name in ("s1", "r1", "s2", "r2", "keep", "own", "final", "back")
    )
    (far_sem, in_sem, w_sem, ready_sem, send_sem, kv_sem, q_sem, pair_sem, z_sem, x_sem, pre_sem, r1_sem, r2_sem, back_sem) = (
        at[name] for name in (
            "far_sem", "in_sem", "w_sem", "ready_sem", "send_sem", "kv_sem", "q_sem", "pair_sem", "z_sem", "x_sem",
            "pre_sem", "r1_sem", "r2_sem", "back_sem")
    )
    me = lax.axis_index("expert")
    wave = x_buf.shape[2]
    devices = wave * group
    tokens, width = out.shape
    both = 2 * tokens
    half = width // 2
    quarter = half // 2
    block = half // CHUNKS
    rows = wave * 16
    plane = me // group
    mine = me % group
    core = me % 2
    other = 1 - core


    sends = []

    def go(src, dst, recv, device):
        copy = remote(src, dst, send_sem, recv, device)
        copy.start()
        sends.append(copy)

    def early(c):
        return [pl.ds(pl.multiple_of(q * quarter, 128), quarter) for q in (1 + c, 3 * c)]

    def split(source, target, sem, send):
        for n, columns in enumerate(early(core if send is None else other)):
            place = target.at[:, pl.ds(n * quarter, quarter)]
            if send is None:
                pltpu.make_async_copy(source.at[:, columns], place, sem).start()
            else:
                go(source.at[:, columns], place, sem, send)

    def across(rz):
        return (plane ^ rz) * group + mine

    def within(r):
        return plane * group + (mine ^ r)

    partner = within(1)
    fetched = {}
    for number, (name, source, target) in enumerate((
        ("keys", keys, keys_v), ("values", values, values_v), ("routes", routes, routes_v), ("gates", gates, gates_v),
        ("ids", ids, ids_v),
    )):
        fetched[name] = pltpu.make_async_copy(source, target, in_sem.at[number])
        fetched[name].start()
    barrier = pltpu.get_barrier_semaphore()
    partners = [within(r) for r in range(1, group)] + [across(rz) for rz in range(1, wave)]
    for device in partners:
        pl.semaphore_signal(barrier, inc=1, device_id={"expert": device}, device_id_type=MESH)
    split(res, res_v.at[core], pair_sem.at[1], None)
    split(gain, gain_v, in_sem.at[5], None)
    split(wg, w_v.at[0, core], w_sem.at[0], None)
    split(wu, w_v.at[1, core], w_sem.at[0], None)
    split(wd, wd_v.at[core], w_sem.at[1], None)
    pl.semaphore_wait(barrier, len(partners))
    for rz in range(1, wave):
        pl.semaphore_signal(ready_sem, inc=1, device_id={"expert": across(rz)}, device_id_type=MESH)

    for name in ("keys", "values"):
        fetched[name].wait()
    for place, head in enumerate((1, 2, 0, 3)):
        columns = slice(head * HEAD_DIM, (head + 1) * HEAD_DIM)
        kv_pack[place] = jnp.concatenate([keys_v[:, columns], values_v[:, columns]], axis=1)
    planes = SPAN // (group * tokens)
    halves = KV_HEADS // 2
    for h in range(halves):
        for rz in range(1, planes):
            pair = pl.ds(2 * h, 2)
            go(kv_pack.at[pair], kv_far.at[rz - 1, pair], far_sem.at[rz - 1, h], across(rz))

    def share(h, source, at_plane, sem):
        for r in range(1, group):
            go(source.at[2 * h + (core ^ (r % 2))], kv_buf.at[h, at_plane, mine], sem, within(r))
        kv_buf[h, at_plane, mine] = source[2 * h + core]

    share(0, kv_pack, plane % planes, kv_sem.at[0, 0])
    pl.semaphore_wait(ready_sem, wave - 1)
    side = me // (devices // 2)
    number = (me % (devices // 2)) ^ ((1 - side) * (devices // 4))
    per_chunk = devices // 2 // CHUNKS
    query_sem = q_sem.at[number // per_chunk]

    def ask(r):
        pair = (me // 2) ^ r
        source = queries.at[pl.ds(pl.multiple_of(pair * both, both), both)]
        return remote(source, q_buf.at[number], at["ask_sem"], query_sem, pair * 2 + side)

    def ask_planes(distances):
        for rz in distances:
            for r in range((rz + 1) * group // 2 - 1, rz * group // 2 - 1, -1):
                if r:
                    ask(r).start()
        if 0 in distances:

            @pl.when(core == side)
            def _():
                source = queries.at[pl.ds(pl.multiple_of(me // 2 * both, both), both)]
                pltpu.make_async_copy(source, q_buf.at[number], query_sem).start()

            @pl.when(core != side)
            def _():
                ask(0).start()

    distant = list(range(wave - 1, -1, -1))
    soon = SOON

    @pl.when(number < devices // 4)
    def _():
        ask_planes(distant)

    @pl.when(number >= devices // 4)
    def _():
        ask_planes([rz for rz in distant if rz in soon])

    for name in ("routes", "gates"):
        fetched[name].wait()
    rg_v[core, :8, :tokens] = routes_v[...].astype(F32)
    rg_v[core, 8:, :tokens] = gates_v[...]
    go(rg_v.at[core], rg_v.at[core], pair_sem.at[0], partner)
    def pass_on(h):
        for rz in range(1, planes):
            arrived(kv_far.at[rz - 1, pl.ds(2 * h, 2)], far_sem.at[rz - 1, h])
            share(h, kv_far.at[rz - 1], (plane ^ rz) % planes, kv_sem.at[1, h])

    pass_on(0)
    split(res, res_v.at[core], pair_sem.at[1], partner)
    fetched["ids"].wait()
    _, mix = route_matrix(routes_v[...].astype(F32).T, gates_v[...].T, wave, 8, 1)
    arrived(rg_v.at[0], pair_sem.at[0])
    named = jnp.concatenate([rg_v[c, :8, :].T[:tokens] for c in range(2)], axis=0)
    weights = jnp.concatenate([rg_v[c, 8:, :].T[:tokens] for c in range(2)], axis=0)
    chosen, _ = route_matrix(named, weights, wave, 8, 2)
    chosen = chosen.T.astype(BF16)

    stretch = group * tokens
    wide = per_chunk * both
    first = plane // planes * planes
    key_ids = jnp.concatenate(
        [jnp.broadcast_to(ids_v[first + i].astype(F32), (128, stretch)).T for i in range(planes)], axis=0
    )
    key_ids = jnp.concatenate([key_ids] * (wide // 128), axis=1)
    key_at = lax.broadcasted_iota(jnp.int32, (SPAN, wide), 0)
    query_at = (
        lax.broadcasted_iota(jnp.int32, (SPAN, wide), 1) % both
        + ((plane - first) * stretch + mine // 2 * both)
    )
    query_ids = jnp.sum(jnp.where(key_at == query_at, key_ids, 0.0), axis=0, keepdims=True)
    bias_v[...] = jnp.where((key_at <= query_at) & (key_ids == query_ids), 0.0, -jnp.inf)
    share(1, kv_pack, plane % planes, kv_sem.at[0, 1])
    pass_on(1)

    @pl.when(number >= devices // 4)
    def _():
        ask_planes([rz for rz in distant if rz not in soon])

    def gathered(h):
        arrived(kv_buf.at[h, 0, pl.ds(0, group - 1)], kv_sem.at[0, h])
        if planes > 1:
            arrived(kv_buf.at[h, pl.ds(0, planes - 1), pl.ds(0, group - 1)], kv_sem.at[1, h])

    gathered(0)
    split(wg, w_v.at[0, core], w_sem.at[0], partner)
    split(wu, w_v.at[1, core], w_sem.at[0], partner)
    split(wd, wd_v.at[core], w_sem.at[1], partner)

    def attend(g):
        head = g * halves // CHUNKS
        held = kv_buf[head].reshape(SPAN, 2 * HEAD_DIM)
        key_blk = held[:, :HEAD_DIM]
        value_rows = jnp.concatenate([held.T[HEAD_DIM:], jnp.ones((16, SPAN), BF16)], axis=0)
        query = q_buf[g * per_chunk:(g + 1) * per_chunk].reshape(wide, -1) * BF16(1.0 / math.sqrt(HEAD_DIM))
        count = query.shape[1] // HEAD_DIM
        query = jnp.concatenate([query[:, n * HEAD_DIM:(n + 1) * HEAD_DIM] for n in range(count)], axis=0)
        scores = lax.dot_general(key_blk, query, (((1,), (1,)), ((), ())), preferred_element_type=F32)
        scores = scores + jnp.concatenate([bias_v[...]] * count, axis=1)
        raised = jnp.exp(scores - jnp.max(scores, axis=0, keepdims=True)).astype(BF16)
        summed = jnp.dot(value_rows, raised, preferred_element_type=F32)
        summed = summed[:HEAD_DIM] * (1.0 / summed[HEAD_DIM:HEAD_DIM + 1])
        heads = [summed[:, n * wide:(n + 1) * wide] for n in range(count)]
        joined = heads[0] if len(heads) == 1 else jnp.concatenate(heads, axis=0)
        joined = joined.T.astype(BF16)
        return jnp.concatenate([joined[i * both:(i + 1) * both] for i in range(per_chunk)], axis=1)

    near = (within(2), within(4))

    def attention(g):
        if g == CHUNKS // halves:
            gathered(1)
        arrived(q_buf.at[pl.ds(g * per_chunk, per_chunk)], q_sem.at[g])
        if g == 0:
            arrived(res_v, pair_sem.at[1])
        columns = slice(g * block, (g + 1) * block)
        attended = attend(g)
        stream = (res_v[:, :, columns].reshape(both, block).astype(F32) + attended.astype(F32)).astype(BF16)
        stream_v[g] = stream
        outg[g] = jnp.dot(chosen, stream, preferred_element_type=F32).astype(BF16).reshape(wave, 16, block)

    def leave(g, rz):
        go(outg.at[g, plane ^ rz], x_buf.at[g, 0, rz], z_sem.at[g, rz - 1], across(rz))

    def spread(g, rz):
        for hop in range(2):
            recv = x_sem.at[g, rz] if rz % 2 == hop else x_sem.at[g, wave]
            go(x_buf.at[g, 0, rz], x_buf.at[g, 1 + hop, rz], recv, near[hop])

    def forward(g, rz):
        arrived(x_buf.at[g, 0, rz], z_sem.at[g, rz - 1])
        spread(g, rz)

    def relay(g, rz):
        hop = rz % 2
        piece = x_buf.at[g, 1 + hop, rz]
        arrived(piece, x_sem.at[g, rz])
        go(piece, x_buf.at[g, 3, rz], x_sem.at[g, wave], near[1 - hop])

    def tell(g):
        ours = pl.ds(pl.multiple_of(other * tokens, tokens), tokens)
        go(stream_v.at[g, ours], stream_all.at[core, g], pair_sem.at[2], partner)
        stream_all[core, g] = stream_v[g, pl.ds(pl.multiple_of(core * tokens, tokens), tokens)]
        x_buf[g, 0, 0] = outg[g, plane]
        spread(g, 0)

    total = {}

    def up(g):
        if g == 0:
            arrived(gain_v, in_sem.at[5])
            arrived(w_v, w_sem.at[0])
        arrived(x_buf.at[g, pl.ds(0, 2)], x_sem.at[g, wave])
        columns = slice(g * block, (g + 1) * block)
        x = x_buf[g].reshape(4 * rows, block).astype(F32)
        square = x * x
        square = sum(square[:, i:i + 128] for i in range(0, block, 128))
        x = (x * gain_v[:, columns]).astype(BF16)
        weight = w_v[:, :, :, columns].reshape(-1, block)
        pre = lax.dot_general(x, weight, (((1,), (1,)), ((), ())), preferred_element_type=F32)
        total["square"] = square if g == 0 else total["square"] + square
        total["pre"] = pre if g == 0 else total["pre"] + pre

    def offer():
        pre = total["pre"]
        units = pre.shape[1]
        square = jnp.sum(total["square"], axis=1, keepdims=True)
        total["square"] = square
        coarse = square.astype(BF16)
        rest = (square - coarse.astype(F32)).astype(BF16)
        lane = lax.broadcasted_iota(jnp.int32, (4 * rows, 128), 1)
        pre_out[:, :units] = pre.astype(BF16)
        pre_out[:, units:] = jnp.where(lane < 64, coarse.astype(F32), rest.astype(F32)).astype(BF16)
        go(pre_out, pre_in, pre_sem, partner)

    def hide():
        units = total["pre"].shape[1]
        arrived(pre_in, pre_sem)
        square = (
            total["square"] + pre_in[:, units:units + 1].astype(F32) + pre_in[:, units + 64:units + 65].astype(F32)
        )
        inverse = lax.rsqrt(square * (1.0 / width) + 1e-06)
        pre = (total["pre"] + pre_in[:, :units].astype(F32)) * inverse
        gate_pre, up_pre = pre[:, :units // 2], pre[:, units // 2:]
        total["hidden"] = (gate_pre / (1.0 + jnp.exp(-gate_pre)) * up_pre).astype(BF16)
        arrived(wd_v, w_sem.at[1])

    def product(blks, which):
        hidden = jnp.concatenate([total["hidden"][blk * rows:(blk + 1) * rows] for blk in blks], axis=0)
        weight = wd_v[:, :, which * quarter:(which + 1) * quarter].reshape(-1, quarter)
        return jnp.dot(hidden, weight, preferred_element_type=F32).reshape(2, wave, 16, quarter)

    def first_hop(rz, sides=(0, 1)):
        for which in sides:
            go(s1.at[which, rz], r1.at[which, rz], r1_sem.at[which, rz], near[which])

    def down(early):
        for which in range(2):
            piece = product((3, 1 + which), which).astype(BF16)
            s1[which, :, 0], s1[which, :, 1] = piece[0], piece[1]
            for rz in early:
                first_hop(rz, (which,))
        for which in range(2):
            keep[which], own[which] = product((2 - which, 0), which)

    def second_hop(rz):
        for which in range(2):
            arrived(r1.at[which, rz], r1_sem.at[which, rz])
            s2[which, rz] = (keep[which, rz] + r1[which, rz, 0].astype(F32)).astype(BF16)
            go(s2.at[which, rz], r2.at[which, rz], r2_sem.at[rz], near[1 - which])

    def finish(rz):
        arrived(r2.at[:, rz], r2_sem.at[rz])
        sides = [
            own[which, rz] + r1[which, rz, 1].astype(F32) + r2[which, rz].astype(F32) for which in range(2)
        ]
        for c in range(2):
            final[rz, c] = jnp.concatenate([one[c * 8:(c + 1) * 8] for one in sides], axis=0).astype(BF16)
        go(final.at[rz, other], back.at[plane * 2 + core], back_sem, (plane ^ rz) * group + (mine ^ 1))
        if rz:
            go(final.at[rz, core], back.at[plane * 2 + core], back_sem, across(rz))
        else:
            back[plane * 2 + core] = final[0, core]

    for g in range(CHUNKS):
        attention(g)
        for i in range(1, wave):
            leave(g, i)
        tell(g)
        if g >= 2:
            relay(g - 2, 0)

    come = range(1, wave)
    steps = []

    def then(step, *where):
        steps.append((step, *where))

    def many(step, g):
        for rz in come:
            then(step, g, rz)

    many(forward, 0)
    then(relay, 2, 0)
    many(forward, 1)
    then(relay, 3, 0)
    many(forward, 2)
    many(forward, 3)
    many(relay, 0)
    many(relay, 1)
    many(relay, 2)
    many(relay, 3)
    for g in range(CHUNKS):
        then(up, g)
    then(offer)
    then(hide)
    behind = list(range(wave - 1, -1, -1))
    then(down, behind[:WINDOW])
    for n, rz in enumerate(behind):
        then(second_hop, rz)
        if n + WINDOW < wave:
            then(first_hop, behind[n + WINDOW])
        if n >= 1:
            then(finish, behind[n - 1])
    then(finish, behind[-1])
    for step, *where in steps:
        step(*where)
    arrived(back.at[pl.ds(0, 2 * wave - 1)], back_sem)
    arrived(stream_all.at[0], pair_sem.at[2])
    high_mix = mix.astype(BF16)
    rest = mix - high_mix.astype(F32)
    middle = rest.astype(BF16)
    lowest = (rest - middle.astype(F32)).astype(BF16)
    outs = back[...].reshape(wave, 2, 16, quarter).astype(F32)
    for c in range(2):
        for which in range(2):
            rows = outs[:, c, which * 8:(which + 1) * 8].reshape(wave * 8, quarter).astype(BF16)
            added = (
                jnp.dot(lowest, rows, preferred_element_type=F32)
                + jnp.dot(middle, rows, preferred_element_type=F32)
                + jnp.dot(high_mix, rows, preferred_element_type=F32)
            )
            for g in range(CHUNKS // 2):
                at_chunk = which * (CHUNKS // 2) + g
                start = (1 + c, 3 * c)[which] * quarter + g * block
                out[:, start:start + block] = (
                    stream_all[c, at_chunk].astype(F32) + added[:, g * block:(g + 1) * block]
                ).astype(BF16)

    for r in range(1, devices // 2):
        ask(r).wait_send()

    @pl.when(core != side)
    def _():
        ask(0).wait_send()

    for copy in sends:
        copy.wait_send()


def layer(queries, keys, values, span_ids, res, gain, routes, gates, wg, wu, wd):
    devices = lax.axis_size("expert")
    group = FF_WIN // wg.shape[0]
    wave = devices // group
    tokens, width = res.shape
    half = width // 2
    hidden = wg.shape[0]
    both = 2 * tokens
    block = half // CHUNKS
    planes = SPAN // (group * tokens)
    halves = KV_HEADS // 2
    rows = wave * 16
    per_chunk = devices // 2 // CHUNKS
    hbm = pl.BlockSpec(memory_space=pl.ANY)
    dma = pltpu.SemaphoreType.DMA

    def vmem(*shape, dtype=BF16):
        return pltpu.VMEM(shape, dtype)

    scratch = {
        "keys_v": vmem(*keys.shape),
        "values_v": vmem(*values.shape),
        "ids_v": vmem(wave, 1, group * tokens, dtype=jnp.int32),
        "gain_v": vmem(1, half, dtype=F32),
        "routes_v": vmem(*routes.shape[::-1], dtype=jnp.int32),
        "gates_v": vmem(*gates.shape[::-1], dtype=F32),
        "rg_v": vmem(2, 16, 128, dtype=F32),
        "res_v": vmem(2, tokens, half),
        "w_v": vmem(2, 2, hidden, half),
        "wd_v": vmem(2, hidden, half),
        "kv_pack": vmem(KV_HEADS, tokens, 2 * HEAD_DIM),
        "kv_far": vmem(max(planes - 1, 1), KV_HEADS, tokens, 2 * HEAD_DIM),
        "kv_buf": vmem(halves, planes, group, tokens, 2 * HEAD_DIM),
        "q_buf": vmem(devices // 2, both, queries.shape[1]),
        "bias_v": vmem(SPAN, per_chunk * both, dtype=F32),
        "stream_v": vmem(CHUNKS, both, block),
        "stream_all": vmem(2, CHUNKS, tokens, block),
        "outg": vmem(CHUNKS, wave, 16, block),
        "x_buf": vmem(CHUNKS, 4, wave, 16, block),
        "pre_out": vmem(4 * rows, 4 * hidden + 128),
        "pre_in": vmem(4 * rows, 4 * hidden + 128),
        "s1": vmem(2, wave, 2, 16, half // 2),
        "r1": vmem(2, wave, 2, 16, half // 2),
        "s2": vmem(2, wave, 16, half // 2),
        "r2": vmem(2, wave, 16, half // 2),
        "keep": vmem(2, wave, 16, half // 2, dtype=F32),
        "own": vmem(2, wave, 16, half // 2, dtype=F32),
        "final": vmem(wave, 2, 16, half // 2),
        "back": vmem(2 * wave, 16, half // 2),
        "in_sem": dma((6,)),
        "w_sem": dma((2,)),
        "ready_sem": pltpu.SemaphoreType.REGULAR,
        "send_sem": dma(()),
        "ask_sem": dma(()),
        "far_sem": dma((max(planes - 1, 1), halves)),
        "kv_sem": dma((2, halves)),
        "q_sem": dma((CHUNKS,)),
        "pair_sem": dma((3,)),
        "z_sem": dma((CHUNKS, wave - 1)),
        "x_sem": dma((CHUNKS, wave + 1)),
        "pre_sem": dma(()),
        "r1_sem": dma((2, wave)),
        "r2_sem": dma((wave,)),
        "back_sem": dma(()),
    }
    names = ("queries", "keys", "values", "ids", "res", "gain", "routes", "gates", "wg", "wu", "wd", "out", *scratch)
    return pl.pallas_call(
        functools.partial(moe_kernel, names, group),
        out_shape=pltpu.VMEM((tokens, width), BF16),
        in_specs=[hbm] * 11,
        out_specs=pl.BlockSpec(memory_space=pltpu.VMEM),
        scratch_shapes=list(scratch.values()),
        compiler_params=pltpu.CompilerParams(
            collective_id=0, has_side_effects=True, vmem_limit_bytes=60 * 2**20
        ),
    )(
        queries, keys, values, span_ids.reshape(wave, 1, group * tokens), res, gain.reshape(1, width),
        routes.T, gates.T, wg, wu, wd,
    )


def solution(mesh):
    return jax.shard_map(
        layer,
        mesh=mesh,
        in_specs=(
            P("dp", "expert"),
            P(("dp", "expert"), None),
            P(("dp", "expert"), None),
            P("dp"),
            P(("dp", "expert"), None),
            P(),
            P(("dp", "expert"), None),
            P(("dp", "expert"), None),
            P("expert", None),
            P("expert", None),
            P("expert", None),
        ),
        out_specs=P(("dp", "expert"), None),
        check_vma=False,
    )
```

```python
import functools
import math

import jax
import jax.numpy as jnp
from jax import lax
from jax.experimental import pallas as pl
from jax.experimental.pallas import tpu as pltpu
from jax.sharding import PartitionSpec as P

KV_HEADS = 4
HEAD_DIM = 64
FF_WIN = 1024
SPAN = 512
CHUNKS = 4
WINDOW = 3
SOON = (1,)
MESH = pl.DeviceIdType.MESH
F32 = jnp.float32
BF16 = jnp.bfloat16


def remote(src, dst, send, recv, device):
    return pltpu.make_async_remote_copy(
        src_ref=src, dst_ref=dst, send_sem=send, recv_sem=recv,
        device_id={"expert": device}, device_id_type=MESH,
    )


def arrived(ref, sem):
    pltpu.make_async_copy(ref, ref, sem).wait()


def route_matrix(routes, gates, wave, capacity, cores):
    tokens = routes.shape[0]
    here = tokens // cores
    columns = wave * cores * capacity
    column = lax.broadcasted_iota(jnp.int32, (tokens, columns), 1)
    token = lax.broadcasted_iota(jnp.int32, (tokens, columns), 0)
    one = lax.broadcasted_iota(jnp.int32, (tokens, tokens), 0)
    other = lax.broadcasted_iota(jnp.int32, (tokens, tokens), 1)
    lower = jnp.where((one >= other) & (one // here == other // here), 1.0, 0.0)
    named_wide = jnp.zeros((tokens, columns), F32)
    weight_wide = jnp.zeros((tokens, columns), F32)
    for expert in range(wave):
        hits = routes == expert
        named = jnp.max(jnp.where(hits, 1.0, 0.0), axis=1, keepdims=True)
        weight = jnp.sum(jnp.where(hits, gates, 0.0), axis=1, keepdims=True)
        mask = column // (cores * capacity) == expert
        named_wide = jnp.where(mask, named, named_wide)
        weight_wide = jnp.where(mask, weight, weight_wide)
    count = jnp.dot(lower.astype(BF16), named_wide.astype(BF16), preferred_element_type=F32)
    slot = (column % capacity + 1).astype(F32)
    fits = (count == slot) & (column % (cores * capacity) // capacity == token // here)
    chosen = jnp.where(fits, named_wide, 0.0)
    return chosen, chosen * weight_wide


def moe_kernel(names, group, *refs):
    at = dict(zip(names, refs, strict=True))
    (queries, keys, values, ids, res, gain, routes, gates, wg, wu, wd, out) = (
        at[name] for name in ("queries", "keys", "values", "ids", "res", "gain", "routes", "gates", "wg", "wu", "wd", "out")
    )
    (keys_v, values_v, ids_v, gain_v, routes_v, gates_v, rg_v, res_v, w_v, wd_v) = (
        at[name] for name in ("keys_v", "values_v", "ids_v", "gain_v", "routes_v", "gates_v", "rg_v", "res_v", "w_v", "wd_v")
    )
    (kv_pack, kv_far, kv_buf, q_buf, bias_v, stream_v, stream_all, outg, x_buf, pre_out, pre_in) = (
        at[name] for name in (
            "kv_pack", "kv_far", "kv_buf", "q_buf", "bias_v", "stream_v", "stream_all", "outg", "x_buf", "pre_out", "pre_in")
    )
    (s1, r1, s2, r2, keep, own, final, back) = (
        at[name] for name in ("s1", "r1", "s2", "r2", "keep", "own", "final", "back")
    )
    (far_sem, in_sem, w_sem, ready_sem, send_sem, kv_sem, q_sem, pair_sem, z_sem, x_sem, pre_sem, r1_sem, r2_sem, back_sem) = (
        at[name] for name in (
            "far_sem", "in_sem", "w_sem", "ready_sem", "send_sem", "kv_sem", "q_sem", "pair_sem", "z_sem", "x_sem",
            "pre_sem", "r1_sem", "r2_sem", "back_sem")
    )
    me = lax.axis_index("expert")
    wave = x_buf.shape[2]
    devices = wave * group
    tokens, width = out.shape
    both = 2 * tokens
    half = width // 2
    quarter = half // 2
    block = half // CHUNKS
    rows = wave * 16
    plane = me // group
    mine = me % group
    core = me % 2
    other = 1 - core


    sends = []

    def go(src, dst, recv, device):
        copy = remote(src, dst, send_sem, recv, device)
        copy.start()
        sends.append(copy)

    def early(c):
        return [pl.ds(pl.multiple_of(q * quarter, 128), quarter) for q in (1 + c, 3 * c)]

    def split(source, target, sem, send):
        for n, columns in enumerate(early(core if send is None else other)):
            place = target.at[:, pl.ds(n * quarter, quarter)]
            if send is None:
                pltpu.make_async_copy(source.at[:, columns], place, sem).start()
            else:
                go(source.at[:, columns], place, sem, send)

    def across(rz):
        return (plane ^ rz) * group + mine

    def within(r):
        return plane * group + (mine ^ r)

    partner = within(1)
    fetched = {}
    for number, (name, source, target) in enumerate((
        ("keys", keys, keys_v), ("values", values, values_v), ("routes", routes, routes_v), ("gates", gates, gates_v),
        ("ids", ids, ids_v),
    )):
        fetched[name] = pltpu.make_async_copy(source, target, in_sem.at[number])
        fetched[name].start()
    barrier = pltpu.get_barrier_semaphore()
    partners = [within(r) for r in range(1, group)] + [across(rz) for rz in range(1, wave)]
    for device in partners:
        pl.semaphore_signal(barrier, inc=1, device_id={"expert": device}, device_id_type=MESH)
    split(res, res_v.at[core], pair_sem.at[1], None)
    split(gain, gain_v, in_sem.at[5], None)
    split(wg, w_v.at[0, core], w_sem.at[0], None)
    split(wu, w_v.at[1, core], w_sem.at[0], None)
    split(wd, wd_v.at[core], w_sem.at[1], None)
    pl.semaphore_wait(barrier, len(partners))
    for rz in range(1, wave):
        pl.semaphore_signal(ready_sem, inc=1, device_id={"expert": across(rz)}, device_id_type=MESH)

    for name in ("keys", "values"):
        fetched[name].wait()
    for place, head in enumerate((1, 2, 0, 3)):
        columns = slice(head * HEAD_DIM, (head + 1) * HEAD_DIM)
        kv_pack[place] = jnp.concatenate([keys_v[:, columns], values_v[:, columns]], axis=1)
    planes = SPAN // (group * tokens)
    halves = KV_HEADS // 2
    for h in range(halves):
        for rz in range(1, planes):
            pair = pl.ds(2 * h, 2)
            go(kv_pack.at[pair], kv_far.at[rz - 1, pair], far_sem.at[rz - 1, h], across(rz))

    def share(h, source, at_plane, sem):
        for r in range(1, group):
            go(source.at[2 * h + (core ^ (r % 2))], kv_buf.at[h, at_plane, mine], sem, within(r))
        kv_buf[h, at_plane, mine] = source[2 * h + core]

    share(0, kv_pack, plane % planes, kv_sem.at[0, 0])
    pl.semaphore_wait(ready_sem, wave - 1)
    side = me // (devices // 2)
    number = (me % (devices // 2)) ^ ((1 - side) * (devices // 4))
    per_chunk = devices // 2 // CHUNKS
    query_sem = q_sem.at[number // per_chunk]

    def ask(r):
        pair = (me // 2) ^ r
        source = queries.at[pl.ds(pl.multiple_of(pair * both, both), both)]
        return remote(source, q_buf.at[number], at["ask_sem"], query_sem, pair * 2 + side)

    def ask_planes(distances):
        for rz in distances:
            for r in range((rz + 1) * group // 2 - 1, rz * group // 2 - 1, -1):
                if r:
                    ask(r).start()
        if 0 in distances:

            @pl.when(core == side)
            def _():
                source = queries.at[pl.ds(pl.multiple_of(me // 2 * both, both), both)]
                pltpu.make_async_copy(source, q_buf.at[number], query_sem).start()

            @pl.when(core != side)
            def _():
                ask(0).start()

    distant = list(range(wave - 1, -1, -1))
    soon = SOON

    @pl.when(number < devices // 4)
    def _():
        ask_planes(distant[:-1])

    @pl.when(number >= devices // 4)
    def _():
        ask_planes([rz for rz in distant if rz in soon])

    for name in ("routes", "gates"):
        fetched[name].wait()
    rg_v[core, :8, :tokens] = routes_v[...].astype(F32)
    rg_v[core, 8:, :tokens] = gates_v[...]
    go(rg_v.at[core], rg_v.at[core], pair_sem.at[0], partner)
    def pass_on(h):
        for rz in range(1, planes):
            arrived(kv_far.at[rz - 1, pl.ds(2 * h, 2)], far_sem.at[rz - 1, h])
            share(h, kv_far.at[rz - 1], (plane ^ rz) % planes, kv_sem.at[1, h])

    pass_on(0)

    @pl.when(number < devices // 4)
    def _():
        ask_planes([0])

    split(res, res_v.at[core], pair_sem.at[1], partner)
    fetched["ids"].wait()
    _, mix = route_matrix(routes_v[...].astype(F32).T, gates_v[...].T, wave, 8, 1)
    arrived(rg_v.at[0], pair_sem.at[0])
    named = jnp.concatenate([rg_v[c, :8, :].T[:tokens] for c in range(2)], axis=0)
    weights = jnp.concatenate([rg_v[c, 8:, :].T[:tokens] for c in range(2)], axis=0)
    chosen, _ = route_matrix(named, weights, wave, 8, 2)
    chosen = chosen.T.astype(BF16)

    stretch = group * tokens
    wide = per_chunk * both
    first = plane // planes * planes
    key_ids = jnp.concatenate(
        [jnp.broadcast_to(ids_v[first + i].astype(F32), (128, stretch)).T for i in range(planes)], axis=0
    )
    key_ids = jnp.concatenate([key_ids] * (wide // 128), axis=1)
    key_at = lax.broadcasted_iota(jnp.int32, (SPAN, wide), 0)
    query_at = (
        lax.broadcasted_iota(jnp.int32, (SPAN, wide), 1) % both
        + ((plane - first) * stretch + mine // 2 * both)
    )
    query_ids = jnp.sum(jnp.where(key_at == query_at, key_ids, 0.0), axis=0, keepdims=True)
    bias_v[...] = jnp.where((key_at <= query_at) & (key_ids == query_ids), 0.0, -jnp.inf)
    share(1, kv_pack, plane % planes, kv_sem.at[0, 1])
    pass_on(1)

    @pl.when(number >= devices // 4)
    def _():
        ask_planes([rz for rz in distant if rz not in soon])

    def gathered(h):
        arrived(kv_buf.at[h, 0, pl.ds(0, group - 1)], kv_sem.at[0, h])
        if planes > 1:
            arrived(kv_buf.at[h, pl.ds(0, planes - 1), pl.ds(0, group - 1)], kv_sem.at[1, h])

    gathered(0)
    split(wg, w_v.at[0, core], w_sem.at[0], partner)
    split(wu, w_v.at[1, core], w_sem.at[0], partner)
    split(wd, wd_v.at[core], w_sem.at[1], partner)

    def attend(g):
        head = g * halves // CHUNKS
        held = kv_buf[head].reshape(SPAN, 2 * HEAD_DIM)
        key_blk = held[:, :HEAD_DIM]
        value_rows = jnp.concatenate([held.T[HEAD_DIM:], jnp.ones((16, SPAN), BF16)], axis=0)
        query = q_buf[g * per_chunk:(g + 1) * per_chunk].reshape(wide, -1) * BF16(1.0 / math.sqrt(HEAD_DIM))
        count = query.shape[1] // HEAD_DIM
        query = jnp.concatenate([query[:, n * HEAD_DIM:(n + 1) * HEAD_DIM] for n in range(count)], axis=0)
        scores = lax.dot_general(key_blk, query, (((1,), (1,)), ((), ())), preferred_element_type=F32)
        scores = scores + jnp.concatenate([bias_v[...]] * count, axis=1)
        raised = jnp.exp(scores - jnp.max(scores, axis=0, keepdims=True)).astype(BF16)
        summed = jnp.dot(value_rows, raised, preferred_element_type=F32)
        summed = summed[:HEAD_DIM] * (1.0 / summed[HEAD_DIM:HEAD_DIM + 1])
        heads = [summed[:, n * wide:(n + 1) * wide] for n in range(count)]
        joined = heads[0] if len(heads) == 1 else jnp.concatenate(heads, axis=0)
        joined = joined.T.astype(BF16)
        return jnp.concatenate([joined[i * both:(i + 1) * both] for i in range(per_chunk)], axis=1)

    near = (within(2), within(4))

    def attention(g):
        if g == CHUNKS // halves:
            gathered(1)
        arrived(q_buf.at[pl.ds(g * per_chunk, per_chunk)], q_sem.at[g])
        if g == 0:
            arrived(res_v, pair_sem.at[1])
        columns = slice(g * block, (g + 1) * block)
        attended = attend(g)
        stream = (res_v[:, :, columns].reshape(both, block).astype(F32) + attended.astype(F32)).astype(BF16)
        stream_v[g] = stream
        outg[g] = jnp.dot(chosen, stream, preferred_element_type=F32).astype(BF16).reshape(wave, 16, block)

    def leave(g, rz):
        go(outg.at[g, plane ^ rz], x_buf.at[g, 0, rz], z_sem.at[g, rz - 1], across(rz))

    def spread(g, rz):
        for hop in range(2):
            recv = x_sem.at[g, rz] if rz % 2 == hop else x_sem.at[g, wave]
            go(x_buf.at[g, 0, rz], x_buf.at[g, 1 + hop, rz], recv, near[hop])

    def forward(g, rz):
        arrived(x_buf.at[g, 0, rz], z_sem.at[g, rz - 1])
        spread(g, rz)

    def relay(g, rz):
        hop = rz % 2
        piece = x_buf.at[g, 1 + hop, rz]
        arrived(piece, x_sem.at[g, rz])
        go(piece, x_buf.at[g, 3, rz], x_sem.at[g, wave], near[1 - hop])

    def tell(g):
        ours = pl.ds(pl.multiple_of(other * tokens, tokens), tokens)
        go(stream_v.at[g, ours], stream_all.at[core, g], pair_sem.at[2], partner)
        stream_all[core, g] = stream_v[g, pl.ds(pl.multiple_of(core * tokens, tokens), tokens)]
        x_buf[g, 0, 0] = outg[g, plane]
        spread(g, 0)

    total = {}

    def up(g):
        if g == 0:
            arrived(gain_v, in_sem.at[5])
            arrived(w_v, w_sem.at[0])
        arrived(x_buf.at[g, pl.ds(0, 2)], x_sem.at[g, wave])
        columns = slice(g * block, (g + 1) * block)
        x = x_buf[g].reshape(4 * rows, block).astype(F32)
        square = x * x
        square = sum(square[:, i:i + 128] for i in range(0, block, 128))
        x = (x * gain_v[:, columns]).astype(BF16)
        weight = w_v[:, :, :, columns].reshape(-1, block)
        pre = lax.dot_general(x, weight, (((1,), (1,)), ((), ())), preferred_element_type=F32)
        total["square"] = square if g == 0 else total["square"] + square
        total["pre"] = pre if g == 0 else total["pre"] + pre

    def offer():
        pre = total["pre"]
        units = pre.shape[1]
        square = jnp.sum(total["square"], axis=1, keepdims=True)
        total["square"] = square
        coarse = square.astype(BF16)
        rest = (square - coarse.astype(F32)).astype(BF16)
        lane = lax.broadcasted_iota(jnp.int32, (4 * rows, 128), 1)
        pre_out[:, :units] = pre.astype(BF16)
        pre_out[:, units:] = jnp.where(lane < 64, coarse.astype(F32), rest.astype(F32)).astype(BF16)
        go(pre_out, pre_in, pre_sem, partner)

    def hide():
        units = total["pre"].shape[1]
        arrived(pre_in, pre_sem)
        square = (
            total["square"] + pre_in[:, units:units + 1].astype(F32) + pre_in[:, units + 64:units + 65].astype(F32)
        )
        inverse = lax.rsqrt(square * (1.0 / width) + 1e-06)
        pre = (total["pre"] + pre_in[:, :units].astype(F32)) * inverse
        gate_pre, up_pre = pre[:, :units // 2], pre[:, units // 2:]
        total["hidden"] = (gate_pre / (1.0 + jnp.exp(-gate_pre)) * up_pre).astype(BF16)
        arrived(wd_v, w_sem.at[1])

    def product(blks, which):
        hidden = jnp.concatenate([total["hidden"][blk * rows:(blk + 1) * rows] for blk in blks], axis=0)
        weight = wd_v[:, :, which * quarter:(which + 1) * quarter].reshape(-1, quarter)
        return jnp.dot(hidden, weight, preferred_element_type=F32).reshape(2, wave, 16, quarter)

    def first_hop(rz, sides=(0, 1)):
        for which in sides:
            go(s1.at[which, rz], r1.at[which, rz], r1_sem.at[which, rz], near[which])

    def down(early):
        for which in range(2):
            piece = product((3, 1 + which), which).astype(BF16)
            s1[which, :, 0], s1[which, :, 1] = piece[0], piece[1]
            for rz in early:
                first_hop(rz, (which,))
        for which in range(2):
            keep[which], own[which] = product((2 - which, 0), which)

    def second_hop(rz):
        for which in range(2):
            arrived(r1.at[which, rz], r1_sem.at[which, rz])
            s2[which, rz] = (keep[which, rz] + r1[which, rz, 0].astype(F32)).astype(BF16)
            go(s2.at[which, rz], r2.at[which, rz], r2_sem.at[rz], near[1 - which])

    def finish(rz):
        arrived(r2.at[:, rz], r2_sem.at[rz])
        sides = [
            own[which, rz] + r1[which, rz, 1].astype(F32) + r2[which, rz].astype(F32) for which in range(2)
        ]
        for c in range(2):
            final[rz, c] = jnp.concatenate([one[c * 8:(c + 1) * 8] for one in sides], axis=0).astype(BF16)
        go(final.at[rz, other], back.at[plane * 2 + core], back_sem, (plane ^ rz) * group + (mine ^ 1))
        if rz:
            go(final.at[rz, core], back.at[plane * 2 + core], back_sem, across(rz))
        else:
            back[plane * 2 + core] = final[0, core]

    for g in range(CHUNKS):
        attention(g)
        for i in range(1, wave):
            leave(g, i)
        tell(g)
        if g >= 2:
            relay(g - 2, 0)

    come = range(1, wave)
    steps = []

    def then(step, *where):
        steps.append((step, *where))

    def many(step, g):
        for rz in come:
            then(step, g, rz)

    many(forward, 0)
    then(relay, 2, 0)
    many(forward, 1)
    then(relay, 3, 0)
    many(forward, 2)
    many(forward, 3)
    many(relay, 0)
    many(relay, 1)
    many(relay, 2)
    many(relay, 3)
    for g in range(CHUNKS):
        then(up, g)
    then(offer)
    then(hide)
    behind = list(range(wave - 1, -1, -1))
    then(down, behind[:WINDOW])
    for n, rz in enumerate(behind):
        then(second_hop, rz)
        if n + WINDOW < wave:
            then(first_hop, behind[n + WINDOW])
        if n >= 1:
            then(finish, behind[n - 1])
    then(finish, behind[-1])
    for step, *where in steps:
        step(*where)
    arrived(back.at[pl.ds(0, 2 * wave - 1)], back_sem)
    arrived(stream_all.at[0], pair_sem.at[2])
    high_mix = mix.astype(BF16)
    rest = mix - high_mix.astype(F32)
    middle = rest.astype(BF16)
    lowest = (rest - middle.astype(F32)).astype(BF16)
    outs = back[...].reshape(wave, 2, 16, quarter).astype(F32)
    for c in range(2):
        for which in range(2):
            rows = outs[:, c, which * 8:(which + 1) * 8].reshape(wave * 8, quarter).astype(BF16)
            added = (
                jnp.dot(lowest, rows, preferred_element_type=F32)
                + jnp.dot(middle, rows, preferred_element_type=F32)
                + jnp.dot(high_mix, rows, preferred_element_type=F32)
            )
            for g in range(CHUNKS // 2):
                at_chunk = which * (CHUNKS // 2) + g
                start = (1 + c, 3 * c)[which] * quarter + g * block
                out[:, start:start + block] = (
                    stream_all[c, at_chunk].astype(F32) + added[:, g * block:(g + 1) * block]
                ).astype(BF16)

    for r in range(1, devices // 2):
        ask(r).wait_send()

    @pl.when(core != side)
    def _():
        ask(0).wait_send()

    for copy in sends:
        copy.wait_send()


def layer(queries, keys, values, span_ids, res, gain, routes, gates, wg, wu, wd):
    devices = lax.axis_size("expert")
    group = FF_WIN // wg.shape[0]
    wave = devices // group
    tokens, width = res.shape
    half = width // 2
    hidden = wg.shape[0]
    both = 2 * tokens
    block = half // CHUNKS
    planes = SPAN // (group * tokens)
    halves = KV_HEADS // 2
    rows = wave * 16
    per_chunk = devices // 2 // CHUNKS
    hbm = pl.BlockSpec(memory_space=pl.ANY)
    dma = pltpu.SemaphoreType.DMA

    def vmem(*shape, dtype=BF16):
        return pltpu.VMEM(shape, dtype)

    scratch = {
        "keys_v": vmem(*keys.shape),
        "values_v": vmem(*values.shape),
        "ids_v": vmem(wave, 1, group * tokens, dtype=jnp.int32),
        "gain_v": vmem(1, half, dtype=F32),
        "routes_v": vmem(*routes.shape[::-1], dtype=jnp.int32),
        "gates_v": vmem(*gates.shape[::-1], dtype=F32),
        "rg_v": vmem(2, 16, 128, dtype=F32),
        "res_v": vmem(2, tokens, half),
        "w_v": vmem(2, 2, hidden, half),
        "wd_v": vmem(2, hidden, half),
        "kv_pack": vmem(KV_HEADS, tokens, 2 * HEAD_DIM),
        "kv_far": vmem(max(planes - 1, 1), KV_HEADS, tokens, 2 * HEAD_DIM),
        "kv_buf": vmem(halves, planes, group, tokens, 2 * HEAD_DIM),
        "q_buf": vmem(devices // 2, both, queries.shape[1]),
        "bias_v": vmem(SPAN, per_chunk * both, dtype=F32),
        "stream_v": vmem(CHUNKS, both, block),
        "stream_all": vmem(2, CHUNKS, tokens, block),
        "outg": vmem(CHUNKS, wave, 16, block),
        "x_buf": vmem(CHUNKS, 4, wave, 16, block),
        "pre_out": vmem(4 * rows, 4 * hidden + 128),
        "pre_in": vmem(4 * rows, 4 * hidden + 128),
        "s1": vmem(2, wave, 2, 16, half // 2),
        "r1": vmem(2, wave, 2, 16, half // 2),
        "s2": vmem(2, wave, 16, half // 2),
        "r2": vmem(2, wave, 16, half // 2),
        "keep": vmem(2, wave, 16, half // 2, dtype=F32),
        "own": vmem(2, wave, 16, half // 2, dtype=F32),
        "final": vmem(wave, 2, 16, half // 2),
        "back": vmem(2 * wave, 16, half // 2),
        "in_sem": dma((6,)),
        "w_sem": dma((2,)),
        "ready_sem": pltpu.SemaphoreType.REGULAR,
        "send_sem": dma(()),
        "ask_sem": dma(()),
        "far_sem": dma((max(planes - 1, 1), halves)),
        "kv_sem": dma((2, halves)),
        "q_sem": dma((CHUNKS,)),
        "pair_sem": dma((3,)),
        "z_sem": dma((CHUNKS, wave - 1)),
        "x_sem": dma((CHUNKS, wave + 1)),
        "pre_sem": dma(()),
        "r1_sem": dma((2, wave)),
        "r2_sem": dma((wave,)),
        "back_sem": dma(()),
    }
    names = ("queries", "keys", "values", "ids", "res", "gain", "routes", "gates", "wg", "wu", "wd", "out", *scratch)
    return pl.pallas_call(
        functools.partial(moe_kernel, names, group),
        out_shape=pltpu.VMEM((tokens, width), BF16),
        in_specs=[hbm] * 11,
        out_specs=pl.BlockSpec(memory_space=pltpu.VMEM),
        scratch_shapes=list(scratch.values()),
        compiler_params=pltpu.CompilerParams(
            collective_id=0, has_side_effects=True, vmem_limit_bytes=60 * 2**20
        ),
    )(
        queries, keys, values, span_ids.reshape(wave, 1, group * tokens), res, gain.reshape(1, width),
        routes.T, gates.T, wg, wu, wd,
    )


def solution(mesh):
    return jax.shard_map(
        layer,
        mesh=mesh,
        in_specs=(
            P("dp", "expert"),
            P(("dp", "expert"), None),
            P(("dp", "expert"), None),
            P("dp"),
            P(("dp", "expert"), None),
            P(),
            P(("dp", "expert"), None),
            P(("dp", "expert"), None),
            P("expert", None),
            P("expert", None),
            P("expert", None),
        ),
        out_specs=P(("dp", "expert"), None),
        check_vma=False,
    )
```

```python
import functools
import math

import jax
import jax.numpy as jnp
from jax import lax
from jax.experimental import pallas as pl
from jax.experimental.pallas import tpu as pltpu
from jax.sharding import PartitionSpec as P

KV_HEADS = 4
HEAD_DIM = 64
FF_WIN = 1024
SPAN = 512
CHUNKS = 4
WINDOW = 5
AHEAD = 3
NEXT = 2
LAG = 2
SOON = (1,)
MESH = pl.DeviceIdType.MESH
F32 = jnp.float32
BF16 = jnp.bfloat16


def remote(src, dst, send, recv, device):
    return pltpu.make_async_remote_copy(
        src_ref=src, dst_ref=dst, send_sem=send, recv_sem=recv,
        device_id={"expert": device}, device_id_type=MESH,
    )


def arrived(ref, sem):
    pltpu.make_async_copy(ref, ref, sem).wait()


def route_matrix(routes, gates, wave, capacity, cores):
    tokens = routes.shape[0]
    here = tokens // cores
    columns = wave * cores * capacity
    column = lax.broadcasted_iota(jnp.int32, (tokens, columns), 1)
    token = lax.broadcasted_iota(jnp.int32, (tokens, columns), 0)
    one = lax.broadcasted_iota(jnp.int32, (tokens, tokens), 0)
    other = lax.broadcasted_iota(jnp.int32, (tokens, tokens), 1)
    lower = jnp.where((one >= other) & (one // here == other // here), 1.0, 0.0)
    named_wide = jnp.zeros((tokens, columns), F32)
    weight_wide = jnp.zeros((tokens, columns), F32)
    for expert in range(wave):
        hits = routes == expert
        named = jnp.max(jnp.where(hits, 1.0, 0.0), axis=1, keepdims=True)
        weight = jnp.sum(jnp.where(hits, gates, 0.0), axis=1, keepdims=True)
        mask = column // (cores * capacity) == expert
        named_wide = jnp.where(mask, named, named_wide)
        weight_wide = jnp.where(mask, weight, weight_wide)
    count = jnp.dot(lower.astype(BF16), named_wide.astype(BF16), preferred_element_type=F32)
    slot = (column % capacity + 1).astype(F32)
    fits = (count == slot) & (column % (cores * capacity) // capacity == token // here)
    chosen = jnp.where(fits, named_wide, 0.0)
    return chosen, chosen * weight_wide


def moe_kernel(names, group, *refs):
    at = dict(zip(names, refs, strict=True))
    (queries, keys, values, ids, res, gain, routes, gates, wg, wu, wd, out) = (
        at[name] for name in ("queries", "keys", "values", "ids", "res", "gain", "routes", "gates", "wg", "wu", "wd", "out")
    )
    (keys_v, values_v, ids_v, gain_v, routes_v, gates_v, rg_v, res_v, w_v, wd_v) = (
        at[name] for name in ("keys_v", "values_v", "ids_v", "gain_v", "routes_v", "gates_v", "rg_v", "res_v", "w_v", "wd_v")
    )
    (kv_pack, kv_far, kv_buf, q_buf, bias_v, stream_v, stream_all, outg, x_buf, pre_out, pre_in) = (
        at[name] for name in (
            "kv_pack", "kv_far", "kv_buf", "q_buf", "bias_v", "stream_v", "stream_all", "outg", "x_buf", "pre_out", "pre_in")
    )
    (s1, r1, s2, r2, keep, own, final, back) = (
        at[name] for name in ("s1", "r1", "s2", "r2", "keep", "own", "final", "back")
    )
    (far_sem, in_sem, w_sem, ready_sem, send_sem, kv_sem, q_sem, pair_sem, z_sem, x_sem, pre_sem, r1_sem, r2_sem, back_sem) = (
        at[name] for name in (
            "far_sem", "in_sem", "w_sem", "ready_sem", "send_sem", "kv_sem", "q_sem", "pair_sem", "z_sem", "x_sem",
            "pre_sem", "r1_sem", "r2_sem", "back_sem")
    )
    me = lax.axis_index("expert")
    wave = x_buf.shape[2]
    devices = wave * group
    tokens, width = out.shape
    both = 2 * tokens
    half = width // 2
    quarter = half // 2
    block = half // CHUNKS
    rows = wave * 16
    plane = me // group
    mine = me % group
    core = me % 2
    other = 1 - core


    sends = []

    def go(src, dst, recv, device):
        copy = remote(src, dst, send_sem, recv, device)
        copy.start()
        sends.append(copy)

    def early(c):
        return [pl.ds(pl.multiple_of(q * quarter, 128), quarter) for q in (1 + c, 3 * c)]

    def split(source, target, sem, send):
        for n, columns in enumerate(early(core if send is None else other)):
            place = target.at[:, pl.ds(n * quarter, quarter)]
            if send is None:
                pltpu.make_async_copy(source.at[:, columns], place, sem).start()
            else:
                go(source.at[:, columns], place, sem, send)

    def across(rz):
        return (plane ^ rz) * group + mine

    def within(r):
        return plane * group + (mine ^ r)

    partner = within(1)
    fetched = {}
    for number, (name, source, target) in enumerate((
        ("keys", keys, keys_v), ("values", values, values_v), ("routes", routes, routes_v), ("gates", gates, gates_v),
        ("ids", ids, ids_v),
    )):
        fetched[name] = pltpu.make_async_copy(source, target, in_sem.at[number])
        fetched[name].start()
    barrier = pltpu.get_barrier_semaphore()
    partners = [within(r) for r in range(1, group)] + [across(rz) for rz in range(1, wave)]
    for device in partners:
        pl.semaphore_signal(barrier, inc=1, device_id={"expert": device}, device_id_type=MESH)
    split(res, res_v.at[core], pair_sem.at[1], None)
    split(gain, gain_v, in_sem.at[5], None)
    split(wg, w_v.at[0, core], w_sem.at[0], None)
    split(wu, w_v.at[1, core], w_sem.at[0], None)
    split(wd, wd_v.at[core], w_sem.at[1], None)
    pl.semaphore_wait(barrier, len(partners))
    for rz in range(1, wave):
        pl.semaphore_signal(ready_sem, inc=1, device_id={"expert": across(rz)}, device_id_type=MESH)

    for name in ("keys", "values"):
        fetched[name].wait()
    for place, head in enumerate((1, 2, 0, 3)):
        columns = slice(head * HEAD_DIM, (head + 1) * HEAD_DIM)
        kv_pack[place] = jnp.concatenate([keys_v[:, columns], values_v[:, columns]], axis=1)
    planes = SPAN // (group * tokens)
    halves = KV_HEADS // 2
    for h in range(halves):
        for rz in range(1, planes):
            pair = pl.ds(2 * h, 2)
            go(kv_pack.at[pair], kv_far.at[rz - 1, pair], far_sem.at[rz - 1, h], across(rz))

    def share(h, source, at_plane, sem):
        for r in range(1, group):
            go(source.at[2 * h + (core ^ (r % 2))], kv_buf.at[h, at_plane, mine], sem, within(r))
        kv_buf[h, at_plane, mine] = source[2 * h + core]

    share(0, kv_pack, plane % planes, kv_sem.at[0, 0])
    pl.semaphore_wait(ready_sem, wave - 1)
    side = me // (devices // 2)
    number = (me % (devices // 2)) ^ ((1 - side) * (devices // 4))
    per_chunk = devices // 2 // CHUNKS
    query_sem = q_sem.at[number // per_chunk]

    def ask(r):
        pair = (me // 2) ^ r
        source = queries.at[pl.ds(pl.multiple_of(pair * both, both), both)]
        return remote(source, q_buf.at[number], at["ask_sem"], query_sem, pair * 2 + side)

    def ask_planes(distances):
        for rz in distances:
            for r in range((rz + 1) * group // 2 - 1, rz * group // 2 - 1, -1):
                if r:
                    ask(r).start()
        if 0 in distances:

            @pl.when(core == side)
            def _():
                source = queries.at[pl.ds(pl.multiple_of(me // 2 * both, both), both)]
                pltpu.make_async_copy(source, q_buf.at[number], query_sem).start()

            @pl.when(core != side)
            def _():
                ask(0).start()

    distant = list(range(wave - 1, -1, -1))
    soon = SOON

    @pl.when(number < devices // 4)
    def _():
        ask_planes(distant[:-1])

    @pl.when(number >= devices // 4)
    def _():
        ask_planes([rz for rz in distant if rz in soon])

    for name in ("routes", "gates"):
        fetched[name].wait()
    rg_v[core, :8, :tokens] = routes_v[...].astype(F32)
    rg_v[core, 8:, :tokens] = gates_v[...]
    go(rg_v.at[core], rg_v.at[core], pair_sem.at[0], partner)
    def pass_on(h):
        for rz in range(1, planes):
            arrived(kv_far.at[rz - 1, pl.ds(2 * h, 2)], far_sem.at[rz - 1, h])
            share(h, kv_far.at[rz - 1], (plane ^ rz) % planes, kv_sem.at[1, h])

    pass_on(0)

    @pl.when(number < devices // 4)
    def _():
        ask_planes([0])

    split(res, res_v.at[core], pair_sem.at[1], partner)
    fetched["ids"].wait()
    _, mix = route_matrix(routes_v[...].astype(F32).T, gates_v[...].T, wave, 8, 1)
    arrived(rg_v.at[0], pair_sem.at[0])
    named = jnp.concatenate([rg_v[c, :8, :].T[:tokens] for c in range(2)], axis=0)
    weights = jnp.concatenate([rg_v[c, 8:, :].T[:tokens] for c in range(2)], axis=0)
    chosen, _ = route_matrix(named, weights, wave, 8, 2)
    chosen = chosen.T.astype(BF16)

    stretch = group * tokens
    wide = per_chunk * both
    first = plane // planes * planes
    key_ids = jnp.concatenate(
        [jnp.broadcast_to(ids_v[first + i].astype(F32), (128, stretch)).T for i in range(planes)], axis=0
    )
    key_ids = jnp.concatenate([key_ids] * (wide // 128), axis=1)
    key_at = lax.broadcasted_iota(jnp.int32, (SPAN, wide), 0)
    query_at = (
        lax.broadcasted_iota(jnp.int32, (SPAN, wide), 1) % both
        + ((plane - first) * stretch + mine // 2 * both)
    )
    query_ids = jnp.sum(jnp.where(key_at == query_at, key_ids, 0.0), axis=0, keepdims=True)
    bias_v[...] = jnp.where((key_at <= query_at) & (key_ids == query_ids), 0.0, -jnp.inf)
    share(1, kv_pack, plane % planes, kv_sem.at[0, 1])
    pass_on(1)

    @pl.when(number >= devices // 4)
    def _():
        ask_planes([rz for rz in distant if rz not in soon])

    def gathered(h):
        arrived(kv_buf.at[h, 0, pl.ds(0, group - 1)], kv_sem.at[0, h])
        if planes > 1:
            arrived(kv_buf.at[h, pl.ds(0, planes - 1), pl.ds(0, group - 1)], kv_sem.at[1, h])

    gathered(0)
    split(wg, w_v.at[0, core], w_sem.at[0], partner)
    split(wu, w_v.at[1, core], w_sem.at[0], partner)
    split(wd, wd_v.at[core], w_sem.at[1], partner)

    def attend(g):
        head = g * halves // CHUNKS
        held = kv_buf[head].reshape(SPAN, 2 * HEAD_DIM)
        key_blk = held[:, :HEAD_DIM]
        value_rows = jnp.concatenate([held.T[HEAD_DIM:], jnp.ones((16, SPAN), BF16)], axis=0)
        query = q_buf[g * per_chunk:(g + 1) * per_chunk].reshape(wide, -1) * BF16(1.0 / math.sqrt(HEAD_DIM))
        count = query.shape[1] // HEAD_DIM
        query = jnp.concatenate([query[:, n * HEAD_DIM:(n + 1) * HEAD_DIM] for n in range(count)], axis=0)
        scores = lax.dot_general(key_blk, query, (((1,), (1,)), ((), ())), preferred_element_type=F32)
        scores = scores + jnp.concatenate([bias_v[...]] * count, axis=1)
        raised = jnp.exp(scores - jnp.max(scores, axis=0, keepdims=True)).astype(BF16)
        summed = jnp.dot(value_rows, raised, preferred_element_type=F32)
        summed = summed[:HEAD_DIM] * (1.0 / summed[HEAD_DIM:HEAD_DIM + 1])
        heads = [summed[:, n * wide:(n + 1) * wide] for n in range(count)]
        joined = heads[0] if len(heads) == 1 else jnp.concatenate(heads, axis=0)
        joined = joined.T.astype(BF16)
        return jnp.concatenate([joined[i * both:(i + 1) * both] for i in range(per_chunk)], axis=1)

    near = (within(2), within(4))

    def attention(g):
        if g == CHUNKS // halves:
            gathered(1)
        arrived(q_buf.at[pl.ds(g * per_chunk, per_chunk)], q_sem.at[g])
        if g == 0:
            arrived(res_v, pair_sem.at[1])
        columns = slice(g * block, (g + 1) * block)
        attended = attend(g)
        stream = (res_v[:, :, columns].reshape(both, block).astype(F32) + attended.astype(F32)).astype(BF16)
        stream_v[g] = stream
        outg[g] = jnp.dot(chosen, stream, preferred_element_type=F32).astype(BF16).reshape(wave, 16, block)

    def leave(g, rz):
        go(outg.at[g, plane ^ rz], x_buf.at[g, 0, rz], z_sem.at[g, rz - 1], across(rz))

    def spread(g, rz):
        for hop in range(2):
            recv = x_sem.at[g, rz] if rz % 2 == hop else x_sem.at[g, wave]
            go(x_buf.at[g, 0, rz], x_buf.at[g, 1 + hop, rz], recv, near[hop])

    def forward(g, rz):
        arrived(x_buf.at[g, 0, rz], z_sem.at[g, rz - 1])
        spread(g, rz)

    def relay(g, rz):
        hop = rz % 2
        piece = x_buf.at[g, 1 + hop, rz]
        arrived(piece, x_sem.at[g, rz])
        go(piece, x_buf.at[g, 3, rz], x_sem.at[g, wave], near[1 - hop])

    def tell(g):
        ours = pl.ds(pl.multiple_of(other * tokens, tokens), tokens)
        go(stream_v.at[g, ours], stream_all.at[core, g], pair_sem.at[2], partner)
        stream_all[core, g] = stream_v[g, pl.ds(pl.multiple_of(core * tokens, tokens), tokens)]
        x_buf[g, 0, 0] = outg[g, plane]
        spread(g, 0)

    total = {}

    def up(g):
        if g == 0:
            arrived(gain_v, in_sem.at[5])
            arrived(w_v, w_sem.at[0])
        arrived(x_buf.at[g, pl.ds(0, 2)], x_sem.at[g, wave])
        columns = slice(g * block, (g + 1) * block)
        x = x_buf[g].reshape(4 * rows, block).astype(F32)
        square = x * x
        square = sum(square[:, i:i + 128] for i in range(0, block, 128))
        x = (x * gain_v[:, columns]).astype(BF16)
        weight = w_v[:, :, :, columns].reshape(-1, block)
        pre = lax.dot_general(x, weight, (((1,), (1,)), ((), ())), preferred_element_type=F32)
        total["square"] = square if g == 0 else total["square"] + square
        total["pre"] = pre if g == 0 else total["pre"] + pre

    def offer():
        pre = total["pre"]
        units = pre.shape[1]
        square = jnp.sum(total["square"], axis=1, keepdims=True)
        total["square"] = square
        coarse = square.astype(BF16)
        rest = (square - coarse.astype(F32)).astype(BF16)
        lane = lax.broadcasted_iota(jnp.int32, (4 * rows, 128), 1)
        pre_out[:, :units] = pre.astype(BF16)
        pre_out[:, units:] = jnp.where(lane < 64, coarse.astype(F32), rest.astype(F32)).astype(BF16)
        go(pre_out, pre_in, pre_sem, partner)

    def hide():
        units = total["pre"].shape[1]
        arrived(pre_in, pre_sem)
        square = (
            total["square"] + pre_in[:, units:units + 1].astype(F32) + pre_in[:, units + 64:units + 65].astype(F32)
        )
        inverse = lax.rsqrt(square * (1.0 / width) + 1e-06)
        pre = (total["pre"] + pre_in[:, :units].astype(F32)) * inverse
        gate_pre, up_pre = pre[:, :units // 2], pre[:, units // 2:]
        total["hidden"] = (gate_pre / (1.0 + jnp.exp(-gate_pre)) * up_pre).astype(BF16)
        arrived(wd_v, w_sem.at[1])

    def product(blks, which):
        hidden = jnp.concatenate([total["hidden"][blk * rows:(blk + 1) * rows] for blk in blks], axis=0)
        weight = wd_v[:, :, which * quarter:(which + 1) * quarter].reshape(-1, quarter)
        return jnp.dot(hidden, weight, preferred_element_type=F32).reshape(2, wave, 16, quarter)

    def first_hop(kind, rz, sides=(0, 1)):
        for which in sides:
            go(s1.at[which, rz, kind], r1.at[which, rz, kind], r1_sem.at[which, rz, kind], near[which])

    def down(early):
        for which in range(2):
            piece = product((3, 1 + which), which).astype(BF16)
            s1[which, :, 0], s1[which, :, 1] = piece[0], piece[1]
            for kind, rz in early:
                first_hop(kind, rz, (which,))
        for which in range(2):
            keep[which], own[which] = product((2 - which, 0), which)

    def second_hop(rz):
        for which in range(2):
            arrived(r1.at[which, rz, 0], r1_sem.at[which, rz, 0])
            s2[which, rz] = (keep[which, rz] + r1[which, rz, 0].astype(F32)).astype(BF16)
            go(s2.at[which, rz], r2.at[which, rz], r2_sem.at[rz], near[1 - which])

    def finish(rz):
        for which in range(2):
            arrived(r1.at[which, rz, 1], r1_sem.at[which, rz, 1])
        arrived(r2.at[:, rz], r2_sem.at[rz])
        sides = [
            own[which, rz] + r1[which, rz, 1].astype(F32) + r2[which, rz].astype(F32) for which in range(2)
        ]
        for c in range(2):
            final[rz, c] = jnp.concatenate([one[c * 8:(c + 1) * 8] for one in sides], axis=0).astype(BF16)
        go(final.at[rz, other], back.at[plane * 2 + core], back_sem, (plane ^ rz) * group + (mine ^ 1))
        if rz:
            go(final.at[rz, core], back.at[plane * 2 + core], back_sem, across(rz))
        else:
            back[plane * 2 + core] = final[0, core]

    for g in range(CHUNKS):
        attention(g)
        for i in range(1, wave):
            leave(g, i)
        tell(g)
        if g >= 2:
            relay(g - 2, 0)

    come = range(1, wave)
    steps = []

    def then(step, *where):
        steps.append((step, *where))

    def many(step, g):
        for rz in come:
            then(step, g, rz)

    many(forward, 0)
    then(relay, 2, 0)
    many(forward, 1)
    then(relay, 3, 0)
    many(forward, 2)
    many(forward, 3)
    many(relay, 0)
    many(relay, 1)
    many(relay, 2)
    many(relay, 3)
    for g in range(CHUNKS):
        then(up, g)
    then(offer)
    then(hide)
    behind = list(range(wave - 1, -1, -1))
    pieces = [(0, rz) for rz in behind[:AHEAD]]
    for n, rz in enumerate(behind):
        pieces.append((1, rz))
        if n + AHEAD < wave:
            pieces.append((0, behind[n + AHEAD]))
    then(down, pieces[:WINDOW])
    del pieces[:WINDOW]
    for n, rz in enumerate(behind):
        then(second_hop, rz)
        for kind, late in pieces[:NEXT]:
            then(first_hop, kind, late)
        del pieces[:NEXT]
        if n >= LAG:
            then(finish, behind[n - LAG])
    for rz in behind[-LAG:]:
        then(finish, rz)
    for step, *where in steps:
        step(*where)
    arrived(back.at[pl.ds(0, 2 * wave - 1)], back_sem)
    arrived(stream_all.at[0], pair_sem.at[2])
    high_mix = mix.astype(BF16)
    rest = mix - high_mix.astype(F32)
    middle = rest.astype(BF16)
    lowest = (rest - middle.astype(F32)).astype(BF16)
    outs = back[...].reshape(wave, 2, 16, quarter).astype(F32)
    for c in range(2):
        for which in range(2):
            rows = outs[:, c, which * 8:(which + 1) * 8].reshape(wave * 8, quarter).astype(BF16)
            added = (
                jnp.dot(lowest, rows, preferred_element_type=F32)
                + jnp.dot(middle, rows, preferred_element_type=F32)
                + jnp.dot(high_mix, rows, preferred_element_type=F32)
            )
            for g in range(CHUNKS // 2):
                at_chunk = which * (CHUNKS // 2) + g
                start = (1 + c, 3 * c)[which] * quarter + g * block
                out[:, start:start + block] = (
                    stream_all[c, at_chunk].astype(F32) + added[:, g * block:(g + 1) * block]
                ).astype(BF16)

    for r in range(1, devices // 2):
        ask(r).wait_send()

    @pl.when(core != side)
    def _():
        ask(0).wait_send()

    for copy in sends:
        copy.wait_send()


def layer(queries, keys, values, span_ids, res, gain, routes, gates, wg, wu, wd):
    devices = lax.axis_size("expert")
    group = FF_WIN // wg.shape[0]
    wave = devices // group
    tokens, width = res.shape
    half = width // 2
    hidden = wg.shape[0]
    both = 2 * tokens
    block = half // CHUNKS
    planes = SPAN // (group * tokens)
    halves = KV_HEADS // 2
    rows = wave * 16
    per_chunk = devices // 2 // CHUNKS
    hbm = pl.BlockSpec(memory_space=pl.ANY)
    dma = pltpu.SemaphoreType.DMA

    def vmem(*shape, dtype=BF16):
        return pltpu.VMEM(shape, dtype)

    scratch = {
        "keys_v": vmem(*keys.shape),
        "values_v": vmem(*values.shape),
        "ids_v": vmem(wave, 1, group * tokens, dtype=jnp.int32),
        "gain_v": vmem(1, half, dtype=F32),
        "routes_v": vmem(*routes.shape[::-1], dtype=jnp.int32),
        "gates_v": vmem(*gates.shape[::-1], dtype=F32),
        "rg_v": vmem(2, 16, 128, dtype=F32),
        "res_v": vmem(2, tokens, half),
        "w_v": vmem(2, 2, hidden, half),
        "wd_v": vmem(2, hidden, half),
        "kv_pack": vmem(KV_HEADS, tokens, 2 * HEAD_DIM),
        "kv_far": vmem(max(planes - 1, 1), KV_HEADS, tokens, 2 * HEAD_DIM),
        "kv_buf": vmem(halves, planes, group, tokens, 2 * HEAD_DIM),
        "q_buf": vmem(devices // 2, both, queries.shape[1]),
        "bias_v": vmem(SPAN, per_chunk * both, dtype=F32),
        "stream_v": vmem(CHUNKS, both, block),
        "stream_all": vmem(2, CHUNKS, tokens, block),
        "outg": vmem(CHUNKS, wave, 16, block),
        "x_buf": vmem(CHUNKS, 4, wave, 16, block),
        "pre_out": vmem(4 * rows, 4 * hidden + 128),
        "pre_in": vmem(4 * rows, 4 * hidden + 128),
        "s1": vmem(2, wave, 2, 16, half // 2),
        "r1": vmem(2, wave, 2, 16, half // 2),
        "s2": vmem(2, wave, 16, half // 2),
        "r2": vmem(2, wave, 16, half // 2),
        "keep": vmem(2, wave, 16, half // 2, dtype=F32),
        "own": vmem(2, wave, 16, half // 2, dtype=F32),
        "final": vmem(wave, 2, 16, half // 2),
        "back": vmem(2 * wave, 16, half // 2),
        "in_sem": dma((6,)),
        "w_sem": dma((2,)),
        "ready_sem": pltpu.SemaphoreType.REGULAR,
        "send_sem": dma(()),
        "ask_sem": dma(()),
        "far_sem": dma((max(planes - 1, 1), halves)),
        "kv_sem": dma((2, halves)),
        "q_sem": dma((CHUNKS,)),
        "pair_sem": dma((3,)),
        "z_sem": dma((CHUNKS, wave - 1)),
        "x_sem": dma((CHUNKS, wave + 1)),
        "pre_sem": dma(()),
        "r1_sem": dma((2, wave, 2)),
        "r2_sem": dma((wave,)),
        "back_sem": dma(()),
    }
    names = ("queries", "keys", "values", "ids", "res", "gain", "routes", "gates", "wg", "wu", "wd", "out", *scratch)
    return pl.pallas_call(
        functools.partial(moe_kernel, names, group),
        out_shape=pltpu.VMEM((tokens, width), BF16),
        in_specs=[hbm] * 11,
        out_specs=pl.BlockSpec(memory_space=pltpu.VMEM),
        scratch_shapes=list(scratch.values()),
        compiler_params=pltpu.CompilerParams(
            collective_id=0, has_side_effects=True, vmem_limit_bytes=60 * 2**20
        ),
    )(
        queries, keys, values, span_ids.reshape(wave, 1, group * tokens), res, gain.reshape(1, width),
        routes.T, gates.T, wg, wu, wd,
    )


def solution(mesh):
    return jax.shard_map(
        layer,
        mesh=mesh,
        in_specs=(
            P("dp", "expert"),
            P(("dp", "expert"), None),
            P(("dp", "expert"), None),
            P("dp"),
            P(("dp", "expert"), None),
            P(),
            P(("dp", "expert"), None),
            P(("dp", "expert"), None),
            P("expert", None),
            P("expert", None),
            P("expert", None),
        ),
        out_specs=P(("dp", "expert"), None),
        check_vma=False,
    )
```

```python
import functools
import math

import jax
import jax.numpy as jnp
from jax import lax
from jax.experimental import pallas as pl
from jax.experimental.pallas import tpu as pltpu
from jax.sharding import PartitionSpec as P

KV_HEADS = 4
HEAD_DIM = 64
FF_WIN = 1024
SPAN = 512
CHUNKS = 4
WINDOW = 5
AHEAD = 3
NEXT = 2
LAG = 2
SOON = (1,)
MESH = pl.DeviceIdType.MESH
F32 = jnp.float32
BF16 = jnp.bfloat16


def remote(src, dst, send, recv, device):
    return pltpu.make_async_remote_copy(
        src_ref=src, dst_ref=dst, send_sem=send, recv_sem=recv,
        device_id={"expert": device}, device_id_type=MESH,
    )


def arrived(ref, sem):
    pltpu.make_async_copy(ref, ref, sem).wait()


def route_matrix(routes, gates, wave, capacity, cores):
    tokens = routes.shape[0]
    here = tokens // cores
    columns = wave * cores * capacity
    column = lax.broadcasted_iota(jnp.int32, (tokens, columns), 1)
    token = lax.broadcasted_iota(jnp.int32, (tokens, columns), 0)
    one = lax.broadcasted_iota(jnp.int32, (tokens, tokens), 0)
    other = lax.broadcasted_iota(jnp.int32, (tokens, tokens), 1)
    lower = jnp.where((one >= other) & (one // here == other // here), 1.0, 0.0)
    named_wide = jnp.zeros((tokens, columns), F32)
    weight_wide = jnp.zeros((tokens, columns), F32)
    for expert in range(wave):
        hits = routes == expert
        named = jnp.max(jnp.where(hits, 1.0, 0.0), axis=1, keepdims=True)
        weight = jnp.sum(jnp.where(hits, gates, 0.0), axis=1, keepdims=True)
        mask = column // (cores * capacity) == expert
        named_wide = jnp.where(mask, named, named_wide)
        weight_wide = jnp.where(mask, weight, weight_wide)
    count = jnp.dot(lower.astype(BF16), named_wide.astype(BF16), preferred_element_type=F32)
    slot = (column % capacity + 1).astype(F32)
    fits = (count == slot) & (column % (cores * capacity) // capacity == token // here)
    chosen = jnp.where(fits, named_wide, 0.0)
    return chosen, chosen * weight_wide


def moe_kernel(names, group, *refs):
    at = dict(zip(names, refs, strict=True))
    (queries, keys, values, ids, res, gain, routes, gates, wg, wu, wd, out) = (
        at[name] for name in ("queries", "keys", "values", "ids", "res", "gain", "routes", "gates", "wg", "wu", "wd", "out")
    )
    (keys_v, values_v, ids_v, gain_v, routes_v, gates_v, rg_v, res_v, w_v, wd_v) = (
        at[name] for name in ("keys_v", "values_v", "ids_v", "gain_v", "routes_v", "gates_v", "rg_v", "res_v", "w_v", "wd_v")
    )
    (kv_pack, kv_far, kv_buf, q_buf, bias_v, stream_v, stream_all, outg, x_buf, pre_out, pre_in) = (
        at[name] for name in (
            "kv_pack", "kv_far", "kv_buf", "q_buf", "bias_v", "stream_v", "stream_all", "outg", "x_buf", "pre_out", "pre_in")
    )
    (s1, r1, s2, r2, keep, own, final, back) = (
        at[name] for name in ("s1", "r1", "s2", "r2", "keep", "own", "final", "back")
    )
    (far_sem, in_sem, w_sem, ready_sem, send_sem, kv_sem, q_sem, pair_sem, z_sem, x_sem, pre_sem, r1_sem, r2_sem, back_sem) = (
        at[name] for name in (
            "far_sem", "in_sem", "w_sem", "ready_sem", "send_sem", "kv_sem", "q_sem", "pair_sem", "z_sem", "x_sem",
            "pre_sem", "r1_sem", "r2_sem", "back_sem")
    )
    me = lax.axis_index("expert")
    wave = x_buf.shape[2]
    devices = wave * group
    tokens, width = out.shape
    both = 2 * tokens
    half = width // 2
    quarter = half // 2
    block = half // CHUNKS
    rows = wave * 16
    plane = me // group
    mine = me % group
    core = me % 2
    other = 1 - core


    sends = []

    def go(src, dst, recv, device):
        copy = remote(src, dst, send_sem, recv, device)
        copy.start()
        sends.append(copy)

    def early(c):
        return [pl.ds(pl.multiple_of(q * quarter, 128), quarter) for q in (1 + c, 3 * c)]

    def split(source, target, sem, send):
        for n, columns in enumerate(early(core if send is None else other)):
            place = target.at[:, pl.ds(n * quarter, quarter)]
            if send is None:
                pltpu.make_async_copy(source.at[:, columns], place, sem).start()
            else:
                go(source.at[:, columns], place, sem, send)

    def across(rz):
        return (plane ^ rz) * group + mine

    def within(r):
        return plane * group + (mine ^ r)

    partner = within(1)
    fetched = {}
    for number, (name, source, target) in enumerate((
        ("keys", keys, keys_v), ("values", values, values_v), ("routes", routes, routes_v), ("gates", gates, gates_v),
        ("ids", ids, ids_v),
    )):
        fetched[name] = pltpu.make_async_copy(source, target, in_sem.at[number])
        fetched[name].start()
    barrier = pltpu.get_barrier_semaphore()
    partners = [within(r) for r in range(1, group)] + [across(rz) for rz in range(1, wave)]
    for device in partners:
        pl.semaphore_signal(barrier, inc=1, device_id={"expert": device}, device_id_type=MESH)
    split(res, res_v.at[core], pair_sem.at[1], None)
    split(gain, gain_v, in_sem.at[5], None)
    split(wg, w_v.at[0, core], w_sem.at[0], None)
    split(wu, w_v.at[1, core], w_sem.at[0], None)
    split(wd, wd_v.at[core], w_sem.at[1], None)
    pl.semaphore_wait(barrier, len(partners))
    for rz in range(1, wave):
        pl.semaphore_signal(ready_sem, inc=1, device_id={"expert": across(rz)}, device_id_type=MESH)

    for name in ("keys", "values"):
        fetched[name].wait()
    for place, head in enumerate((1, 2, 0, 3)):
        columns = slice(head * HEAD_DIM, (head + 1) * HEAD_DIM)
        kv_pack[place] = jnp.concatenate([keys_v[:, columns], values_v[:, columns]], axis=1)
    planes = SPAN // (group * tokens)
    halves = KV_HEADS // 2
    for h in range(halves):
        for rz in range(1, planes):
            pair = pl.ds(2 * h, 2)
            go(kv_pack.at[pair], kv_far.at[rz - 1, pair], far_sem.at[rz - 1, h], across(rz))

    def share(h, source, at_plane, sem):
        for r in range(1, group):
            go(source.at[2 * h + (core ^ (r % 2))], kv_buf.at[h, at_plane, mine], sem, within(r))
        kv_buf[h, at_plane, mine] = source[2 * h + core]

    share(0, kv_pack, plane % planes, kv_sem.at[0, 0])
    pl.semaphore_wait(ready_sem, wave - 1)
    side = me // (devices // 2)
    number = (me % (devices // 2)) ^ ((1 - side) * (devices // 4))
    per_chunk = devices // 2 // CHUNKS
    query_sem = q_sem.at[number // per_chunk]

    def ask(r):
        pair = (me // 2) ^ r
        source = queries.at[pl.ds(pl.multiple_of(pair * both, both), both)]
        return remote(source, q_buf.at[number], at["ask_sem"], query_sem, pair * 2 + side)

    def ask_planes(distances):
        for rz in distances:
            for r in range((rz + 1) * group // 2 - 1, rz * group // 2 - 1, -1):
                if r:
                    ask(r).start()
        if 0 in distances:

            @pl.when(core == side)
            def _():
                source = queries.at[pl.ds(pl.multiple_of(me // 2 * both, both), both)]
                pltpu.make_async_copy(source, q_buf.at[number], query_sem).start()

            @pl.when(core != side)
            def _():
                ask(0).start()

    distant = list(range(wave - 1, -1, -1))
    soon = SOON

    @pl.when(number < devices // 4)
    def _():
        ask_planes(distant[:-1])

    @pl.when(number >= devices // 4)
    def _():
        ask_planes([rz for rz in distant if rz in soon])

    for name in ("routes", "gates"):
        fetched[name].wait()
    rg_v[core, :8, :tokens] = routes_v[...].astype(F32)
    rg_v[core, 8:, :tokens] = gates_v[...]
    go(rg_v.at[core], rg_v.at[core], pair_sem.at[0], partner)
    def pass_on(h):
        for rz in range(1, planes):
            arrived(kv_far.at[rz - 1, pl.ds(2 * h, 2)], far_sem.at[rz - 1, h])
            share(h, kv_far.at[rz - 1], (plane ^ rz) % planes, kv_sem.at[1, h])

    pass_on(0)

    @pl.when(number < devices // 4)
    def _():
        ask_planes([0])

    split(res, res_v.at[core], pair_sem.at[1], partner)
    fetched["ids"].wait()
    _, mix = route_matrix(routes_v[...].astype(F32).T, gates_v[...].T, wave, 8, 1)
    arrived(rg_v.at[0], pair_sem.at[0])
    named = jnp.concatenate([rg_v[c, :8, :].T[:tokens] for c in range(2)], axis=0)
    weights = jnp.concatenate([rg_v[c, 8:, :].T[:tokens] for c in range(2)], axis=0)
    chosen, _ = route_matrix(named, weights, wave, 8, 2)
    chosen = chosen.T.astype(BF16)

    stretch = group * tokens
    wide = per_chunk * both
    first = plane // planes * planes
    key_ids = jnp.concatenate(
        [jnp.broadcast_to(ids_v[first + i].astype(F32), (128, stretch)).T for i in range(planes)], axis=0
    )
    key_ids = jnp.concatenate([key_ids] * (wide // 128), axis=1)
    key_at = lax.broadcasted_iota(jnp.int32, (SPAN, wide), 0)
    query_at = (
        lax.broadcasted_iota(jnp.int32, (SPAN, wide), 1) % both
        + ((plane - first) * stretch + mine // 2 * both)
    )
    query_ids = jnp.sum(jnp.where(key_at == query_at, key_ids, 0.0), axis=0, keepdims=True)
    bias_v[...] = jnp.where((key_at <= query_at) & (key_ids == query_ids), 0.0, -jnp.inf)
    share(1, kv_pack, plane % planes, kv_sem.at[0, 1])
    pass_on(1)

    @pl.when(number >= devices // 4)
    def _():
        ask_planes([rz for rz in distant if rz not in soon])

    def gathered(h):
        arrived(kv_buf.at[h, 0, pl.ds(0, group - 1)], kv_sem.at[0, h])
        if planes > 1:
            arrived(kv_buf.at[h, pl.ds(0, planes - 1), pl.ds(0, group - 1)], kv_sem.at[1, h])

    gathered(0)
    split(wg, w_v.at[0, core], w_sem.at[0], partner)
    split(wu, w_v.at[1, core], w_sem.at[0], partner)
    split(wd, wd_v.at[core], w_sem.at[1], partner)

    def attend(g):
        head = g * halves // CHUNKS
        held = kv_buf[head].reshape(SPAN, 2 * HEAD_DIM)
        key_blk = held[:, :HEAD_DIM]
        value_rows = jnp.concatenate([held.T[HEAD_DIM:], jnp.ones((16, SPAN), BF16)], axis=0)
        query = q_buf[g * per_chunk:(g + 1) * per_chunk].reshape(wide, -1) * BF16(1.0 / math.sqrt(HEAD_DIM))
        count = query.shape[1] // HEAD_DIM
        query = jnp.concatenate([query[:, n * HEAD_DIM:(n + 1) * HEAD_DIM] for n in range(count)], axis=0)
        scores = lax.dot_general(key_blk, query, (((1,), (1,)), ((), ())), preferred_element_type=F32)
        scores = scores + jnp.concatenate([bias_v[...]] * count, axis=1)
        raised = jnp.exp(scores - jnp.max(scores, axis=0, keepdims=True)).astype(BF16)
        summed = jnp.dot(value_rows, raised, preferred_element_type=F32)
        summed = summed[:HEAD_DIM] * (1.0 / summed[HEAD_DIM:HEAD_DIM + 1])
        heads = [summed[:, n * wide:(n + 1) * wide] for n in range(count)]
        joined = heads[0] if len(heads) == 1 else jnp.concatenate(heads, axis=0)
        joined = joined.T.astype(BF16)
        return jnp.concatenate([joined[i * both:(i + 1) * both] for i in range(per_chunk)], axis=1)

    near = (within(2), within(4))

    def attention(g):
        if g == CHUNKS // halves:
            gathered(1)
        arrived(q_buf.at[pl.ds(g * per_chunk, per_chunk)], q_sem.at[g])
        if g == 0:
            arrived(res_v, pair_sem.at[1])
        columns = slice(g * block, (g + 1) * block)
        attended = attend(g)
        stream = (res_v[:, :, columns].reshape(both, block).astype(F32) + attended.astype(F32)).astype(BF16)
        stream_v[g] = stream
        outg[g] = jnp.dot(chosen, stream, preferred_element_type=F32).astype(BF16).reshape(wave, 16, block)

    def leave(g, rz):
        go(outg.at[g, plane ^ rz], x_buf.at[g, 0, rz], z_sem.at[g, rz - 1], across(rz))

    def spread(g, rz):
        for hop in range(2):
            recv = x_sem.at[g, rz] if rz % 2 == hop else x_sem.at[g, wave]
            go(x_buf.at[g, 0, rz], x_buf.at[g, 1 + hop, rz], recv, near[hop])

    def forward(g, rz):
        arrived(x_buf.at[g, 0, rz], z_sem.at[g, rz - 1])
        spread(g, rz)

    def relay(g, rz):
        hop = rz % 2
        piece = x_buf.at[g, 1 + hop, rz]
        arrived(piece, x_sem.at[g, rz])
        go(piece, x_buf.at[g, 3, rz], x_sem.at[g, wave], near[1 - hop])

    def tell(g):
        ours = pl.ds(pl.multiple_of(other * tokens, tokens), tokens)
        go(stream_v.at[g, ours], stream_all.at[core, g], pair_sem.at[2], partner)
        stream_all[core, g] = stream_v[g, pl.ds(pl.multiple_of(core * tokens, tokens), tokens)]
        x_buf[g, 0, 0] = outg[g, plane]
        spread(g, 0)

    total = {}

    def up(g):
        if g == 0:
            arrived(gain_v, in_sem.at[5])
            arrived(w_v, w_sem.at[0])
        arrived(x_buf.at[g, pl.ds(0, 2)], x_sem.at[g, wave])
        columns = slice(g * block, (g + 1) * block)
        x = x_buf[g].reshape(4 * rows, block).astype(F32)
        square = x * x
        square = sum(square[:, i:i + 128] for i in range(0, block, 128))
        x = (x * gain_v[:, columns]).astype(BF16)
        weight = w_v[:, :, :, columns].reshape(-1, block)
        pre = lax.dot_general(x, weight, (((1,), (1,)), ((), ())), preferred_element_type=F32)
        total["square"] = square if g == 0 else total["square"] + square
        total["pre"] = pre if g == 0 else total["pre"] + pre

    def offer():
        pre = total["pre"]
        units = pre.shape[1]
        square = jnp.sum(total["square"], axis=1, keepdims=True)
        total["square"] = square
        coarse = square.astype(BF16)
        rest = (square - coarse.astype(F32)).astype(BF16)
        lane = lax.broadcasted_iota(jnp.int32, (4 * rows, 128), 1)
        pre_out[:, :units] = pre.astype(BF16)
        pre_out[:, units:] = jnp.where(lane < 64, coarse.astype(F32), rest.astype(F32)).astype(BF16)
        go(pre_out, pre_in, pre_sem, partner)

    def hide():
        units = total["pre"].shape[1]
        arrived(pre_in, pre_sem)
        square = (
            total["square"] + pre_in[:, units:units + 1].astype(F32) + pre_in[:, units + 64:units + 65].astype(F32)
        )
        inverse = lax.rsqrt(square * (1.0 / width) + 1e-06)
        pre = (total["pre"] + pre_in[:, :units].astype(F32)) * inverse
        gate_pre, up_pre = pre[:, :units // 2], pre[:, units // 2:]
        total["hidden"] = (gate_pre / (1.0 + jnp.exp(-gate_pre)) * up_pre).astype(BF16)
        arrived(wd_v, w_sem.at[1])

    def product(blks, which):
        hidden = jnp.concatenate([total["hidden"][blk * rows:(blk + 1) * rows] for blk in blks], axis=0)
        weight = wd_v[:, :, which * quarter:(which + 1) * quarter].reshape(-1, quarter)
        return jnp.dot(hidden, weight, preferred_element_type=F32).reshape(2, wave, 16, quarter)

    def first_hop(kind, rz, sides=(0, 1)):
        for which in sides:
            go(s1.at[which, rz, kind], r1.at[which, rz, kind], r1_sem.at[which, rz, kind], near[which])

    def down(early):
        for which in range(2):
            piece = product((3, 1 + which), which).astype(BF16)
            s1[which, :, 0], s1[which, :, 1] = piece[0], piece[1]
            for kind, rz in early:
                first_hop(kind, rz, (which,))
        for which in range(2):
            keep[which], own[which] = product((2 - which, 0), which)

    def second_hop(rz):
        for which in range(2):
            arrived(r1.at[which, rz, 0], r1_sem.at[which, rz, 0])
            s2[which, rz] = (keep[which, rz] + r1[which, rz, 0].astype(F32)).astype(BF16)
            go(s2.at[which, rz], r2.at[which, rz], r2_sem.at[rz], near[1 - which])

    def finish(rz):
        for which in range(2):
            arrived(r1.at[which, rz, 1], r1_sem.at[which, rz, 1])
        arrived(r2.at[:, rz], r2_sem.at[rz])
        sides = [
            own[which, rz] + r1[which, rz, 1].astype(F32) + r2[which, rz].astype(F32) for which in range(2)
        ]
        for c in range(2):
            final[rz, c] = jnp.concatenate([one[c * 8:(c + 1) * 8] for one in sides], axis=0).astype(BF16)
        go(final.at[rz, other], back.at[plane * 2 + core], back_sem, (plane ^ rz) * group + (mine ^ 1))
        if rz:
            go(final.at[rz, core], back.at[plane * 2 + core], back_sem, across(rz))
        else:
            back[plane * 2 + core] = final[0, core]

    for g in range(CHUNKS):
        attention(g)
        tell(g)
        for i in range(1, wave):
            leave(g, i)
        if g >= 2:
            relay(g - 2, 0)

    come = range(1, wave)
    steps = []

    def then(step, *where):
        steps.append((step, *where))

    def many(step, g):
        for rz in come:
            then(step, g, rz)

    many(forward, 0)
    then(relay, 2, 0)
    many(forward, 1)
    then(relay, 3, 0)
    many(forward, 2)
    many(forward, 3)
    many(relay, 0)
    many(relay, 1)
    many(relay, 2)
    many(relay, 3)
    for g in range(CHUNKS):
        then(up, g)
    then(offer)
    then(hide)
    behind = list(range(wave - 1, -1, -1))
    pieces = [(0, rz) for rz in behind[:AHEAD]]
    for n, rz in enumerate(behind):
        pieces.append((1, rz))
        if n + AHEAD < wave:
            pieces.append((0, behind[n + AHEAD]))
    then(down, pieces[:WINDOW])
    del pieces[:WINDOW]
    for n, rz in enumerate(behind):
        then(second_hop, rz)
        for kind, late in pieces[:NEXT]:
            then(first_hop, kind, late)
        del pieces[:NEXT]
        if n >= LAG:
            then(finish, behind[n - LAG])
    for rz in behind[-LAG:]:
        then(finish, rz)
    for step, *where in steps:
        step(*where)
    arrived(back.at[pl.ds(0, 2 * wave - 1)], back_sem)
    arrived(stream_all.at[0], pair_sem.at[2])
    high_mix = mix.astype(BF16)
    rest = mix - high_mix.astype(F32)
    middle = rest.astype(BF16)
    lowest = (rest - middle.astype(F32)).astype(BF16)
    outs = back[...].reshape(wave, 2, 16, quarter).astype(F32)
    for c in range(2):
        for which in range(2):
            rows = outs[:, c, which * 8:(which + 1) * 8].reshape(wave * 8, quarter).astype(BF16)
            added = (
                jnp.dot(lowest, rows, preferred_element_type=F32)
                + jnp.dot(middle, rows, preferred_element_type=F32)
                + jnp.dot(high_mix, rows, preferred_element_type=F32)
            )
            for g in range(CHUNKS // 2):
                at_chunk = which * (CHUNKS // 2) + g
                start = (1 + c, 3 * c)[which] * quarter + g * block
                out[:, start:start + block] = (
                    stream_all[c, at_chunk].astype(F32) + added[:, g * block:(g + 1) * block]
                ).astype(BF16)

    for r in range(1, devices // 2):
        ask(r).wait_send()

    @pl.when(core != side)
    def _():
        ask(0).wait_send()

    for copy in sends:
        copy.wait_send()


def layer(queries, keys, values, span_ids, res, gain, routes, gates, wg, wu, wd):
    devices = lax.axis_size("expert")
    group = FF_WIN // wg.shape[0]
    wave = devices // group
    tokens, width = res.shape
    half = width // 2
    hidden = wg.shape[0]
    both = 2 * tokens
    block = half // CHUNKS
    planes = SPAN // (group * tokens)
    halves = KV_HEADS // 2
    rows = wave * 16
    per_chunk = devices // 2 // CHUNKS
    hbm = pl.BlockSpec(memory_space=pl.ANY)
    dma = pltpu.SemaphoreType.DMA

    def vmem(*shape, dtype=BF16):
        return pltpu.VMEM(shape, dtype)

    scratch = {
        "keys_v": vmem(*keys.shape),
        "values_v": vmem(*values.shape),
        "ids_v": vmem(wave, 1, group * tokens, dtype=jnp.int32),
        "gain_v": vmem(1, half, dtype=F32),
        "routes_v": vmem(*routes.shape[::-1], dtype=jnp.int32),
        "gates_v": vmem(*gates.shape[::-1], dtype=F32),
        "rg_v": vmem(2, 16, 128, dtype=F32),
        "res_v": vmem(2, tokens, half),
        "w_v": vmem(2, 2, hidden, half),
        "wd_v": vmem(2, hidden, half),
        "kv_pack": vmem(KV_HEADS, tokens, 2 * HEAD_DIM),
        "kv_far": vmem(max(planes - 1, 1), KV_HEADS, tokens, 2 * HEAD_DIM),
        "kv_buf": vmem(halves, planes, group, tokens, 2 * HEAD_DIM),
        "q_buf": vmem(devices // 2, both, queries.shape[1]),
        "bias_v": vmem(SPAN, per_chunk * both, dtype=F32),
        "stream_v": vmem(CHUNKS, both, block),
        "stream_all": vmem(2, CHUNKS, tokens, block),
        "outg": vmem(CHUNKS, wave, 16, block),
        "x_buf": vmem(CHUNKS, 4, wave, 16, block),
        "pre_out": vmem(4 * rows, 4 * hidden + 128),
        "pre_in": vmem(4 * rows, 4 * hidden + 128),
        "s1": vmem(2, wave, 2, 16, half // 2),
        "r1": vmem(2, wave, 2, 16, half // 2),
        "s2": vmem(2, wave, 16, half // 2),
        "r2": vmem(2, wave, 16, half // 2),
        "keep": vmem(2, wave, 16, half // 2, dtype=F32),
        "own": vmem(2, wave, 16, half // 2, dtype=F32),
        "final": vmem(wave, 2, 16, half // 2),
        "back": vmem(2 * wave, 16, half // 2),
        "in_sem": dma((6,)),
        "w_sem": dma((2,)),
        "ready_sem": pltpu.SemaphoreType.REGULAR,
        "send_sem": dma(()),
        "ask_sem": dma(()),
        "far_sem": dma((max(planes - 1, 1), halves)),
        "kv_sem": dma((2, halves)),
        "q_sem": dma((CHUNKS,)),
        "pair_sem": dma((3,)),
        "z_sem": dma((CHUNKS, wave - 1)),
        "x_sem": dma((CHUNKS, wave + 1)),
        "pre_sem": dma(()),
        "r1_sem": dma((2, wave, 2)),
        "r2_sem": dma((wave,)),
        "back_sem": dma(()),
    }
    names = ("queries", "keys", "values", "ids", "res", "gain", "routes", "gates", "wg", "wu", "wd", "out", *scratch)
    return pl.pallas_call(
        functools.partial(moe_kernel, names, group),
        out_shape=pltpu.VMEM((tokens, width), BF16),
        in_specs=[hbm] * 11,
        out_specs=pl.BlockSpec(memory_space=pltpu.VMEM),
        scratch_shapes=list(scratch.values()),
        compiler_params=pltpu.CompilerParams(
            collective_id=0, has_side_effects=True, vmem_limit_bytes=60 * 2**20
        ),
    )(
        queries, keys, values, span_ids.reshape(wave, 1, group * tokens), res, gain.reshape(1, width),
        routes.T, gates.T, wg, wu, wd,
    )


def solution(mesh):
    return jax.shard_map(
        layer,
        mesh=mesh,
        in_specs=(
            P("dp", "expert"),
            P(("dp", "expert"), None),
            P(("dp", "expert"), None),
            P("dp"),
            P(("dp", "expert"), None),
            P(),
            P(("dp", "expert"), None),
            P(("dp", "expert"), None),
            P("expert", None),
            P("expert", None),
            P("expert", None),
        ),
        out_specs=P(("dp", "expert"), None),
        check_vma=False,
    )
```

```python
import functools
import math

import jax
import jax.numpy as jnp
from jax import lax
from jax.experimental import pallas as pl
from jax.experimental.pallas import tpu as pltpu
from jax.sharding import PartitionSpec as P

KV_HEADS = 4
HEAD_DIM = 64
FF_WIN = 1024
SPAN = 512
CHUNKS = 4
WINDOW = 5
AHEAD = 3
NEXT = 2
LAG = 2
SOON = (1,)
MESH = pl.DeviceIdType.MESH
F32 = jnp.float32
BF16 = jnp.bfloat16


def remote(src, dst, send, recv, device):
    return pltpu.make_async_remote_copy(
        src_ref=src, dst_ref=dst, send_sem=send, recv_sem=recv,
        device_id={"expert": device}, device_id_type=MESH,
    )


def arrived(ref, sem):
    pltpu.make_async_copy(ref, ref, sem).wait()


def route_matrix(routes, gates, wave, capacity, cores):
    tokens = routes.shape[0]
    here = tokens // cores
    columns = wave * cores * capacity
    column = lax.broadcasted_iota(jnp.int32, (tokens, columns), 1)
    token = lax.broadcasted_iota(jnp.int32, (tokens, columns), 0)
    one = lax.broadcasted_iota(jnp.int32, (tokens, tokens), 0)
    other = lax.broadcasted_iota(jnp.int32, (tokens, tokens), 1)
    lower = jnp.where((one >= other) & (one // here == other // here), 1.0, 0.0)
    named_wide = jnp.zeros((tokens, columns), F32)
    weight_wide = jnp.zeros((tokens, columns), F32)
    for expert in range(wave):
        hits = routes == expert
        named = jnp.max(jnp.where(hits, 1.0, 0.0), axis=1, keepdims=True)
        weight = jnp.sum(jnp.where(hits, gates, 0.0), axis=1, keepdims=True)
        mask = column // (cores * capacity) == expert
        named_wide = jnp.where(mask, named, named_wide)
        weight_wide = jnp.where(mask, weight, weight_wide)
    count = jnp.dot(lower.astype(BF16), named_wide.astype(BF16), preferred_element_type=F32)
    slot = (column % capacity + 1).astype(F32)
    fits = (count == slot) & (column % (cores * capacity) // capacity == token // here)
    chosen = jnp.where(fits, named_wide, 0.0)
    return chosen, chosen * weight_wide


def moe_kernel(names, group, *refs):
    at = dict(zip(names, refs, strict=True))
    (queries, keys, values, ids, res, gain, routes, gates, wg, wu, wd, out) = (
        at[name] for name in ("queries", "keys", "values", "ids", "res", "gain", "routes", "gates", "wg", "wu", "wd", "out")
    )
    (keys_v, values_v, ids_v, gain_v, routes_v, gates_v, rg_v, res_v, w_v, wd_v) = (
        at[name] for name in ("keys_v", "values_v", "ids_v", "gain_v", "routes_v", "gates_v", "rg_v", "res_v", "w_v", "wd_v")
    )
    (kv_pack, kv_far, kv_buf, q_buf, bias_v, stream_v, stream_all, outg, x_buf, pre_out, pre_in) = (
        at[name] for name in (
            "kv_pack", "kv_far", "kv_buf", "q_buf", "bias_v", "stream_v", "stream_all", "outg", "x_buf", "pre_out", "pre_in")
    )
    (s1, r1, s2, r2, keep, own, final, back) = (
        at[name] for name in ("s1", "r1", "s2", "r2", "keep", "own", "final", "back")
    )
    (far_sem, in_sem, w_sem, ready_sem, send_sem, kv_sem, q_sem, pair_sem, z_sem, x_sem, pre_sem, r1_sem, r2_sem, back_sem) = (
        at[name] for name in (
            "far_sem", "in_sem", "w_sem", "ready_sem", "send_sem", "kv_sem", "q_sem", "pair_sem", "z_sem", "x_sem",
            "pre_sem", "r1_sem", "r2_sem", "back_sem")
    )
    me = lax.axis_index("expert")
    wave = x_buf.shape[2]
    devices = wave * group
    tokens, width = out.shape
    both = 2 * tokens
    half = width // 2
    quarter = half // 2
    block = half // CHUNKS
    rows = wave * 16
    plane = me // group
    mine = me % group
    core = me % 2
    other = 1 - core


    sends = []

    def go(src, dst, recv, device):
        copy = remote(src, dst, send_sem, recv, device)
        copy.start()
        sends.append(copy)

    def early(c):
        return [pl.ds(pl.multiple_of(q * quarter, 128), quarter) for q in (1 + c, 3 * c)]

    def split(source, target, sem, send):
        for n, columns in enumerate(early(core if send is None else other)):
            place = target.at[:, pl.ds(n * quarter, quarter)]
            if send is None:
                pltpu.make_async_copy(source.at[:, columns], place, sem).start()
            else:
                go(source.at[:, columns], place, sem, send)

    def across(rz):
        return (plane ^ rz) * group + mine

    def within(r):
        return plane * group + (mine ^ r)

    partner = within(1)
    fetched = {}
    for number, (name, source, target) in enumerate((
        ("keys", keys, keys_v), ("values", values, values_v), ("routes", routes, routes_v), ("gates", gates, gates_v),
        ("ids", ids, ids_v),
    )):
        fetched[name] = pltpu.make_async_copy(source, target, in_sem.at[number])
        fetched[name].start()
    barrier = pltpu.get_barrier_semaphore()
    partners = [within(r) for r in range(1, group)] + [across(rz) for rz in range(1, wave)]
    for device in partners:
        pl.semaphore_signal(barrier, inc=1, device_id={"expert": device}, device_id_type=MESH)
    split(res, res_v.at[core], pair_sem.at[1], None)
    split(gain, gain_v, in_sem.at[5], None)
    split(wg, w_v.at[0, core], w_sem.at[0], None)
    split(wu, w_v.at[1, core], w_sem.at[0], None)
    split(wd, wd_v.at[core], w_sem.at[1], None)
    pl.semaphore_wait(barrier, len(partners))
    for rz in range(1, wave):
        pl.semaphore_signal(ready_sem, inc=1, device_id={"expert": across(rz)}, device_id_type=MESH)

    for name in ("keys", "values"):
        fetched[name].wait()
    for place, head in enumerate((1, 2, 0, 3)):
        columns = slice(head * HEAD_DIM, (head + 1) * HEAD_DIM)
        kv_pack[place] = jnp.concatenate([keys_v[:, columns], values_v[:, columns]], axis=1)
    planes = SPAN // (group * tokens)
    halves = KV_HEADS // 2
    for h in range(halves):
        for rz in range(1, planes):
            pair = pl.ds(2 * h, 2)
            go(kv_pack.at[pair], kv_far.at[rz - 1, pair], far_sem.at[rz - 1, h], across(rz))

    def share(h, source, at_plane, sem):
        for r in range(1, group):
            go(source.at[2 * h + (core ^ (r % 2))], kv_buf.at[h, at_plane, mine], sem, within(r))
        kv_buf[h, at_plane, mine] = source[2 * h + core]

    share(0, kv_pack, plane % planes, kv_sem.at[0, 0])
    pl.semaphore_wait(ready_sem, wave - 1)
    side = me // (devices // 2)
    number = (me % (devices // 2)) ^ ((1 - side) * (devices // 4))
    per_chunk = devices // 2 // CHUNKS
    query_sem = q_sem.at[number // per_chunk]

    def ask(r):
        pair = (me // 2) ^ r
        source = queries.at[pl.ds(pl.multiple_of(pair * both, both), both)]
        return remote(source, q_buf.at[number], at["ask_sem"], query_sem, pair * 2 + side)

    def ask_planes(distances):
        for rz in distances:
            for r in range((rz + 1) * group // 2 - 1, rz * group // 2 - 1, -1):
                if r:
                    ask(r).start()
        if 0 in distances:

            @pl.when(core == side)
            def _():
                source = queries.at[pl.ds(pl.multiple_of(me // 2 * both, both), both)]
                pltpu.make_async_copy(source, q_buf.at[number], query_sem).start()

            @pl.when(core != side)
            def _():
                ask(0).start()

    distant = list(range(wave - 1, -1, -1))
    soon = SOON

    @pl.when(number < devices // 4)
    def _():
        ask_planes(distant[:-1])

    @pl.when(number >= devices // 4)
    def _():
        ask_planes([rz for rz in distant if rz in soon])

    for name in ("routes", "gates"):
        fetched[name].wait()
    rg_v[core, :8, :tokens] = routes_v[...].astype(F32)
    rg_v[core, 8:, :tokens] = gates_v[...]
    go(rg_v.at[core], rg_v.at[core], pair_sem.at[0], partner)
    def pass_on(h):
        for rz in range(1, planes):
            arrived(kv_far.at[rz - 1, pl.ds(2 * h, 2)], far_sem.at[rz - 1, h])
            share(h, kv_far.at[rz - 1], (plane ^ rz) % planes, kv_sem.at[1, h])

    pass_on(0)

    @pl.when(number < devices // 4)
    def _():
        ask_planes([0])

    split(res, res_v.at[core], pair_sem.at[1], partner)
    fetched["ids"].wait()
    _, mix = route_matrix(routes_v[...].astype(F32).T, gates_v[...].T, wave, 8, 1)
    arrived(rg_v.at[0], pair_sem.at[0])
    named = jnp.concatenate([rg_v[c, :8, :].T[:tokens] for c in range(2)], axis=0)
    weights = jnp.concatenate([rg_v[c, 8:, :].T[:tokens] for c in range(2)], axis=0)
    chosen, _ = route_matrix(named, weights, wave, 8, 2)
    chosen = chosen.T.astype(BF16)

    stretch = group * tokens
    wide = per_chunk * both
    first = plane // planes * planes
    key_ids = jnp.concatenate(
        [jnp.broadcast_to(ids_v[first + i].astype(F32), (128, stretch)).T for i in range(planes)], axis=0
    )
    key_ids = jnp.concatenate([key_ids] * (wide // 128), axis=1)
    key_at = lax.broadcasted_iota(jnp.int32, (SPAN, wide), 0)
    query_at = (
        lax.broadcasted_iota(jnp.int32, (SPAN, wide), 1) % both
        + ((plane - first) * stretch + mine // 2 * both)
    )
    query_ids = jnp.sum(jnp.where(key_at == query_at, key_ids, 0.0), axis=0, keepdims=True)
    bias_v[...] = jnp.where((key_at <= query_at) & (key_ids == query_ids), 0.0, -jnp.inf)
    share(1, kv_pack, plane % planes, kv_sem.at[0, 1])
    pass_on(1)

    @pl.when(number >= devices // 4)
    def _():
        ask_planes([rz for rz in distant if rz not in soon])

    def gathered(h):
        arrived(kv_buf.at[h, 0, pl.ds(0, group - 1)], kv_sem.at[0, h])
        if planes > 1:
            arrived(kv_buf.at[h, pl.ds(0, planes - 1), pl.ds(0, group - 1)], kv_sem.at[1, h])

    gathered(0)
    split(wg, w_v.at[0, core], w_sem.at[0], partner)
    split(wu, w_v.at[1, core], w_sem.at[0], partner)
    split(wd, wd_v.at[core], w_sem.at[1], partner)

    def attend(g):
        head = g * halves // CHUNKS
        held = kv_buf[head].reshape(SPAN, 2 * HEAD_DIM)
        key_blk = held[:, :HEAD_DIM]
        value_rows = jnp.concatenate([held.T[HEAD_DIM:], jnp.ones((16, SPAN), BF16)], axis=0)
        query = q_buf[g * per_chunk:(g + 1) * per_chunk].reshape(wide, -1) * BF16(1.0 / math.sqrt(HEAD_DIM))
        count = query.shape[1] // HEAD_DIM
        query = jnp.concatenate([query[:, n * HEAD_DIM:(n + 1) * HEAD_DIM] for n in range(count)], axis=0)
        scores = lax.dot_general(key_blk, query, (((1,), (1,)), ((), ())), preferred_element_type=F32)
        scores = scores + jnp.concatenate([bias_v[...]] * count, axis=1)
        raised = jnp.exp(scores - jnp.max(scores, axis=0, keepdims=True)).astype(BF16)
        summed = jnp.dot(value_rows, raised, preferred_element_type=F32)
        summed = summed[:HEAD_DIM] * (1.0 / summed[HEAD_DIM:HEAD_DIM + 1])
        heads = [summed[:, n * wide:(n + 1) * wide] for n in range(count)]
        joined = heads[0] if len(heads) == 1 else jnp.concatenate(heads, axis=0)
        joined = joined.T.astype(BF16)
        return jnp.concatenate([joined[i * both:(i + 1) * both] for i in range(per_chunk)], axis=1)

    near = (within(2), within(4))

    def attention(g):
        if g == CHUNKS // halves:
            gathered(1)
        arrived(q_buf.at[pl.ds(g * per_chunk, per_chunk)], q_sem.at[g])
        if g == 0:
            arrived(res_v, pair_sem.at[1])
        columns = slice(g * block, (g + 1) * block)
        attended = attend(g)
        stream = (res_v[:, :, columns].reshape(both, block).astype(F32) + attended.astype(F32)).astype(BF16)
        stream_v[g] = stream
        outg[g] = jnp.dot(chosen, stream, preferred_element_type=F32).astype(BF16).reshape(wave, 16, block)

    def leave(g, rz):
        go(outg.at[g, plane ^ rz], x_buf.at[g, 0, rz], z_sem.at[g, rz - 1], across(rz))

    def spread(g, rz):
        for hop in range(2):
            recv = x_sem.at[g, rz] if rz % 2 == hop else x_sem.at[g, wave]
            go(x_buf.at[g, 0, rz], x_buf.at[g, 1 + hop, rz], recv, near[hop])

    def forward(g, rz):
        arrived(x_buf.at[g, 0, rz], z_sem.at[g, rz - 1])
        spread(g, rz)

    def relay(g, rz):
        hop = rz % 2
        piece = x_buf.at[g, 1 + hop, rz]
        arrived(piece, x_sem.at[g, rz])
        go(piece, x_buf.at[g, 3, rz], x_sem.at[g, wave], near[1 - hop])

    def tell(g):
        ours = pl.ds(pl.multiple_of(other * tokens, tokens), tokens)
        go(stream_v.at[g, ours], stream_all.at[core, g], pair_sem.at[2], partner)
        stream_all[core, g] = stream_v[g, pl.ds(pl.multiple_of(core * tokens, tokens), tokens)]
        x_buf[g, 0, 0] = outg[g, plane]
        spread(g, 0)

    total = {}

    def up(g):
        if g == 0:
            arrived(gain_v, in_sem.at[5])
            arrived(w_v, w_sem.at[0])
        arrived(x_buf.at[g, pl.ds(0, 2)], x_sem.at[g, wave])
        columns = slice(g * block, (g + 1) * block)
        x = x_buf[g].reshape(4 * rows, block).astype(F32)
        square = x * x
        square = sum(square[:, i:i + 128] for i in range(0, block, 128))
        x = (x * gain_v[:, columns]).astype(BF16)
        weight = w_v[:, :, :, columns].reshape(-1, block)
        pre = lax.dot_general(x, weight, (((1,), (1,)), ((), ())), preferred_element_type=F32)
        total["square"] = square if g == 0 else total["square"] + square
        total["pre"] = pre if g == 0 else total["pre"] + pre

    def offer():
        pre = total["pre"]
        units = pre.shape[1]
        square = jnp.sum(total["square"], axis=1, keepdims=True)
        total["square"] = square
        coarse = square.astype(BF16)
        rest = (square - coarse.astype(F32)).astype(BF16)
        lane = lax.broadcasted_iota(jnp.int32, (4 * rows, 128), 1)
        pre_out[:, :units] = pre.astype(BF16)
        pre_out[:, units:] = jnp.where(lane < 64, coarse.astype(F32), rest.astype(F32)).astype(BF16)
        go(pre_out, pre_in, pre_sem, partner)

    def hide():
        units = total["pre"].shape[1]
        arrived(pre_in, pre_sem)
        square = (
            total["square"] + pre_in[:, units:units + 1].astype(F32) + pre_in[:, units + 64:units + 65].astype(F32)
        )
        inverse = lax.rsqrt(square * (1.0 / width) + 1e-06)
        pre = (total["pre"] + pre_in[:, :units].astype(F32)) * inverse
        gate_pre, up_pre = pre[:, :units // 2], pre[:, units // 2:]
        total["hidden"] = (gate_pre / (1.0 + jnp.exp(-gate_pre)) * up_pre).astype(BF16)
        arrived(wd_v, w_sem.at[1])

    def product(blks, which):
        hidden = jnp.concatenate([total["hidden"][blk * rows:(blk + 1) * rows] for blk in blks], axis=0)
        weight = wd_v[:, :, which * quarter:(which + 1) * quarter].reshape(-1, quarter)
        return jnp.dot(hidden, weight, preferred_element_type=F32).reshape(2, wave, 16, quarter)

    def first_hop(kind, rz, sides=(0, 1)):
        for which in sides:
            go(s1.at[which, rz, kind], r1.at[which, rz, kind], r1_sem.at[which, rz, kind], near[which])

    def down(early):
        for which in range(2):
            piece = product((3, 1 + which), which).astype(BF16)
            s1[which, :, 0], s1[which, :, 1] = piece[0], piece[1]
            for kind, rz in early:
                first_hop(kind, rz, (which,))
        for which in range(2):
            keep[which], own[which] = product((2 - which, 0), which)

    def second_hop(rz):
        for which in range(2):
            arrived(r1.at[which, rz, 0], r1_sem.at[which, rz, 0])
            s2[which, rz] = (keep[which, rz] + r1[which, rz, 0].astype(F32)).astype(BF16)
            go(s2.at[which, rz], r2.at[which, rz], r2_sem.at[rz], near[1 - which])

    def finish(rz):
        for which in range(2):
            arrived(r1.at[which, rz, 1], r1_sem.at[which, rz, 1])
        arrived(r2.at[:, rz], r2_sem.at[rz])
        sides = [
            own[which, rz] + r1[which, rz, 1].astype(F32) + r2[which, rz].astype(F32) for which in range(2)
        ]
        for c in range(2):
            final[rz, c] = jnp.concatenate([one[c * 8:(c + 1) * 8] for one in sides], axis=0).astype(BF16)
        go(final.at[rz, other], back.at[plane * 2 + core], back_sem, (plane ^ rz) * group + (mine ^ 1))
        if rz:
            go(final.at[rz, core], back.at[plane * 2 + core], back_sem, across(rz))
        else:
            back[plane * 2 + core] = final[0, core]

    for g in range(CHUNKS):
        attention(g)
        tell(g)
        for i in range(1, wave):
            leave(g, i)
        if g >= 2:
            relay(g - 2, 0)

    come = range(1, wave)
    steps = []

    def then(step, *where):
        steps.append((step, *where))

    def many(step, g):
        for rz in come:
            then(step, g, rz)

    for g in range(CHUNKS):
        many(forward, g)
    then(relay, 2, 0)
    then(relay, 3, 0)
    for g in range(CHUNKS):
        many(relay, g)
    for g in range(CHUNKS):
        then(up, g)
    then(offer)
    then(hide)
    behind = list(range(wave - 1, -1, -1))
    pieces = [(0, rz) for rz in behind[:AHEAD]]
    for n, rz in enumerate(behind):
        pieces.append((1, rz))
        if n + AHEAD < wave:
            pieces.append((0, behind[n + AHEAD]))
    then(down, pieces[:WINDOW])
    del pieces[:WINDOW]
    for n, rz in enumerate(behind):
        then(second_hop, rz)
        for kind, late in pieces[:NEXT]:
            then(first_hop, kind, late)
        del pieces[:NEXT]
        if n >= LAG:
            then(finish, behind[n - LAG])
    for rz in behind[-LAG:]:
        then(finish, rz)
    for step, *where in steps:
        step(*where)
    arrived(back.at[pl.ds(0, 2 * wave - 1)], back_sem)
    arrived(stream_all.at[0], pair_sem.at[2])
    high_mix = mix.astype(BF16)
    rest = mix - high_mix.astype(F32)
    middle = rest.astype(BF16)
    lowest = (rest - middle.astype(F32)).astype(BF16)
    outs = back[...].reshape(wave, 2, 16, quarter).astype(F32)
    for c in range(2):
        for which in range(2):
            rows = outs[:, c, which * 8:(which + 1) * 8].reshape(wave * 8, quarter).astype(BF16)
            added = (
                jnp.dot(lowest, rows, preferred_element_type=F32)
                + jnp.dot(middle, rows, preferred_element_type=F32)
                + jnp.dot(high_mix, rows, preferred_element_type=F32)
            )
            for g in range(CHUNKS // 2):
                at_chunk = which * (CHUNKS // 2) + g
                start = (1 + c, 3 * c)[which] * quarter + g * block
                out[:, start:start + block] = (
                    stream_all[c, at_chunk].astype(F32) + added[:, g * block:(g + 1) * block]
                ).astype(BF16)

    for r in range(1, devices // 2):
        ask(r).wait_send()

    @pl.when(core != side)
    def _():
        ask(0).wait_send()

    for copy in sends:
        copy.wait_send()


def layer(queries, keys, values, span_ids, res, gain, routes, gates, wg, wu, wd):
    devices = lax.axis_size("expert")
    group = FF_WIN // wg.shape[0]
    wave = devices // group
    tokens, width = res.shape
    half = width // 2
    hidden = wg.shape[0]
    both = 2 * tokens
    block = half // CHUNKS
    planes = SPAN // (group * tokens)
    halves = KV_HEADS // 2
    rows = wave * 16
    per_chunk = devices // 2 // CHUNKS
    hbm = pl.BlockSpec(memory_space=pl.ANY)
    dma = pltpu.SemaphoreType.DMA

    def vmem(*shape, dtype=BF16):
        return pltpu.VMEM(shape, dtype)

    scratch = {
        "keys_v": vmem(*keys.shape),
        "values_v": vmem(*values.shape),
        "ids_v": vmem(wave, 1, group * tokens, dtype=jnp.int32),
        "gain_v": vmem(1, half, dtype=F32),
        "routes_v": vmem(*routes.shape[::-1], dtype=jnp.int32),
        "gates_v": vmem(*gates.shape[::-1], dtype=F32),
        "rg_v": vmem(2, 16, 128, dtype=F32),
        "res_v": vmem(2, tokens, half),
        "w_v": vmem(2, 2, hidden, half),
        "wd_v": vmem(2, hidden, half),
        "kv_pack": vmem(KV_HEADS, tokens, 2 * HEAD_DIM),
        "kv_far": vmem(max(planes - 1, 1), KV_HEADS, tokens, 2 * HEAD_DIM),
        "kv_buf": vmem(halves, planes, group, tokens, 2 * HEAD_DIM),
        "q_buf": vmem(devices // 2, both, queries.shape[1]),
        "bias_v": vmem(SPAN, per_chunk * both, dtype=F32),
        "stream_v": vmem(CHUNKS, both, block),
        "stream_all": vmem(2, CHUNKS, tokens, block),
        "outg": vmem(CHUNKS, wave, 16, block),
        "x_buf": vmem(CHUNKS, 4, wave, 16, block),
        "pre_out": vmem(4 * rows, 4 * hidden + 128),
        "pre_in": vmem(4 * rows, 4 * hidden + 128),
        "s1": vmem(2, wave, 2, 16, half // 2),
        "r1": vmem(2, wave, 2, 16, half // 2),
        "s2": vmem(2, wave, 16, half // 2),
        "r2": vmem(2, wave, 16, half // 2),
        "keep": vmem(2, wave, 16, half // 2, dtype=F32),
        "own": vmem(2, wave, 16, half // 2, dtype=F32),
        "final": vmem(wave, 2, 16, half // 2),
        "back": vmem(2 * wave, 16, half // 2),
        "in_sem": dma((6,)),
        "w_sem": dma((2,)),
        "ready_sem": pltpu.SemaphoreType.REGULAR,
        "send_sem": dma(()),
        "ask_sem": dma(()),
        "far_sem": dma((max(planes - 1, 1), halves)),
        "kv_sem": dma((2, halves)),
        "q_sem": dma((CHUNKS,)),
        "pair_sem": dma((3,)),
        "z_sem": dma((CHUNKS, wave - 1)),
        "x_sem": dma((CHUNKS, wave + 1)),
        "pre_sem": dma(()),
        "r1_sem": dma((2, wave, 2)),
        "r2_sem": dma((wave,)),
        "back_sem": dma(()),
    }
    names = ("queries", "keys", "values", "ids", "res", "gain", "routes", "gates", "wg", "wu", "wd", "out", *scratch)
    return pl.pallas_call(
        functools.partial(moe_kernel, names, group),
        out_shape=pltpu.VMEM((tokens, width), BF16),
        in_specs=[hbm] * 11,
        out_specs=pl.BlockSpec(memory_space=pltpu.VMEM),
        scratch_shapes=list(scratch.values()),
        compiler_params=pltpu.CompilerParams(
            collective_id=0, has_side_effects=True, vmem_limit_bytes=60 * 2**20
        ),
    )(
        queries, keys, values, span_ids.reshape(wave, 1, group * tokens), res, gain.reshape(1, width),
        routes.T, gates.T, wg, wu, wd,
    )


def solution(mesh):
    return jax.shard_map(
        layer,
        mesh=mesh,
        in_specs=(
            P("dp", "expert"),
            P(("dp", "expert"), None),
            P(("dp", "expert"), None),
            P("dp"),
            P(("dp", "expert"), None),
            P(),
            P(("dp", "expert"), None),
            P(("dp", "expert"), None),
            P("expert", None),
            P("expert", None),
            P("expert", None),
        ),
        out_specs=P(("dp", "expert"), None),
        check_vma=False,
    )
```
